128 devices in a mesh: row: 16 (over y_hi, z, core), col: 8 (over x, y_lo).
Axes of the slice: x: 4, y: 4 (y_hi: 2, y_lo: 2; y = y_hi * 2 + y_lo), z: 4, core: 2. Of those that a mesh axis runs over, the one named last changes fastest.
Arguments:
- pair_input: bfloat16 [512, 512, 128], P('row', 'col'), may hold values from -18 to 18
- token_mask: int32 [512], replicated, may hold values 0 or 1
- out_check_weights: int32 [512], replicated, may hold values from 1 to 5, as said below
- in_check_weights: int32 [512], replicated, may hold values from 1 to 5, as said below
- out_norm_gain: float32 [128], replicated, may hold values from 0.25 to 1.75
- out_proj: bfloat16 [128, 256], replicated, may hold values from -0.5 to 0.5
- out_gate: bfloat16 [128, 128], replicated, may hold values from -0.5 to 0.5
- out_final_gain: float32 [64], replicated, may hold values from 0.25 to 1.75
- out_final: bfloat16 [64, 128], replicated, may hold values from -0.75 to 0.75
- in_norm_gain: float32 [128], replicated, may hold values from 0.25 to 1.75
- in_proj: bfloat16 [128, 256], replicated, may hold values from -0.5 to 0.5
- in_gate: bfloat16 [128, 128], replicated, may hold values from -0.5 to 0.5
- in_final_gain: float32 [64], replicated, may hold values from 0.25 to 1.75
- in_final: bfloat16 [64, 128], replicated, may hold values from -0.75 to 0.75
- att_norm_gain: float32 [128], replicated, may hold values from 0.25 to 1.75
- att_qkv: bfloat16 [128, 384], replicated, may hold values from -0.5 to 0.5
- att_bias: bfloat16 [128, 4], replicated, may hold values from -20 to 20
- att_gate: bfloat16 [128, 128], replicated, may hold values from -0.5 to 0.5
- att_out: bfloat16 [128, 128], replicated, may hold values from -0.5 to 0.5
Outputs:
- pair_output: bfloat16 [512, 512, 128], P('row', 'col')
- out_checksum: float32 [512, 64], P('row')
- in_checksum: float32 [512, 64], P('col')
The draws below stay inside these ranges and needn't reach their ends.
Inputs may be any that keep to these rules, and one draw needn't show every extreme that they name: `out_check_weights`: entry j lies between 1 + (4 * j) // 512 and 2 + (4 * j) // 512. `in_check_weights`: entry j lies between 1 + (4 * j) // 512 and 2 + (4 * j) // 512.
All inputs are finite; a program needn't handle non-finite values.
Results may differ from the reference program's by a relative error of at most 0.019.
Values may be sent and summed in bfloat16 or wider, within the bound.
No kernel may reach another device: no remote copies, remote signals or barrier semaphores. Data moves between devices by JAX's collectives and lax.ppermute only.
A program may use at most 128 MiB of HBM per device.

```python
import jax
import jax.numpy as jnp
from jax import lax

CZ = 128
CM = 64
HEADS = 4
DH = 32
NT = 512


def rising_weights(key):
    positions = jnp.arange(NT, dtype=jnp.int32)
    base_level = 1 + 4 * positions // NT
    return (base_level + jax.random.randint(key, (NT,), 0, 2)).astype(jnp.int32)


def draw_out_check_weights(key, part):
    key = jax.random.fold_in(key, 21)
    return rising_weights(key)


def draw_in_check_weights(key, part):
    key = jax.random.fold_in(key, 31)
    return rising_weights(key)


def draw_pair_input(key, part):
    key = jax.random.fold_in(key, 11)
    second_key = jax.random.fold_in(key, 1)
    values = jnp.clip(jax.random.normal(second_key, (NT, NT, CZ)), -6.0, 6.0)
    return values.astype(jnp.bfloat16)


def draw_att_bias(key, part):
    key = jax.random.fold_in(key, 41)
    second_key = jax.random.fold_in(key, 1)
    values = jnp.clip(jax.random.normal(second_key, (CZ, HEADS)), -6.0, 6.0) * CZ ** (-0.5)
    return values.astype(jnp.bfloat16)


def set_ends(drawn, key, low, high):
    spot = [jax.random.randint(jax.random.fold_in(key, axis), (), 0, length) for axis, length in enumerate(drawn.shape)]
    widest = drawn.shape.index(max(drawn.shape))
    beside = spot[:widest] + [(spot[widest] + 1) % drawn.shape[widest]] + spot[widest + 1:]
    return drawn.at[tuple(spot)].set(low).at[tuple(beside)].set(high)


def noise(rng, shape, scale, bound, kind=jnp.bfloat16):
    drawn = scale * jax.random.normal(rng, shape, jnp.float32)
    return jnp.clip(drawn, min=-bound, max=bound).astype(kind)


def setup_inputs(seed: int = 0) -> dict:
    keys = jax.random.split(jax.random.key(seed), 20)
    pair_input = draw_pair_input(jax.random.fold_in(keys[19], 71), 0)
    token_mask = set_ends((jax.random.randint(keys[1], (NT,), 0, 8) < 7).astype(jnp.int32), jax.random.fold_in(keys[1], 1), 0, 1)
    out_check_weights = draw_out_check_weights(jax.random.fold_in(keys[19], 71), 0)
    in_check_weights = draw_in_check_weights(jax.random.fold_in(keys[19], 71), 0)
    out_norm_gain = jnp.clip(1.0 + 0.15 * jax.random.normal(keys[4], (CZ,), jnp.float32), 0.25, 1.75)
    out_proj = noise(keys[5], (CZ, 4 * CM), CZ ** -0.5, 0.5)
    out_gate = noise(keys[6], (CZ, CZ), CZ ** -0.5, 0.5)
    out_final_gain = jnp.clip(1.0 + 0.15 * jax.random.normal(keys[7], (CM,), jnp.float32), 0.25, 1.75)
    out_final = noise(keys[8], (CM, CZ), CM ** -0.5, 0.75)
    in_norm_gain = jnp.clip(1.0 + 0.15 * jax.random.normal(keys[9], (CZ,), jnp.float32), 0.25, 1.75)
    in_proj = noise(keys[10], (CZ, 4 * CM), CZ ** -0.5, 0.5)
    in_gate = noise(keys[11], (CZ, CZ), CZ ** -0.5, 0.5)
    in_final_gain = jnp.clip(1.0 + 0.15 * jax.random.normal(keys[12], (CM,), jnp.float32), 0.25, 1.75)
    in_final = noise(keys[13], (CM, CZ), CM ** -0.5, 0.75)
    att_norm_gain = jnp.clip(1.0 + 0.15 * jax.random.normal(keys[14], (CZ,), jnp.float32), 0.25, 1.75)
    att_qkv = noise(keys[15], (CZ, 3 * HEADS * DH), CZ ** -0.5, 0.5)
    att_bias = draw_att_bias(jax.random.fold_in(keys[19], 71), 0)
    att_gate = noise(keys[17], (CZ, HEADS * DH), CZ ** -0.5, 0.5)
    att_out = noise(keys[18], (HEADS * DH, CZ), (HEADS * DH) ** -0.5, 0.5)
    return dict(pair_input=pair_input, token_mask=token_mask, out_check_weights=out_check_weights, in_check_weights=in_check_weights, out_norm_gain=out_norm_gain, out_proj=out_proj, out_gate=out_gate, out_final_gain=out_final_gain, out_final=out_final, in_norm_gain=in_norm_gain, in_proj=in_proj, in_gate=in_gate, in_final_gain=in_final_gain, in_final=in_final, att_norm_gain=att_norm_gain, att_qkv=att_qkv, att_bias=att_bias, att_gate=att_gate, att_out=att_out)


def layer_norm(values_in, gain_vec):
    chan_mean = lax.optimization_barrier(jnp.mean(values_in, axis=-1, keepdims=True))
    centered = values_in - chan_mean
    variance = lax.optimization_barrier(jnp.mean(centered * centered, axis=-1, keepdims=True))
    return centered * lax.rsqrt(variance + 1e-05) * gain_vec

def projections(state, gain_vec, proj_weight, gate_weight, pair_mask):
    normed = layer_norm(state, gain_vec).astype(jnp.bfloat16)
    mixed = jnp.dot(normed, proj_weight, preferred_element_type=jnp.float32)
    left_proj = (jax.nn.sigmoid(mixed[..., 0:CM]) * mixed[..., CM:2 * CM] * pair_mask[..., None]).astype(jnp.bfloat16)
    right_proj = (jax.nn.sigmoid(mixed[..., 2 * CM:3 * CM]) * mixed[..., 3 * CM:4 * CM] * pair_mask[..., None]).astype(jnp.bfloat16)
    gated = jax.nn.sigmoid(jnp.dot(normed, gate_weight, preferred_element_type=jnp.float32)).astype(jnp.bfloat16)
    return (left_proj, right_proj, gated)

def finish_update(state, product, gated, final_gain, final_weight):
    normed_product = layer_norm(product, final_gain).astype(jnp.bfloat16)
    update = jnp.dot(normed_product, final_weight, preferred_element_type=jnp.float32)
    return state + gated.astype(jnp.float32) * update

def reference(pair_input, token_mask, out_check_weights, in_check_weights, out_norm_gain, out_proj, out_gate, out_final_gain, out_final, in_norm_gain, in_proj, in_gate, in_final_gain, in_final, att_norm_gain, att_qkv, att_bias, att_gate, att_out):
    mask_float = token_mask.astype(jnp.float32)
    pair_mask = mask_float[:, None] * mask_float[None, :]
    state = pair_input.astype(jnp.float32)
    left_proj, right_proj, gated = projections(state, out_norm_gain, out_proj, out_gate, pair_mask)
    product = jnp.einsum('ikc,jkc->ijc', left_proj.astype(jnp.float32), right_proj.astype(jnp.float32))
    out_checksum = jnp.einsum('ijc,j->ic', product, out_check_weights.astype(jnp.float32), precision=lax.Precision.HIGHEST) / NT
    state = finish_update(state, product, gated, out_final_gain, out_final)
    left_proj, right_proj, gated = projections(state, in_norm_gain, in_proj, in_gate, pair_mask)
    product = jnp.einsum('kic,kjc->ijc', left_proj.astype(jnp.float32), right_proj.astype(jnp.float32))
    in_checksum = jnp.einsum('ijc,i->jc', product, in_check_weights.astype(jnp.float32), precision=lax.Precision.HIGHEST) / NT
    state = finish_update(state, product, gated, in_final_gain, in_final)
    width = HEADS * DH
    normed = layer_norm(state, att_norm_gain).astype(jnp.bfloat16)
    projected = jnp.dot(normed, att_qkv, preferred_element_type=jnp.float32)
    queries = (projected[..., 0:width] * DH ** (-0.5)).astype(jnp.bfloat16)
    keys_all = projected[..., width:2 * width].astype(jnp.bfloat16)
    values_all = projected[..., 2 * width:3 * width].astype(jnp.bfloat16)
    pair_bias = jnp.dot(normed, att_bias, preferred_element_type=jnp.float32)
    bias_heads = jnp.transpose(pair_bias, (2, 0, 1))
    gate_att = jax.nn.sigmoid(jnp.dot(normed, att_gate, preferred_element_type=jnp.float32))
    key_bias = jnp.where(token_mask > 0, 0.0, -1000000000.0).astype(jnp.float32)

    def attend_row(items):
        query_row, key_row, value_row = items
        query_heads = query_row.astype(jnp.float32).reshape(NT, HEADS, DH)
        key_heads = key_row.astype(jnp.float32).reshape(NT, HEADS, DH)
        value_heads = value_row.astype(jnp.float32).reshape(NT, HEADS, DH)
        scores = jnp.einsum('jhd,khd->hjk', query_heads, key_heads) + bias_heads + key_bias[None, None, :]
        attn_probs = jax.nn.softmax(scores, axis=-1).astype(jnp.bfloat16)
        attended_row = jnp.einsum('hjk,khd->jhd', attn_probs.astype(jnp.float32), value_heads)
        return attended_row.reshape(NT, width)
    attended = lax.map(attend_row, (queries, keys_all, values_all))
    gated_att = (attended * gate_att).astype(jnp.bfloat16)
    state = state + jnp.dot(gated_att, att_out, preferred_element_type=jnp.float32)
    return (state.astype(jnp.bfloat16), out_checksum, in_checksum)
```

```python
import jax
import jax.numpy as jnp
from jax import lax
from jax.experimental import pallas as pl
from jax.experimental.pallas import tpu as pltpu
from jax.sharding import Mesh, PartitionSpec as P

F32 = jnp.float32
BF16 = jnp.bfloat16
NT = 512
CZ = 128
CM = 64
HEADS = 4
DH = 32
LANES = 128
CHUNKS = NT // LANES
PLANE = ("p", "q")
PARAMS = pltpu.CompilerParams(vmem_limit_bytes=48 * 1024 * 1024)
VMEM = pl.BlockSpec(memory_space=pltpu.VMEM)
SMEM = pl.BlockSpec(memory_space=pltpu.SMEM)


def dot(left, right, left_dim, right_dim):
    return lax.dot_general(
        left, right, (((left_dim,), (right_dim,)), ((), ())), preferred_element_type=F32
    )


def column(row):
    return jnp.transpose(jnp.broadcast_to(row, (8, row.shape[1])))[:, 0:1]


def flipped(weight):
    return jnp.transpose(weight.astype(F32)).astype(BF16)


def eye():
    rows = lax.broadcasted_iota(jnp.int32, (LANES, LANES), 0)
    cols = lax.broadcasted_iota(jnp.int32, (LANES, LANES), 1)
    return jnp.where(rows == cols, 1.0, 0.0).astype(BF16)


def norm(values, gain_col):
    mean = jnp.mean(values, axis=0, keepdims=True)
    centered = values - mean
    variance = jnp.mean(centered * centered, axis=0, keepdims=True)
    return (centered * lax.rsqrt(variance + 1e-05) * gain_col).astype(BF16)


def sigmoid(values):
    return jax.nn.sigmoid(values)


def thirds(values):
    high = values.astype(BF16)
    rest = values - high.astype(F32)
    middle = rest.astype(BF16)
    return high, middle, (rest - middle.astype(F32)).astype(BF16)


def call(kernel, outs, scratch, ins, cost=None):
    return pl.pallas_call(
        kernel,
        out_shape=tuple(jax.ShapeDtypeStruct(shape, kind) for shape, kind in outs),
        in_specs=[SMEM if kind == "s" else VMEM for kind, _ in ins],
        out_specs=tuple(VMEM for _ in outs),
        scratch_shapes=[pltpu.VMEM(shape, kind) for shape, kind in scratch],
        compiler_params=PARAMS,
    )(*[value for _, value in ins])


def first_row():
    return (2 * lax.axis_index("p") + lax.axis_index("core")) * 32


def project_tile(mask_s, mask_v, x, gain, weight, out, stage):
    row0 = first_row()
    shift = lax.rem(NT - 64 * lax.axis_index("q"), NT)
    mask_all = jnp.broadcast_to(mask_v[...].astype(F32), (8, NT))
    col_mask = pltpu.roll(mask_all, shift, 1)[0:1, 0:64]
    gain_col = column(gain[...])
    weight_t = flipped(weight[...])
    unit = eye()
    for group in range(4):
        steps = range(group * 4, group * 4 + 4)
        pieces, masks = [], []
        for s in steps:
            for i in (s, s + 16):
                pieces.append(x[i * 64 : (i + 1) * 64, :])
                masks.append(col_mask * mask_s[row0 + i].astype(F32))
        state = dot(unit, jnp.concatenate(pieces, axis=0), 1, 1)
        mask = jnp.concatenate(masks, axis=1)
        mixed = dot(weight_t, norm(state, gain_col), 1, 0)
        left = sigmoid(mixed[0:CM]) * mixed[CM : 2 * CM] * mask
        right = sigmoid(mixed[2 * CM : 3 * CM]) * mixed[3 * CM : 4 * CM] * mask
        for at, s in enumerate(steps):
            lanes = slice(at * LANES, (at + 1) * LANES)
            stage[pl.ds(s, CM, stride=32), :] = left[:, lanes]
            stage[pl.ds(16 + s, CM, stride=32), :] = right[:, lanes]
    out[...] = stage[...].astype(BF16).reshape(CM, 32, LANES)


def gate_rows(x, gain, weight, state_out, gate_out):
    gain_col = column(gain[...])
    weight_t = flipped(weight[...])
    unit = eye()
    for r in range(4):
        rows = jnp.concatenate([x[q, r] for q in range(8)], axis=0)
        state = dot(unit, rows, 1, 1)
        span = slice(r * NT, (r + 1) * NT)
        state_out[:, span] = state.astype(BF16)
        gate_out[:, span] = sigmoid(dot(weight_t, norm(state, gain_col), 1, 0)).astype(BF16)


def product_rows(mine, other, weights, out, check_out, left, right, stage):
    core = lax.axis_index("core")
    low = lax.broadcasted_iota(jnp.int32, (16, LANES), 1) < 64

    def paired(ref, src, rows):
        first = ref[src, rows, :].astype(F32)
        second = ref[src + 1, rows, :].astype(F32)
        head = jnp.where(low, first, pltpu.roll(second, 64, 1))
        tail = jnp.where(low, pltpu.roll(first, 64, 1), second)
        return jnp.concatenate([head, tail], axis=0).astype(BF16)

    for p in range(8):
        for a in range(CHUNKS):
            lanes = slice(a * LANES, (a + 1) * LANES)
            src = p * 8 + 2 * a
            left[p * 32 : (p + 1) * 32, lanes] = paired(mine, src, slice(0, 16))
            at = pl.multiple_of(p * 64 + core * 32, 32)
            right[pl.ds(at, 32), lanes] = paired(mine, src, slice(16, 32))
            at = pl.multiple_of(p * 64 + (1 - core) * 32, 32)
            right[pl.ds(at, 32), lanes] = paired(other, src, slice(16, 32))
    product = dot(left[...], right[...], 1, 1)
    for chunk in range(CHUNKS):
        stage[pl.ds(chunk, 256, stride=4), :] = product[:, chunk * LANES : (chunk + 1) * LANES]
    out[...] = stage[...].astype(BF16).reshape(64, 16, LANES)
    weight_rows = jnp.broadcast_to(weights[...].astype(F32), (8, NT)).astype(BF16)
    total = sum(dot(part, left[...], 1, 1) for part in thirds(dot(weight_rows, right[...], 1, 0)))
    check_out[...] = total / NT


def update_rows(recv_stage, stride, r, state, gate, final_gain, final_t):
    product = jnp.concatenate(
        [recv_stage[pl.ds(r * 4 + chunk, CM, stride=stride), :] for chunk in range(CHUNKS)], axis=1
    )
    update = dot(final_t, norm(product, final_gain), 1, 0)
    return state + gate.astype(F32) * update


def project_rows(
    mask_s, mask_v, recv, state_in, gate, final_gain, final_weight, gain, weight,
    out, state_out, normed_out, stage, recv_stage,
):
    row0 = first_row() + 4 * lax.axis_index("q")
    mask_all = mask_v[...].astype(F32)
    gain_col = column(gain[...])
    final_col = column(final_gain[...])
    final_t = flipped(final_weight[...])
    weight_t = flipped(weight[...])
    recv_stage[...] = recv[...].astype(F32).reshape(CM * 16, LANES)
    for r in range(4):
        span = slice(r * NT, (r + 1) * NT)
        state = update_rows(
            recv_stage, 16, r, state_in[:, span].astype(F32), gate[:, span], final_col, final_t
        )
        state_out[:, span] = state
        normed = norm(state, gain_col)
        normed_out[:, span] = normed
        mixed = dot(weight_t, normed, 1, 0)
        mask = mask_all * mask_s[row0 + r].astype(F32)
        left = sigmoid(mixed[0:CM]) * mixed[CM : 2 * CM] * mask
        right = sigmoid(mixed[2 * CM : 3 * CM]) * mixed[3 * CM : 4 * CM] * mask
        for chunk in range(CHUNKS):
            lanes = slice(chunk * LANES, (chunk + 1) * LANES)
            stage[pl.ds(r * 8 + chunk, CM, stride=32), :] = left[:, lanes]
            stage[pl.ds(r * 8 + 4 + chunk, CM, stride=32), :] = right[:, lanes]
    out[...] = stage[...].astype(BF16).reshape(CM, 32, LANES)


def gate_only(normed, weight, gate_out):
    weight_t = flipped(weight[...])
    for r in range(4):
        span = slice(r * NT, (r + 1) * NT)
        gate_out[:, span] = sigmoid(dot(weight_t, normed[:, span], 1, 0)).astype(BF16)


def product_cols(mine, other, weights, check_in, out, left, right, product, stage, stage_out):
    core = lax.axis_index("core")
    for side, buf in enumerate((mine, other)):
        stage[...] = buf[...].astype(F32).reshape(64 * 32, LANES)
        rows = slice(side * 256, (side + 1) * 256)
        for chunk in range(CHUNKS):
            lanes = slice(chunk * LANES, (chunk + 1) * LANES)
            left[rows, lanes] = stage[pl.ds(chunk, 256, stride=8), :].astype(BF16)
            right[rows, lanes] = stage[pl.ds(4 + chunk, 256, stride=8), :].astype(BF16)
    product[...] = dot(left[...], right[...], 0, 0)
    for p in range(8):
        rows = product[pl.ds(pl.multiple_of(p * 64 + core * 32, 32), 32), :]
        for chunk in range(CHUNKS):
            stage_out[pl.ds(p * 128 + chunk, 32, stride=4), :] = rows[
                :, chunk * LANES : (chunk + 1) * LANES
            ]
    out[:, 0:16, :] = stage_out[...].astype(BF16).reshape(64, 16, LANES)
    weight_rows = jnp.broadcast_to(weights[...].astype(F32), (8, NT)).astype(BF16)
    total = sum(dot(part, right[...], 1, 0) for part in thirds(dot(weight_rows, left[...], 1, 1)))
    lines = []
    for check, count in ((check_in[...], 2), (total / NT, 4)):
        high = check.astype(BF16).astype(F32)
        for part in (high, check - high):
            lines += [part[0:1, c * LANES : (c + 1) * LANES] for c in range(count)]
    lines.append(jnp.zeros((4, LANES), F32))
    tail = jnp.concatenate(lines, axis=0).astype(BF16)
    out[:, 16:32, :] = jnp.broadcast_to(tail[None], (64, 16, LANES))


def bias_rows(
    recv, state_in, gate, final_gain, final_weight, gain, weight, out, state_out, normed_out,
    recv_stage, bias_stage,
):
    gain_col = column(gain[...])
    final_col = column(final_gain[...])
    final_t = flipped(final_weight[...])
    weight_t = flipped(weight[...])
    recv_stage[...] = recv[...].astype(F32).reshape(CM * 32, LANES)
    for r in range(4):
        span = slice(r * NT, (r + 1) * NT)
        state = update_rows(recv_stage, 32, r, state_in[:, span], gate[:, span], final_col, final_t)
        state_out[:, span] = state
        normed = norm(state, gain_col)
        normed_out[:, span] = normed
        bias = dot(weight_t, normed, 1, 0)
        for chunk in range(CHUNKS):
            bias_stage[pl.ds(r * 16 + chunk, HEADS, stride=4), :] = bias[
                0:HEADS, chunk * LANES : (chunk + 1) * LANES
            ]
    out[...] = jnp.broadcast_to(bias_stage[...].astype(BF16)[None], (64, 64, LANES))


def attention_inputs(
    recv, normed, qkv, gate_weight, query_out, key_out, value_out, gate_out, check_row, check_col,
    recv_stage, turn,
):
    width = HEADS * DH
    qkv_all = qkv[...]
    query_t = flipped(qkv_all[:, 0:width])
    value_t = flipped(qkv_all[:, 2 * width : 3 * width])
    gate_t = flipped(gate_weight[...])
    for r in range(4):
        span = slice(r * NT, (r + 1) * NT)
        rows = normed[:, span]
        query_out[:, span] = (dot(query_t, rows, 1, 0) * DH ** (-0.5)).astype(BF16)
        key_out[span, :] = dot(rows, qkv_all[:, width : 2 * width], 0, 0).astype(BF16)
        value_out[:, span] = dot(value_t, rows, 1, 0).astype(BF16)
        gate_out[:, span] = sigmoid(dot(gate_t, rows, 1, 0))
    recv_stage[...] = recv[:, 16:32, :].astype(F32).reshape(CM * 16, LANES)
    p, q = lax.axis_index("p"), lax.axis_index("q")

    def rows_of(at, gap):
        high = recv_stage[pl.ds(at, CM, stride=16), :]
        return jnp.transpose(high + recv_stage[pl.ds(at + gap, CM, stride=16), :])

    turn[...] = rows_of(p // 4, 2)
    check_row[...] = turn[pl.ds(pl.multiple_of(lax.rem(p, 4) * 32, 32), 32), :]
    turn[...] = rows_of(4 + q // 2, 4)
    check_col[...] = turn[pl.ds(pl.multiple_of(lax.rem(q, 2) * 64, 64), 64), :]


def attend(
    mask_v, mine, other, query, key, value, gate, state, weight, out, bias_stage, bias,
):
    core = lax.axis_index("core")
    bias_stage[core] = mine[...].astype(F32).reshape(64 * 64, LANES)
    bias_stage[1 - core] = other[...].astype(F32).reshape(64 * 64, LANES)
    key_bias = jnp.where(mask_v[...] > 0, 0.0, -1000000000.0).astype(F32)
    for chunk in range(CHUNKS):
        key_col = column(key_bias[:, chunk * LANES : (chunk + 1) * LANES])
        for h in range(HEADS):
            blocks = [
                bias_stage[plane, pl.ds(p * 512 + h * 4 + chunk, 32, stride=16), :]
                for p in range(8)
                for plane in range(2)
            ]
            turned = jnp.transpose(jnp.concatenate(blocks, axis=0))
            bias[h, chunk * LANES : (chunk + 1) * LANES, :] = turned + key_col
    weight_t = flipped(weight[...])

    def one_row(r, carry):
        span = pl.ds(pl.multiple_of(r * NT, NT), NT)
        query_row = query[:, span]
        key_row = key[span, :]
        value_row = value[:, span]
        zeros = jnp.zeros((DH, NT), BF16)
        parts = []
        for h in range(HEADS):
            head = slice(h * DH, (h + 1) * DH)
            masked = jnp.concatenate(
                [query_row[head] if at == h else zeros for at in range(HEADS)], axis=0
            )
            scores = dot(key_row, masked, 1, 0) + bias[h]
            top = jnp.max(scores, axis=0, keepdims=True)
            weights = jnp.exp(scores - top)
            total = jnp.sum(weights, axis=0, keepdims=True)
            parts.append(dot(value_row[head], weights.astype(BF16), 1, 0) / total)
        attended = jnp.concatenate(parts, axis=0) * gate[:, span]
        result = state[:, span] + dot(weight_t, attended.astype(BF16), 1, 0)
        out[:, r, :, :] = jnp.transpose(result).astype(BF16).reshape(8, 64, CZ)
        return carry

    lax.fori_loop(0, 4, one_row, 0)


def swap(values):
    return lax.ppermute(values, "core", [(0, 1), (1, 0)])


def exchange(values, axes):
    return lax.all_to_all(values, axes, 0, 0, tiled=True)


def on_device(
    pair_input,
    token_mask,
    out_check_weights,
    in_check_weights,
    out_norm_gain,
    out_proj,
    out_gate,
    out_final_gain,
    out_final,
    in_norm_gain,
    in_proj,
    in_gate,
    in_final_gain,
    in_final,
    att_norm_gain,
    att_qkv,
    att_bias,
    att_gate,
    att_out,
):
    def row(vector):
        return vector.reshape(1, vector.shape[0])

    tokens = 4 * NT
    mask_v = row(token_mask)
    state_rows = exchange(pair_input.reshape(8, 4, 64, CZ), "q")
    (sent,) = call(
        project_tile,
        [((CM, 32, LANES), BF16)],
        [((CM * 32, LANES), F32)],
        [("s", token_mask), ("v", mask_v), ("v", pair_input.reshape(tokens, CZ)),
         ("v", row(out_norm_gain)), ("v", out_proj)],
    )
    mine = exchange(sent, PLANE)
    state, gate = call(
        gate_rows,
        [((CZ, tokens), BF16), ((CZ, tokens), BF16)],
        [],
        [("v", state_rows), ("v", row(out_norm_gain)), ("v", out_gate)],
    )
    other = swap(mine)
    sent, check_out = call(
        product_rows,
        [((64, 16, LANES), BF16), ((8, 256), F32)],
        [((256, NT), BF16), ((NT, NT), BF16), ((1024, LANES), F32)],
        [("v", mine), ("v", other), ("v", row(out_check_weights))],
    )
    recv = exchange(sent, PLANE)
    sent, state, normed = call(
        project_rows,
        [((CM, 32, LANES), BF16), ((CZ, tokens), F32), ((CZ, tokens), BF16)],
        [((CM * 32, LANES), F32), ((CM * 16, LANES), F32)],
        [("s", token_mask), ("v", mask_v), ("v", recv), ("v", state), ("v", gate),
         ("v", row(out_final_gain)), ("v", out_final), ("v", row(in_norm_gain)), ("v", in_proj)],
    )
    mine = exchange(sent, PLANE)
    (gate,) = call(
        gate_only, [((CZ, tokens), BF16)], [], [("v", normed), ("v", in_gate)]
    )
    other = swap(mine)
    (sent,) = call(
        product_cols,
        [((64, 32, LANES), BF16)],
        [((NT, NT), BF16), ((NT, NT), BF16), ((NT, NT), F32), ((64 * 32, LANES), F32),
         ((1024, LANES), F32)],
        [("v", mine), ("v", other), ("v", row(in_check_weights)), ("v", check_out)],
    )
    recv = exchange(sent, PLANE)
    sent, state, normed = call(
        bias_rows,
        [((64, 64, LANES), BF16), ((CZ, tokens), F32), ((CZ, tokens), BF16)],
        [((CM * 32, LANES), F32), ((64, LANES), F32)],
        [("v", recv), ("v", state), ("v", gate), ("v", row(in_final_gain)), ("v", in_final),
         ("v", row(att_norm_gain)), ("v", att_bias)],
    )
    mine = exchange(sent, PLANE)
    query, key, value, gate, check_row, check_col = call(
        attention_inputs,
        [((CZ, tokens), BF16), ((tokens, CZ), BF16), ((CZ, tokens), BF16), ((CZ, tokens), F32),
         ((32, CM), F32), ((64, CM), F32)],
        [((CM * 16, LANES), F32), ((LANES, CM), F32)],
        [("v", recv), ("v", normed), ("v", att_qkv), ("v", att_gate)],
    )
    other = swap(mine)
    (sent,) = call(
        attend,
        [((8, 4, 64, CZ), BF16)],
        [((2, 64 * 64, LANES), F32), ((HEADS, NT, NT), F32)],
        [("v", mask_v), ("v", mine), ("v", other), ("v", query), ("v", key), ("v", value),
         ("v", gate), ("v", state), ("v", att_out)],
    )
    result = exchange(sent, "q").reshape(32, 64, CZ)
    return result, check_row, check_col


def solution(mesh):
    grid = Mesh(mesh.devices.reshape(8, 2, 8), ("p", "core", "q"))
    tile = P(("p", "core"), "q", None)
    in_specs = (tile,) + (P(),) * 18
    out_specs = (tile, P(("p", "core"), None), P("q", None))
    return jax.shard_map(
        on_device, mesh=grid, in_specs=in_specs, out_specs=out_specs, check_vma=False
    )
```

```python
import jax
import jax.numpy as jnp
from jax import lax
from jax.experimental import pallas as pl
from jax.experimental.pallas import tpu as pltpu
from jax.sharding import Mesh, PartitionSpec as P

F32 = jnp.float32
BF16 = jnp.bfloat16
NT = 512
CZ = 128
CM = 64
HEADS = 4
DH = 32
LANES = 128
CHUNKS = NT // LANES
PLANE = ("p", "q")
VMEM = pl.BlockSpec(memory_space=pltpu.VMEM)
SMEM = pl.BlockSpec(memory_space=pltpu.SMEM)
HBM = pl.BlockSpec(memory_space=pltpu.HBM)
SPECS = {"s": SMEM, "v": VMEM, "h": HBM, "w": VMEM}
LOG2E = 1.4426950408889634


def dot(left, right, left_dim, right_dim):
    return lax.dot_general(
        left, right, (((left_dim,), (right_dim,)), ((), ())), preferred_element_type=F32
    )


def column(row):
    return jnp.transpose(jnp.broadcast_to(row, (8, row.shape[1])))[:, 0:1]


def flipped(weight):
    return jnp.transpose(weight.astype(F32)).astype(BF16)


def eye():
    rows = lax.broadcasted_iota(jnp.int32, (LANES, LANES), 0)
    cols = lax.broadcasted_iota(jnp.int32, (LANES, LANES), 1)
    return jnp.where(rows == cols, 1.0, 0.0).astype(BF16)


def norm(values, gain_col):
    mean = jnp.mean(values, axis=0, keepdims=True)
    centered = values - mean
    variance = jnp.mean(centered * centered, axis=0, keepdims=True)
    return (centered * lax.rsqrt(variance + 1e-05) * gain_col).astype(BF16)


def sigmoid(values):
    return jax.nn.sigmoid(values)


def thirds(values):
    high = values.astype(BF16)
    rest = values - high.astype(F32)
    middle = rest.astype(BF16)
    return high, middle, (rest - middle.astype(F32)).astype(BF16)


def call(kernel, outs, scratch, ins, mib=48):
    def shape_of(shape, kind, place="v"):
        return (pltpu.HBM if place == "h" else jax.ShapeDtypeStruct)(shape, kind)

    def placed(place, value):
        return pltpu.with_memory_space_constraint(value, pltpu.HBM) if place in "hw" else value

    return pl.pallas_call(
        kernel,
        out_shape=tuple(shape_of(*out) for out in outs),
        in_specs=[SPECS[place] for place, _ in ins],
        out_specs=tuple(HBM if out[2:] == ("h",) else VMEM for out in outs),
        scratch_shapes=[
            pltpu.SemaphoreType.DMA(shape) if kind is None else pltpu.VMEM(shape, kind)
            for shape, kind in scratch
        ],
        compiler_params=pltpu.CompilerParams(vmem_limit_bytes=mib * 1024 * 1024),
    )(*[placed(place, value) for place, value in ins])


def span_of(r):
    return pl.ds(r * NT, NT)


def start(copies):
    for copy in copies:
        copy.start()
    return copies


def wait(copies):
    for copy in copies:
        copy.wait()


def first_row():
    return (2 * lax.axis_index("p") + lax.axis_index("core")) * 32


def project_tile(mask_s, mask_v, x, gain, weight, out, stage):
    row0 = first_row()
    shift = lax.rem(NT - 64 * lax.axis_index("q"), NT)
    mask_all = jnp.broadcast_to(mask_v[...].astype(F32), (8, NT))
    col_mask = pltpu.roll(mask_all, shift, 1)[0:1, 0:64]
    gain_col = column(gain[...])
    weight_t = flipped(weight[...])
    unit = eye()
    for group in range(4):
        steps = range(group * 4, group * 4 + 4)
        pieces, masks = [], []
        for s in steps:
            for i in (s, s + 16):
                pieces.append(x[i * 64 : (i + 1) * 64, :])
                masks.append(col_mask * mask_s[row0 + i].astype(F32))
        state = dot(unit, jnp.concatenate(pieces, axis=0), 1, 1)
        mask = jnp.concatenate(masks, axis=1)
        mixed = dot(weight_t, norm(state, gain_col), 1, 0)
        left = sigmoid(mixed[0:CM]) * mixed[CM : 2 * CM] * mask
        right = sigmoid(mixed[2 * CM : 3 * CM]) * mixed[3 * CM : 4 * CM] * mask
        for at, s in enumerate(steps):
            lanes = slice(at * LANES, (at + 1) * LANES)
            stage[pl.ds(s, CM, stride=32), :] = left[:, lanes]
            stage[pl.ds(16 + s, CM, stride=32), :] = right[:, lanes]
    out[...] = stage[...].astype(BF16).reshape(CM, 32, LANES)


OUT_GATE = slice(0, 128)
IN_PROJ = slice(128, 384)
IN_GATE = slice(384, 512)
QUERY = slice(512, 640)
KEY = slice(640, 768)
VALUE = slice(768, 896)
ATT_GATE = slice(896, 1024)
ATT_OUT = slice(1024, 1152)
BIAS = slice(1152, 1156)
PACKED = 1168


def prepare(
    out_norm_gain, out_gate, out_final_gain, out_final, in_norm_gain, in_proj, in_gate,
    in_final_gain, in_final, att_norm_gain, att_qkv, att_bias, att_gate, att_out,
    packed, finals, gains,
):
    packed[OUT_GATE, :] = flipped(out_gate[...])
    packed[IN_PROJ, :] = flipped(in_proj[...])
    packed[IN_GATE, :] = flipped(in_gate[...])
    packed[QUERY, :] = flipped(att_qkv[:, 0:128])
    packed[KEY, :] = att_qkv[:, 128:256]
    packed[VALUE, :] = flipped(att_qkv[:, 256:384])
    packed[ATT_GATE, :] = flipped(att_gate[...])
    packed[ATT_OUT, :] = flipped(att_out[...])
    turned = jnp.concatenate([flipped(att_bias[...]), jnp.zeros((16 - HEADS, CZ), BF16)], axis=0)
    packed[BIAS.start : PACKED, :] = turned
    finals[:, 0:CM] = flipped(out_final[...])
    finals[:, CM : 2 * CM] = flipped(in_final[...])
    pad = jnp.zeros((1, CM), F32)
    rows = [
        out_norm_gain[...],
        in_norm_gain[...],
        att_norm_gain[...],
        jnp.concatenate([out_final_gain[...], pad], axis=1),
        jnp.concatenate([in_final_gain[...], pad], axis=1),
        jnp.zeros((3, CZ), F32),
    ]
    gains[...] = jnp.transpose(jnp.concatenate(rows, axis=0))


def gate_rows(x, packed, gains, state_out, gate_out):
    gain_col = gains[:, 0:1]
    weight_t = packed[OUT_GATE, :]
    unit = eye()
    for r in range(4):
        rows = jnp.concatenate([x[q, r] for q in range(8)], axis=0)
        state = dot(unit, rows, 1, 1)
        span = slice(r * NT, (r + 1) * NT)
        state_out[:, span] = state.astype(BF16)
        gate_out[:, span] = sigmoid(dot(weight_t, norm(state, gain_col), 1, 0)).astype(BF16)


def product_rows(mine, other, weights, out, check_out, left, right, stage):
    core = lax.axis_index("core")
    low = lax.broadcasted_iota(jnp.int32, (16, LANES), 1) < 64

    def paired(ref, src, rows):
        first = ref[src, rows, :].astype(F32)
        second = ref[src + 1, rows, :].astype(F32)
        head = jnp.where(low, first, pltpu.roll(second, 64, 1))
        tail = jnp.where(low, pltpu.roll(first, 64, 1), second)
        return jnp.concatenate([head, tail], axis=0).astype(BF16)

    for p in range(8):
        for a in range(CHUNKS):
            lanes = slice(a * LANES, (a + 1) * LANES)
            src = p * 8 + 2 * a
            left[p * 32 : (p + 1) * 32, lanes] = paired(mine, src, slice(0, 16))
            at = pl.multiple_of(p * 64 + core * 32, 32)
            right[pl.ds(at, 32), lanes] = paired(mine, src, slice(16, 32))
            at = pl.multiple_of(p * 64 + (1 - core) * 32, 32)
            right[pl.ds(at, 32), lanes] = paired(other, src, slice(16, 32))
    product = dot(left[...], right[...], 1, 1)
    for chunk in range(CHUNKS):
        stage[pl.ds(chunk, 256, stride=4), :] = product[:, chunk * LANES : (chunk + 1) * LANES]
    out[...] = stage[...].astype(BF16).reshape(64, 16, LANES)
    weight_rows = jnp.broadcast_to(weights[...].astype(F32), (8, NT)).astype(BF16)
    total = sum(dot(part, left[...], 1, 1) for part in thirds(dot(weight_rows, right[...], 1, 0)))
    check_out[...] = total / NT


def update_rows(recv_stage, stride, r, state, gate, final_gain, final_t):
    product = jnp.concatenate(
        [recv_stage[pl.ds(r * 4 + chunk, CM, stride=stride), :] for chunk in range(CHUNKS)], axis=1
    )
    update = dot(final_t, norm(product, final_gain), 1, 0)
    return state.astype(F32) + gate.astype(F32) * update


def project_rows(
    mask_s, mask_v, recv, state_in, gate, packed, finals, gains, out, state_out, stage, recv_stage
):
    row0 = first_row() + 4 * lax.axis_index("q")
    mask_all = mask_v[...].astype(F32)
    gain_col = gains[:, 1:2]
    final_col = gains[0:CM, 3:4]
    final_t = finals[:, 0:CM]
    weight_t = packed[IN_PROJ, :]
    recv_stage[...] = recv[...].astype(F32).reshape(CM * 16, LANES)
    for r in range(4):
        span = slice(r * NT, (r + 1) * NT)
        state = update_rows(
            recv_stage, 16, r, state_in[:, span], gate[:, span], final_col, final_t
        )
        state_out[:, span] = state.astype(BF16)
        mixed = dot(weight_t, norm(state, gain_col), 1, 0)
        mask = mask_all * mask_s[row0 + r].astype(F32)
        left = sigmoid(mixed[0:CM]) * mixed[CM : 2 * CM] * mask
        right = sigmoid(mixed[2 * CM : 3 * CM]) * mixed[3 * CM : 4 * CM] * mask
        for chunk in range(CHUNKS):
            lanes = slice(chunk * LANES, (chunk + 1) * LANES)
            stage[pl.ds(r * 8 + chunk, CM, stride=32), :] = left[:, lanes]
            stage[pl.ds(r * 8 + 4 + chunk, CM, stride=32), :] = right[:, lanes]
    out[...] = stage[...].astype(BF16).reshape(CM, 32, LANES)


def gate_only(state, packed, gains, gate_out):
    gain_col = gains[:, 1:2]
    weight_t = packed[IN_GATE, :]
    for r in range(4):
        span = slice(r * NT, (r + 1) * NT)
        normed = norm(state[:, span].astype(F32), gain_col)
        gate_out[:, span] = sigmoid(dot(weight_t, normed, 1, 0)).astype(BF16)


def product_cols(mine, other, weights, check_in, out, left, right, product, stage, stage_out):
    core = lax.axis_index("core")
    for side, buf in enumerate((mine, other)):
        stage[...] = buf[...].astype(F32).reshape(64 * 32, LANES)
        rows = slice(side * 256, (side + 1) * 256)
        for chunk in range(CHUNKS):
            lanes = slice(chunk * LANES, (chunk + 1) * LANES)
            left[rows, lanes] = stage[pl.ds(chunk, 256, stride=8), :].astype(BF16)
            right[rows, lanes] = stage[pl.ds(4 + chunk, 256, stride=8), :].astype(BF16)
    product[...] = dot(left[...], right[...], 0, 0)
    for p in range(8):
        rows = product[pl.ds(pl.multiple_of(p * 64 + core * 32, 32), 32), :]
        for chunk in range(CHUNKS):
            stage_out[pl.ds(p * 128 + chunk, 32, stride=4), :] = rows[
                :, chunk * LANES : (chunk + 1) * LANES
            ]
    out[:, 0:16, :] = stage_out[...].astype(BF16).reshape(64, 16, LANES)
    weight_rows = jnp.broadcast_to(weights[...].astype(F32), (8, NT)).astype(BF16)
    total = sum(dot(part, right[...], 1, 0) for part in thirds(dot(weight_rows, left[...], 1, 1)))
    high = check_in[...].astype(BF16).astype(F32)
    lines = []
    for part, count in ((high, 2), (check_in[...] - high, 2), (total / NT, 4)):
        lines += [part[0:1, c * LANES : (c + 1) * LANES] for c in range(count)]
    tail = jnp.concatenate(lines, axis=0).astype(BF16)
    out[:, 16:24, :] = jnp.broadcast_to(tail[None], (64, 8, LANES))


def bias_rows(
    recv, state_in, gate, packed, finals, gains, out, state_out_h, check_row, check_col,
    recv_stage, bias_stage, turn, state_out, sems,
):
    gain_col = gains[:, 2:3]
    final_col = gains[0:CM, 4:5]
    final_t = finals[:, CM : 2 * CM]
    weight_t = packed[BIAS.start : PACKED, :]
    recv_stage[...] = recv[...].astype(F32).reshape(CM * 24, LANES)
    p, q = lax.axis_index("p"), lax.axis_index("q")

    def rows_of(at):
        return recv_stage[pl.ds(at, CM, stride=24), :]

    turn[0] = jnp.transpose(rows_of(16 + p // 4) + rows_of(18 + p // 4))
    check_row[...] = turn[0, pl.ds(pl.multiple_of(lax.rem(p, 4) * 32, 32), 32), :]
    turn[1] = jnp.transpose(rows_of(20 + q // 2))
    check_col[...] = turn[1, pl.ds(pl.multiple_of(lax.rem(q, 2) * 64, 64), 64), :]
    stores = []
    for r in range(4):
        span = slice(r * NT, (r + 1) * NT)
        state = update_rows(recv_stage, 24, r, state_in[:, span], gate[:, span], final_col, final_t)
        state_out[:, span] = state.astype(BF16)
        copy = pltpu.make_async_copy(
            state_out.at[:, span_of(r)], state_out_h.at[:, span_of(r)], sems.at[r]
        )
        stores += start([copy])
        normed = norm(state, gain_col)
        bias = dot(weight_t, normed, 1, 0) * LOG2E
        for chunk in range(CHUNKS):
            bias_stage[pl.ds(r * 16 + chunk, HEADS, stride=4), :] = bias[
                0:HEADS, chunk * LANES : (chunk + 1) * LANES
            ]
    out[...] = jnp.broadcast_to(bias_stage[...].astype(BF16)[None], (64, 64, LANES))
    wait(stores)


def attention_inputs(
    state, packed, gains, query_h, key_h, value_h, gate_h,
    query_out, key_out, value_out, gate_out, sems,
):
    gain_col = gains[:, 2:3]
    query_t = packed[QUERY, :]
    value_t = packed[VALUE, :]
    gate_t = packed[ATT_GATE, :]
    for r in range(4):
        span = slice(r * NT, (r + 1) * NT)
        rows = norm(state[:, span].astype(F32), gain_col)
        query_out[:, span] = (dot(query_t, rows, 1, 0) * (LOG2E * DH ** (-0.5))).astype(BF16)
        key_out[span, :] = dot(rows, packed[KEY, :], 0, 0).astype(BF16)
        value_out[:, span] = dot(value_t, rows, 1, 0).astype(BF16)
        gate_out[:, span] = sigmoid(dot(gate_t, rows, 1, 0))
    pairs = ((query_out, query_h), (key_out, key_h), (value_out, value_h), (gate_out, gate_h))
    wait(
        start(
            [
                pltpu.make_async_copy(source, target, sems.at[at])
                for at, (source, target) in enumerate(pairs)
            ]
        )
    )


def attend(
    mask_v, mine, other, query_h, key_h, value_h, gate_h, state_h, packed, out,
    bias_stage, bias, query, key, value, gate, state, sems,
):
    pairs = ((query_h, query), (key_h, key), (value_h, value), (gate_h, gate), (state_h, state))
    loads = start(
        [
            pltpu.make_async_copy(source, target, sems.at[at])
            for at, (source, target) in enumerate(pairs)
        ]
    )
    core = lax.axis_index("core")
    bias_stage[core] = mine[...].astype(F32).reshape(64 * 64, LANES)
    bias_stage[1 - core] = other[...].astype(F32).reshape(64 * 64, LANES)
    key_bias = jnp.where(mask_v[...] > 0, 0.0, -1000000000.0 * LOG2E).astype(F32)
    key_cols = [column(key_bias[:, c * LANES : (c + 1) * LANES]) for c in range(CHUNKS)]
    weight_t = packed[ATT_OUT, :]

    def turn_bias(h):
        for chunk in range(CHUNKS):
            blocks = [
                bias_stage[plane, pl.ds(p * 512 + h * 4 + chunk, 32, stride=16), :]
                for p in range(8)
                for plane in range(2)
            ]
            turned = jnp.transpose(jnp.concatenate(blocks, axis=0))
            bias[h, chunk * LANES : (chunk + 1) * LANES, :] = turned + key_cols[chunk]

    def scores(h, query_row, key_row):
        zeros = jnp.zeros((DH, NT), BF16)
        masked = jnp.concatenate(
            [query_row[h * DH : (h + 1) * DH] if at == h else zeros for at in range(HEADS)], axis=0
        )
        return dot(key_row, masked, 1, 0) + bias[h]

    def weighted(h, weights, value_row):
        padded = jnp.concatenate(
            [value_row[h * DH : (h + 1) * DH], jnp.ones((16, NT), BF16)], axis=0
        )
        both = dot(padded, weights.astype(BF16), 1, 0)
        return both[0:DH] / both[DH : DH + 1], both[DH : DH + 1]

    def finish(r, span, parts):
        attended = jnp.concatenate(parts, axis=0) * gate[:, span]
        result = state[:, span].astype(F32) + dot(weight_t, attended.astype(BF16), 1, 0)
        out[:, r, :, :] = jnp.transpose(result).astype(BF16).reshape(8, 64, CZ)

    low = high = jnp.ones((1, NT), F32)
    parts = [[] for _ in range(4)]
    for h in range(HEADS):
        turn_bias(h)
        if h == 0:
            wait(loads)
        for r in range(4):
            span = slice(r * NT, (r + 1) * NT)
            weights = jnp.exp2(scores(h, query[:, span], key[span, :]))
            part, total = weighted(h, weights, value[:, span])
            low, high = jnp.minimum(low, total), jnp.maximum(high, total)
            parts[r].append(part)
    for r in range(4):
        finish(r, slice(r * NT, (r + 1) * NT), parts[r])
    in_range = jnp.logical_and(jnp.min(low) > 1e-25, jnp.max(high) < 1e30)

    @pl.when(jnp.logical_not(in_range))
    def _():
        def one_row(r, carry):
            span = pl.ds(pl.multiple_of(r * NT, NT), NT)
            again = []
            for h in range(HEADS):
                values = scores(h, query[:, span], key[span, :])
                weights = jnp.exp2(values - jnp.max(values, axis=0, keepdims=True))
                again.append(weighted(h, weights, value[:, span])[0])
            finish(r, span, again)
            return carry

        lax.fori_loop(0, 4, one_row, 0)


def swap(values):
    return lax.ppermute(values, "core", [(0, 1), (1, 0)])


def exchange(values, axes):
    return lax.all_to_all(values, axes, 0, 0, tiled=True)


def on_device(
    pair_input,
    token_mask,
    out_check_weights,
    in_check_weights,
    out_norm_gain,
    out_proj,
    out_gate,
    out_final_gain,
    out_final,
    in_norm_gain,
    in_proj,
    in_gate,
    in_final_gain,
    in_final,
    att_norm_gain,
    att_qkv,
    att_bias,
    att_gate,
    att_out,
):
    def row(vector):
        return vector.reshape(1, vector.shape[0])

    tokens = 4 * NT
    mask_v = row(token_mask)
    state_rows = exchange(pair_input.reshape(8, 4, 64, CZ), "q")
    (sent,) = call(
        project_tile,
        [((CM, 32, LANES), BF16)],
        [((CM * 32, LANES), F32)],
        [("s", token_mask), ("v", mask_v), ("v", pair_input.reshape(tokens, CZ)),
         ("v", row(out_norm_gain)), ("v", out_proj)],
    )
    state_rows, sent = lax.optimization_barrier((state_rows, sent))
    mine = exchange(sent, PLANE)
    gain_out, _ = lax.optimization_barrier((row(out_norm_gain), sent))
    packed, finals, gains = call(
        prepare,
        [((PACKED, CZ), BF16), ((CZ, CZ), BF16), ((CZ, 8), F32)],
        [],
        [("v", value) for value in (
            gain_out, out_gate, row(out_final_gain), out_final,
            row(in_norm_gain), in_proj, in_gate, row(in_final_gain), in_final,
            row(att_norm_gain), att_qkv, att_bias, att_gate, att_out,
        )],
    )
    wide = (CZ, tokens)
    state, gate = call(
        gate_rows,
        [(wide, BF16), (wide, BF16)],
        [],
        [("v", state_rows), ("v", packed), ("v", gains)],
    )
    mine, state, gate = lax.optimization_barrier((mine, state, gate))
    other = swap(mine)
    sent, check_out = call(
        product_rows,
        [((64, 16, LANES), BF16), ((8, 256), F32)],
        [((256, NT), BF16), ((NT, NT), BF16), ((1024, LANES), F32)],
        [("v", mine), ("v", other), ("v", row(out_check_weights))],
    )
    recv = exchange(sent, PLANE)
    sent, state = call(
        project_rows,
        [((CM, 32, LANES), BF16), (wide, BF16)],
        [((CM * 32, LANES), F32), ((CM * 16, LANES), F32)],
        [("s", token_mask), ("v", mask_v), ("v", recv), ("v", state), ("v", gate),
         ("v", packed), ("v", finals), ("v", gains)],
    )
    mine = exchange(sent, PLANE)
    (gate,) = call(
        gate_only, [(wide, BF16)], [], [("v", state), ("v", packed), ("v", gains)]
    )
    mine, gate = lax.optimization_barrier((mine, gate))
    other = swap(mine)
    (sent,) = call(
        product_cols,
        [((64, 24, LANES), BF16)],
        [((NT, NT), BF16), ((NT, NT), BF16), ((NT, NT), F32), ((64 * 32, LANES), F32),
         ((1024, LANES), F32)],
        [("v", mine), ("v", other), ("v", row(in_check_weights)), ("v", check_out)],
    )
    recv = exchange(sent, PLANE)
    sent, state, check_row, check_col = call(
        bias_rows,
        [((64, 64, LANES), BF16), (wide, BF16, "h"), ((32, CM), F32), ((64, CM), F32)],
        [((CM * 24, LANES), F32), ((64, LANES), F32), ((2, LANES, CM), F32), (wide, BF16),
         ((4,), None)],
        [("v", recv), ("v", state), ("v", gate), ("v", packed), ("v", finals), ("v", gains)],
    )
    mine = exchange(sent, PLANE)
    query, key, value, gate = call(
        attention_inputs,
        [(wide, BF16, "h"), ((tokens, CZ), BF16, "h"), (wide, BF16, "h"), (wide, F32, "h")],
        [(wide, BF16), ((tokens, CZ), BF16), (wide, BF16), (wide, F32), ((4,), None)],
        [("w", state), ("v", packed), ("v", gains)],
    )
    mine, query = lax.optimization_barrier((mine, query))
    other = swap(mine)
    (sent,) = call(
        attend,
        [((8, 4, 64, CZ), BF16)],
        [((2, 64 * 64, LANES), F32), ((HEADS, NT, NT), F32), (wide, BF16), ((tokens, CZ), BF16),
         (wide, BF16), (wide, F32), (wide, BF16), ((5,), None)],
        [("v", mask_v), ("v", mine), ("v", other), ("h", query), ("h", key), ("h", value),
         ("h", gate), ("h", state), ("v", packed)],
    )
    result = exchange(sent, "q").reshape(32, 64, CZ)
    return result, check_row, check_col


def solution(mesh):
    grid = Mesh(mesh.devices.reshape(8, 2, 8), ("p", "core", "q"))
    tile = P(("p", "core"), "q", None)
    in_specs = (tile,) + (P(),) * 18
    out_specs = (tile, P(("p", "core"), None), P("q", None))
    return jax.shard_map(
        on_device, mesh=grid, in_specs=in_specs, out_specs=out_specs, check_vma=False
    )
```

```python
import jax
import jax.numpy as jnp
from jax import lax
from jax.experimental import pallas as pl
from jax.experimental.pallas import tpu as pltpu
from jax.sharding import Mesh, PartitionSpec as P

F32 = jnp.float32
BF16 = jnp.bfloat16
NT = 512
CZ = 128
CM = 64
HEADS = 4
DH = 32
LANES = 128
CHUNKS = NT // LANES
PLANE = ("p", "q")
VMEM = pl.BlockSpec(memory_space=pltpu.VMEM)
SMEM = pl.BlockSpec(memory_space=pltpu.SMEM)
HBM = pl.BlockSpec(memory_space=pltpu.HBM)
SPECS = {"s": SMEM, "v": VMEM, "h": HBM, "w": VMEM}
LOG2E = 1.4426950408889634


def dot(left, right, left_dim, right_dim):
    return lax.dot_general(
        left, right, (((left_dim,), (right_dim,)), ((), ())), preferred_element_type=F32
    )


def column(row):
    return jnp.transpose(jnp.broadcast_to(row, (8, row.shape[1])))[:, 0:1]


def flipped(weight):
    return jnp.transpose(weight.astype(F32)).astype(BF16)


def eye():
    rows = lax.broadcasted_iota(jnp.int32, (LANES, LANES), 0)
    cols = lax.broadcasted_iota(jnp.int32, (LANES, LANES), 1)
    return jnp.where(rows == cols, 1.0, 0.0).astype(BF16)


def norm(values, gain_col):
    mean = jnp.mean(values, axis=0, keepdims=True)
    centered = values - mean
    variance = jnp.mean(centered * centered, axis=0, keepdims=True)
    return (centered * lax.rsqrt(variance + 1e-05) * gain_col).astype(BF16)


def sigmoid(values):
    return jax.nn.sigmoid(values)


def thirds(values):
    high = values.astype(BF16)
    rest = values - high.astype(F32)
    middle = rest.astype(BF16)
    return high, middle, (rest - middle.astype(F32)).astype(BF16)


def call(kernel, outs, scratch, ins, mib=48):
    def shape_of(shape, kind, place="v"):
        return (pltpu.HBM if place == "h" else jax.ShapeDtypeStruct)(shape, kind)

    def placed(place, value):
        return pltpu.with_memory_space_constraint(value, pltpu.HBM) if place in "hw" else value

    return pl.pallas_call(
        kernel,
        out_shape=tuple(shape_of(*out) for out in outs),
        in_specs=[SPECS[place] for place, _ in ins],
        out_specs=tuple(HBM if out[2:] == ("h",) else VMEM for out in outs),
        scratch_shapes=[
            pltpu.SemaphoreType.DMA(shape) if kind is None else pltpu.VMEM(shape, kind)
            for shape, kind in scratch
        ],
        compiler_params=pltpu.CompilerParams(vmem_limit_bytes=mib * 1024 * 1024),
    )(*[placed(place, value) for place, value in ins])


def start(copies):
    for copy in copies:
        copy.start()
    return copies


def wait(copies):
    for copy in copies:
        copy.wait()


def first_row():
    return (2 * lax.axis_index("p") + lax.axis_index("core")) * 32


def project_tile(mask_s, mask_v, x, gain, weight, out, stage):
    row0 = first_row()
    shift = lax.rem(NT - 64 * lax.axis_index("q"), NT)
    mask_all = jnp.broadcast_to(mask_v[...].astype(F32), (8, NT))
    col_mask = pltpu.roll(mask_all, shift, 1)[0:1, 0:64]
    gain_col = column(gain[...])
    weight_t = flipped(weight[...])
    unit = eye()
    for group in range(4):
        steps = range(group * 4, group * 4 + 4)
        pieces, masks = [], []
        for s in steps:
            for i in (s, s + 16):
                pieces.append(x[i * 64 : (i + 1) * 64, :])
                masks.append(col_mask * mask_s[row0 + i].astype(F32))
        state = dot(unit, jnp.concatenate(pieces, axis=0), 1, 1)
        mask = jnp.concatenate(masks, axis=1)
        mixed = dot(weight_t, norm(state, gain_col), 1, 0)
        left = sigmoid(mixed[0:CM]) * mixed[CM : 2 * CM] * mask
        right = sigmoid(mixed[2 * CM : 3 * CM]) * mixed[3 * CM : 4 * CM] * mask
        for at, s in enumerate(steps):
            lanes = slice(at * LANES, (at + 1) * LANES)
            stage[pl.ds(s, CM, stride=32), :] = left[:, lanes]
            stage[pl.ds(16 + s, CM, stride=32), :] = right[:, lanes]
    out[...] = stage[...].astype(BF16).reshape(CM, 32, LANES)


OUT_GATE = slice(0, 128)
IN_PROJ = slice(128, 384)
IN_GATE = slice(384, 512)
QUERY = slice(512, 640)
KEY = slice(640, 768)
VALUE = slice(768, 896)
ATT_GATE = slice(896, 1024)
ATT_OUT = slice(1024, 1152)
BIAS = slice(1152, 1156)
PACKED = 1168


def prepare(*refs):
    sources, (packed, finals, gains), targets, sems = refs[:14], refs[14:17], refs[17:31], refs[31]
    wait(
        start(
            [
                pltpu.make_async_copy(source, target, sems.at[at])
                for at, (source, target) in enumerate(zip(sources, targets))
            ]
        )
    )
    (
        out_norm_gain, out_gate, out_final_gain, out_final, in_norm_gain, in_proj, in_gate,
        in_final_gain, in_final, att_norm_gain, att_qkv, att_bias, att_gate, att_out,
    ) = targets
    packed[OUT_GATE, :] = flipped(out_gate[...])
    packed[IN_PROJ, :] = flipped(in_proj[...])
    packed[IN_GATE, :] = flipped(in_gate[...])
    packed[QUERY, :] = flipped(att_qkv[:, 0:128])
    packed[KEY, :] = att_qkv[:, 128:256]
    packed[VALUE, :] = flipped(att_qkv[:, 256:384])
    packed[ATT_GATE, :] = flipped(att_gate[...])
    packed[ATT_OUT, :] = flipped(att_out[...])
    turned = jnp.concatenate([att_bias[...], jnp.zeros((16 - HEADS, CZ), BF16)], axis=0)
    packed[BIAS.start : PACKED, :] = turned
    finals[:, 0:CM] = flipped(out_final[...])
    finals[:, CM : 2 * CM] = flipped(in_final[...])
    pad = jnp.zeros((1, CM), F32)
    rows = [
        out_norm_gain[...],
        in_norm_gain[...],
        att_norm_gain[...],
        jnp.concatenate([out_final_gain[...], pad], axis=1),
        jnp.concatenate([in_final_gain[...], pad], axis=1),
        jnp.zeros((3, CZ), F32),
    ]
    gains[...] = jnp.transpose(jnp.concatenate(rows, axis=0))


def gate_rows(x, packed, gains, state_out, gate_out):
    gain_col = gains[:, 0:1]
    weight_t = packed[OUT_GATE, :]
    unit = eye()
    for r in range(4):
        rows = jnp.concatenate([x[q, r] for q in range(8)], axis=0)
        state = dot(unit, rows, 1, 1)
        span = slice(r * NT, (r + 1) * NT)
        state_out[:, span] = state.astype(BF16)
        gate_out[:, span] = sigmoid(dot(weight_t, norm(state, gain_col), 1, 0)).astype(BF16)


def product_rows(mine, other, weights, out, check_out, left, right, stage):
    core = lax.axis_index("core")
    low = lax.broadcasted_iota(jnp.int32, (16, LANES), 1) < 64

    def paired(ref, src, rows):
        first = ref[src, rows, :].astype(F32)
        second = ref[src + 1, rows, :].astype(F32)
        head = jnp.where(low, first, pltpu.roll(second, 64, 1))
        tail = jnp.where(low, pltpu.roll(first, 64, 1), second)
        return jnp.concatenate([head, tail], axis=0).astype(BF16)

    for p in range(8):
        for a in range(CHUNKS):
            lanes = slice(a * LANES, (a + 1) * LANES)
            src = p * 8 + 2 * a
            left[p * 32 : (p + 1) * 32, lanes] = paired(mine, src, slice(0, 16))
            at = pl.multiple_of(p * 64 + core * 32, 32)
            right[pl.ds(at, 32), lanes] = paired(mine, src, slice(16, 32))
            at = pl.multiple_of(p * 64 + (1 - core) * 32, 32)
            right[pl.ds(at, 32), lanes] = paired(other, src, slice(16, 32))
    product = dot(left[...], right[...], 1, 1)
    for chunk in range(CHUNKS):
        stage[pl.ds(chunk, 256, stride=4), :] = product[:, chunk * LANES : (chunk + 1) * LANES]
    out[...] = stage[...].astype(BF16).reshape(64, 16, LANES)
    weight_rows = jnp.broadcast_to(weights[...].astype(F32), (8, NT)).astype(BF16)
    total = sum(dot(part, left[...], 1, 1) for part in thirds(dot(weight_rows, right[...], 1, 0)))
    check_out[...] = total / NT


def update_rows(recv_stage, stride, r, state, gate, final_gain, final_t):
    product = jnp.concatenate(
        [recv_stage[pl.ds(r * 4 + chunk, CM, stride=stride), :] for chunk in range(CHUNKS)], axis=1
    )
    update = dot(final_t, norm(product, final_gain), 1, 0)
    return state.astype(F32) + gate.astype(F32) * update


def project_rows(
    mask_s, mask_v, recv, state_in, gate, packed, finals, gains, out, state_out, stage, recv_stage
):
    row0 = first_row() + 4 * lax.axis_index("q")
    mask_all = mask_v[...].astype(F32)
    gain_col = gains[:, 1:2]
    final_col = gains[0:CM, 3:4]
    final_t = finals[:, 0:CM]
    weight_t = packed[IN_PROJ, :]
    recv_stage[...] = recv[...].astype(F32).reshape(CM * 16, LANES)
    for r in range(4):
        span = slice(r * NT, (r + 1) * NT)
        state = update_rows(
            recv_stage, 16, r, state_in[:, span], gate[:, span], final_col, final_t
        )
        state_out[:, span] = state.astype(BF16)
        mixed = dot(weight_t, norm(state, gain_col), 1, 0)
        mask = mask_all * mask_s[row0 + r].astype(F32)
        left = sigmoid(mixed[0:CM]) * mixed[CM : 2 * CM] * mask
        right = sigmoid(mixed[2 * CM : 3 * CM]) * mixed[3 * CM : 4 * CM] * mask
        for chunk in range(CHUNKS):
            lanes = slice(chunk * LANES, (chunk + 1) * LANES)
            stage[pl.ds(r * 8 + chunk, CM, stride=32), :] = left[:, lanes]
            stage[pl.ds(r * 8 + 4 + chunk, CM, stride=32), :] = right[:, lanes]
    out[...] = stage[...].astype(BF16).reshape(CM, 32, LANES)


def gate_only(state, packed, gains, gate_out):
    gain_col = gains[:, 1:2]
    weight_t = packed[IN_GATE, :]
    for r in range(4):
        span = slice(r * NT, (r + 1) * NT)
        normed = norm(state[:, span].astype(F32), gain_col)
        gate_out[:, span] = sigmoid(dot(weight_t, normed, 1, 0)).astype(BF16)


def product_cols(mine, other, weights, check_in, out, left, right, product, stage, stage_out):
    core = lax.axis_index("core")
    for side, buf in enumerate((mine, other)):
        stage[...] = buf[...].astype(F32).reshape(64 * 32, LANES)
        rows = slice(side * 256, (side + 1) * 256)
        for chunk in range(CHUNKS):
            lanes = slice(chunk * LANES, (chunk + 1) * LANES)
            left[rows, lanes] = stage[pl.ds(chunk, 256, stride=8), :].astype(BF16)
            right[rows, lanes] = stage[pl.ds(4 + chunk, 256, stride=8), :].astype(BF16)
    product[...] = dot(left[...], right[...], 0, 0)
    for p in range(8):
        rows = product[pl.ds(pl.multiple_of(p * 64 + core * 32, 32), 32), :]
        for chunk in range(CHUNKS):
            stage_out[pl.ds(p * 128 + chunk, 32, stride=4), :] = rows[
                :, chunk * LANES : (chunk + 1) * LANES
            ]
    out[:, 0:16, :] = stage_out[...].astype(BF16).reshape(64, 16, LANES)
    weight_rows = jnp.broadcast_to(weights[...].astype(F32), (8, NT)).astype(BF16)
    total = sum(dot(part, right[...], 1, 0) for part in thirds(dot(weight_rows, left[...], 1, 1)))
    high = check_in[...].astype(BF16).astype(F32)
    lines = []
    for part, count in ((high, 2), (check_in[...] - high, 2), (total / NT, 4)):
        lines += [part[0:1, c * LANES : (c + 1) * LANES] for c in range(count)]
    tail = jnp.concatenate(lines, axis=0).astype(BF16)
    out[:, 16:24, :] = jnp.broadcast_to(tail[None], (64, 8, LANES))


def bias_rows(
    recv, state_in, gate, packed, finals, gains, out, state_out, check_row, check_col,
    recv_stage, bias_stage, turn,
):
    gain_col = gains[:, 2:3]
    final_col = gains[0:CM, 4:5]
    final_t = finals[:, CM : 2 * CM]
    weight_t = packed[BIAS.start : PACKED, :]
    recv_stage[...] = recv[...].astype(F32).reshape(CM * 24, LANES)
    p, q = lax.axis_index("p"), lax.axis_index("q")

    def rows_of(at):
        return recv_stage[pl.ds(at, CM, stride=24), :]

    turn[0] = jnp.transpose(rows_of(16 + p // 4) + rows_of(18 + p // 4))
    check_row[...] = turn[0, pl.ds(pl.multiple_of(lax.rem(p, 4) * 32, 32), 32), :]
    turn[1] = jnp.transpose(rows_of(20 + q // 2))
    check_col[...] = turn[1, pl.ds(pl.multiple_of(lax.rem(q, 2) * 64, 64), 64), :]
    for r in range(4):
        span = slice(r * NT, (r + 1) * NT)
        state = update_rows(recv_stage, 24, r, state_in[:, span], gate[:, span], final_col, final_t)
        state_out[:, span] = state.astype(BF16)
        normed = norm(state, gain_col)
        bias = dot(weight_t, normed, 1, 0) * LOG2E
        for chunk in range(CHUNKS):
            bias_stage[pl.ds(r * 16 + chunk, HEADS, stride=4), :] = bias[
                0:HEADS, chunk * LANES : (chunk + 1) * LANES
            ]
    out[...] = jnp.broadcast_to(bias_stage[...].astype(BF16)[None], (64, 64, LANES))


def attention_inputs(state, packed, gains, query_out, key_out, value_out, gate_out):
    gain_col = gains[:, 2:3]
    for r in range(4):
        span = slice(r * NT, (r + 1) * NT)
        rows = norm(state[:, span].astype(F32), gain_col)
        query_out[:, span] = (dot(packed[QUERY, :], rows, 1, 0) * (LOG2E * DH ** (-0.5))).astype(
            BF16
        )
        key_out[span, :] = dot(rows, packed[KEY, :], 0, 0).astype(BF16)
        value_out[:, span] = dot(packed[VALUE, :], rows, 1, 0).astype(BF16)
        gate_out[:, span] = sigmoid(dot(packed[ATT_GATE, :], rows, 1, 0)).astype(BF16)


def attend(
    mask_v, mine, other, query, key, value, gate, state, packed, out, bias_stage, bias
):
    core = lax.axis_index("core")
    bias_stage[core] = mine[...].astype(F32).reshape(64 * 64, LANES)
    bias_stage[1 - core] = other[...].astype(F32).reshape(64 * 64, LANES)
    key_bias = jnp.where(mask_v[...] > 0, 0.0, -1000000000.0 * LOG2E).astype(F32)
    key_cols = [column(key_bias[:, c * LANES : (c + 1) * LANES]) for c in range(CHUNKS)]
    weight_t = packed[ATT_OUT, :]

    def turn_bias(h):
        for chunk in range(CHUNKS):
            blocks = [
                bias_stage[plane, pl.ds(p * 512 + h * 4 + chunk, 32, stride=16), :]
                for p in range(8)
                for plane in range(2)
            ]
            turned = jnp.transpose(jnp.concatenate(blocks, axis=0))
            bias[h, chunk * LANES : (chunk + 1) * LANES, :] = turned + key_cols[chunk]

    def scores(h, query_row, key_row):
        zeros = jnp.zeros((DH, NT), BF16)
        masked = jnp.concatenate(
            [query_row[h * DH : (h + 1) * DH] if at == h else zeros for at in range(HEADS)], axis=0
        )
        return dot(key_row, masked, 1, 0) + bias[h]

    def weighted(h, weights, value_row):
        padded = jnp.concatenate(
            [value_row[h * DH : (h + 1) * DH], jnp.ones((16, NT), BF16)], axis=0
        )
        both = dot(padded, weights.astype(BF16), 1, 0)
        return both[0:DH] / both[DH : DH + 1], both[DH : DH + 1]

    def finish(r, span, parts):
        attended = jnp.concatenate(parts, axis=0) * gate[:, span].astype(F32)
        result = state[:, span].astype(F32) + dot(weight_t, attended.astype(BF16), 1, 0)
        out[:, r, :, :] = jnp.transpose(result).astype(BF16).reshape(8, 64, CZ)

    low = high = jnp.ones((1, NT), F32)
    parts = [[] for _ in range(4)]
    for h in range(HEADS):
        turn_bias(h)
        for r in range(4):
            span = slice(r * NT, (r + 1) * NT)
            weights = jnp.exp2(scores(h, query[:, span], key[span, :]))
            part, total = weighted(h, weights, value[:, span])
            low, high = jnp.minimum(low, total), jnp.maximum(high, total)
            parts[r].append(part)
    for r in range(4):
        finish(r, slice(r * NT, (r + 1) * NT), parts[r])
    in_range = jnp.logical_and(jnp.min(low) > 1e-25, jnp.max(high) < 1e30)

    @pl.when(jnp.logical_not(in_range))
    def _():
        def one_row(r, carry):
            span = pl.ds(pl.multiple_of(r * NT, NT), NT)
            again = []
            for h in range(HEADS):
                values = scores(h, query[:, span], key[span, :])
                weights = jnp.exp2(values - jnp.max(values, axis=0, keepdims=True))
                again.append(weighted(h, weights, value[:, span])[0])
            finish(r, span, again)
            return carry

        lax.fori_loop(0, 4, one_row, 0)


def swap(values):
    return lax.ppermute(values, "core", [(0, 1), (1, 0)])


def exchange(values, axes):
    return lax.all_to_all(values, axes, 0, 0, tiled=True)


def on_device(
    pair_input,
    token_mask,
    out_check_weights,
    in_check_weights,
    out_norm_gain,
    out_proj,
    out_gate,
    out_final_gain,
    out_final,
    in_norm_gain,
    in_proj,
    in_gate,
    in_final_gain,
    in_final,
    att_norm_gain,
    att_qkv,
    att_bias,
    att_gate,
    att_out,
):
    def row(vector):
        return vector.reshape(1, vector.shape[0])

    tokens = 4 * NT
    mask_v = row(token_mask)
    state_rows = exchange(pair_input.reshape(8, 4, 64, CZ), "q")
    (sent,) = call(
        project_tile,
        [((CM, 32, LANES), BF16)],
        [((CM * 32, LANES), F32)],
        [("s", token_mask), ("w", mask_v), ("w", pair_input.reshape(tokens, CZ)),
         ("w", row(out_norm_gain)), ("w", out_proj)],
    )
    state_rows, sent = lax.optimization_barrier((state_rows, sent))
    mine = exchange(sent, PLANE)
    gain_out, _ = lax.optimization_barrier((row(out_norm_gain), sent))
    weights = (
        gain_out, out_gate, row(out_final_gain), out_final, row(in_norm_gain), in_proj, in_gate,
        row(in_final_gain), in_final, row(att_norm_gain), att_qkv, att_bias.T, att_gate, att_out,
    )
    packed, finals, gains = call(
        prepare,
        [((PACKED, CZ), BF16), ((CZ, CZ), BF16), ((CZ, 8), F32)],
        [(value.shape, value.dtype) for value in weights] + [((14,), None)],
        [("h", value) for value in weights],
    )
    wide = (CZ, tokens)
    state, gate = call(
        gate_rows,
        [(wide, BF16), (wide, BF16)],
        [],
        [("v", state_rows), ("v", packed), ("v", gains)],
    )
    mine, state, gate = lax.optimization_barrier((mine, state, gate))
    other = swap(mine)
    sent, check_out = call(
        product_rows,
        [((64, 16, LANES), BF16), ((8, 256), F32)],
        [((256, NT), BF16), ((NT, NT), BF16), ((1024, LANES), F32)],
        [("v", mine), ("v", other), ("v", row(out_check_weights))],
    )
    recv = exchange(sent, PLANE)
    sent, state = call(
        project_rows,
        [((CM, 32, LANES), BF16), (wide, BF16)],
        [((CM * 32, LANES), F32), ((CM * 16, LANES), F32)],
        [("s", token_mask), ("v", mask_v), ("v", recv), ("v", state), ("v", gate),
         ("v", packed), ("v", finals), ("v", gains)],
    )
    mine = exchange(sent, PLANE)
    mine, state = lax.optimization_barrier((mine, state))
    other = swap(mine)
    (gate,) = call(
        gate_only, [(wide, BF16)], [], [("v", state), ("v", packed), ("v", gains)]
    )
    other, gate = lax.optimization_barrier((other, gate))
    (sent,) = call(
        product_cols,
        [((64, 24, LANES), BF16)],
        [((NT, NT), BF16), ((NT, NT), BF16), ((NT, NT), F32), ((64 * 32, LANES), F32),
         ((1024, LANES), F32)],
        [("v", mine), ("v", other), ("v", row(in_check_weights)), ("v", check_out)],
    )
    recv = exchange(sent, PLANE)
    sent, state, check_row, check_col = call(
        bias_rows,
        [((64, 64, LANES), BF16), (wide, BF16), ((32, CM), F32), ((64, CM), F32)],
        [((CM * 24, LANES), F32), ((64, LANES), F32), ((2, LANES, CM), F32)],
        [("v", recv), ("v", state), ("v", gate), ("v", packed), ("v", finals), ("v", gains)],
    )
    mine = exchange(sent, PLANE)
    mine, state = lax.optimization_barrier((mine, state))
    other = swap(mine)
    query, key, value, gate = call(
        attention_inputs,
        [(wide, BF16), ((tokens, CZ), BF16), (wide, BF16), (wide, BF16)],
        [],
        [("v", state), ("v", packed), ("v", gains)],
    )
    other, query = lax.optimization_barrier((other, query))
    (sent,) = call(
        attend,
        [((8, 4, 64, CZ), BF16)],
        [((2, 64 * 64, LANES), F32), ((HEADS, NT, NT), F32)],
        [("v", mask_v), ("v", mine), ("v", other), ("v", query), ("v", key), ("v", value),
         ("v", gate), ("v", state), ("v", packed)],
    )
    result = exchange(sent, "q").reshape(32, 64, CZ)
    return result, check_row, check_col


def solution(mesh):
    grid = Mesh(mesh.devices.reshape(8, 2, 8), ("p", "core", "q"))
    tile = P(("p", "core"), "q", None)
    in_specs = (tile,) + (P(),) * 18
    out_specs = (tile, P(("p", "core"), None), P("q", None))
    return jax.shard_map(
        on_device, mesh=grid, in_specs=in_specs, out_specs=out_specs, check_vma=False
    )
```

```python
import jax
import jax.numpy as jnp
from jax import lax
from jax.experimental import pallas as pl
from jax.experimental.pallas import tpu as pltpu
from jax.sharding import Mesh, PartitionSpec as P

F32 = jnp.float32
BF16 = jnp.bfloat16
NT = 512
CZ = 128
CM = 64
HEADS = 4
DH = 32
LANES = 128
CHUNKS = NT // LANES
PLANE = ("p", "q")
VMEM = pl.BlockSpec(memory_space=pltpu.VMEM)
SMEM = pl.BlockSpec(memory_space=pltpu.SMEM)
HBM = pl.BlockSpec(memory_space=pltpu.HBM)
SPECS = {"s": SMEM, "v": VMEM, "h": HBM, "w": VMEM}
LOG2E = 1.4426950408889634


def dot(left, right, left_dim, right_dim):
    return lax.dot_general(
        left, right, (((left_dim,), (right_dim,)), ((), ())), preferred_element_type=F32
    )


def column(row):
    return jnp.transpose(jnp.broadcast_to(row, (8, row.shape[1])))[:, 0:1]


def flipped(weight):
    return jnp.transpose(weight.astype(F32)).astype(BF16)


def eye():
    rows = lax.broadcasted_iota(jnp.int32, (LANES, LANES), 0)
    cols = lax.broadcasted_iota(jnp.int32, (LANES, LANES), 1)
    return jnp.where(rows == cols, 1.0, 0.0).astype(BF16)


def norm(values, gain_col):
    mean = jnp.mean(values, axis=0, keepdims=True)
    centered = values - mean
    variance = jnp.mean(centered * centered, axis=0, keepdims=True)
    return (centered * lax.rsqrt(variance + 1e-05) * gain_col).astype(BF16)


def sigmoid(values):
    return jax.nn.sigmoid(values)


def thirds(values):
    high = values.astype(BF16)
    rest = values - high.astype(F32)
    middle = rest.astype(BF16)
    return high, middle, (rest - middle.astype(F32)).astype(BF16)


def call(kernel, outs, scratch, ins, mib=48):
    def shape_of(shape, kind, place="v"):
        return (pltpu.HBM if place == "h" else jax.ShapeDtypeStruct)(shape, kind)

    def placed(place, value):
        return pltpu.with_memory_space_constraint(value, pltpu.HBM) if place in "hw" else value

    return pl.pallas_call(
        kernel,
        out_shape=tuple(shape_of(*out) for out in outs),
        in_specs=[SPECS[place] for place, _ in ins],
        out_specs=tuple(HBM if out[2:] == ("h",) else VMEM for out in outs),
        scratch_shapes=[
            pltpu.SemaphoreType.DMA(shape) if kind is None else pltpu.VMEM(shape, kind)
            for shape, kind in scratch
        ],
        compiler_params=pltpu.CompilerParams(vmem_limit_bytes=mib * 1024 * 1024),
    )(*[placed(place, value) for place, value in ins])


def start(copies):
    for copy in copies:
        copy.start()
    return copies


def wait(copies):
    for copy in copies:
        copy.wait()


def first_row():
    return (2 * lax.axis_index("p") + lax.axis_index("core")) * 32


def project_tile(mask_s, mask_v, x, gain, weight, out, stage):
    row0 = first_row()
    shift = lax.rem(NT - 64 * lax.axis_index("q"), NT)
    mask_all = jnp.broadcast_to(mask_v[...].astype(F32), (8, NT))
    col_mask = pltpu.roll(mask_all, shift, 1)[0:1, 0:64]
    gain_col = column(gain[...])
    weight_t = flipped(weight[...])
    unit = eye()
    for group in range(4):
        steps = range(group * 4, group * 4 + 4)
        pieces, masks = [], []
        for s in steps:
            for i in (s, s + 16):
                pieces.append(x[i * 64 : (i + 1) * 64, :])
                masks.append(col_mask * mask_s[row0 + i].astype(F32))
        state = dot(unit, jnp.concatenate(pieces, axis=0), 1, 1)
        mask = jnp.concatenate(masks, axis=1)
        mixed = dot(weight_t, norm(state, gain_col), 1, 0)
        left = sigmoid(mixed[0:CM]) * mixed[CM : 2 * CM] * mask
        right = sigmoid(mixed[2 * CM : 3 * CM]) * mixed[3 * CM : 4 * CM] * mask
        for at, s in enumerate(steps):
            lanes = slice(at * LANES, (at + 1) * LANES)
            stage[pl.ds(s, CM, stride=32), :] = left[:, lanes]
            stage[pl.ds(16 + s, CM, stride=32), :] = right[:, lanes]
    out[...] = stage[...].astype(BF16).reshape(CM, 32, LANES)


OUT_GATE = slice(0, 128)
IN_PROJ = slice(128, 384)
IN_GATE = slice(384, 512)
QUERY = slice(512, 640)
KEY = slice(640, 768)
VALUE = slice(768, 896)
ATT_GATE = slice(896, 1024)
ATT_OUT = slice(1024, 1152)
BIAS = slice(1152, 1156)
PACKED = 1168
COUNT = 17
MASK = slice(0, 1)
OUT_CHECK = slice(8, 16)
IN_CHECK = slice(16, 24)


def prepare(*refs):
    sources, (packed, finals, gains, lines) = refs[:COUNT], refs[COUNT : COUNT + 4]
    targets, sems = refs[COUNT + 4 : 2 * COUNT + 4], refs[2 * COUNT + 4]
    wait(
        start(
            [
                pltpu.make_async_copy(source, target, sems.at[at])
                for at, (source, target) in enumerate(zip(sources, targets))
            ]
        )
    )
    (
        out_norm_gain, out_gate, out_final_gain, out_final, in_norm_gain, in_proj, in_gate,
        in_final_gain, in_final, att_norm_gain, att_qkv, att_bias, att_gate, att_out,
        mask, out_check, in_check,
    ) = targets
    for at, line in enumerate((mask, out_check, in_check)):
        lines[at * 8 : (at + 1) * 8, :] = jnp.broadcast_to(line[...].astype(F32), (8, NT))
    packed[OUT_GATE, :] = flipped(out_gate[...])
    packed[IN_PROJ, :] = flipped(in_proj[...])
    packed[IN_GATE, :] = flipped(in_gate[...])
    packed[QUERY, :] = flipped(att_qkv[:, 0:128])
    packed[KEY, :] = att_qkv[:, 128:256]
    packed[VALUE, :] = flipped(att_qkv[:, 256:384])
    packed[ATT_GATE, :] = flipped(att_gate[...])
    packed[ATT_OUT, :] = flipped(att_out[...])
    turned = jnp.concatenate([att_bias[...], jnp.zeros((16 - HEADS, CZ), BF16)], axis=0)
    packed[BIAS.start : PACKED, :] = turned
    finals[:, 0:CM] = flipped(out_final[...])
    finals[:, CM : 2 * CM] = flipped(in_final[...])
    pad = jnp.zeros((1, CM), F32)
    rows = [
        out_norm_gain[...],
        in_norm_gain[...],
        att_norm_gain[...],
        jnp.concatenate([out_final_gain[...], pad], axis=1),
        jnp.concatenate([in_final_gain[...], pad], axis=1),
        jnp.zeros((3, CZ), F32),
    ]
    gains[...] = jnp.transpose(jnp.concatenate(rows, axis=0))


def gate_rows(x, packed, gains, state_out, gate_out):
    gain_col = gains[:, 0:1]
    weight_t = packed[OUT_GATE, :]
    unit = eye()
    for r in range(4):
        rows = jnp.concatenate([x[q, r] for q in range(8)], axis=0)
        state = dot(unit, rows, 1, 1)
        span = slice(r * NT, (r + 1) * NT)
        state_out[:, span] = state.astype(BF16)
        gate_out[:, span] = sigmoid(dot(weight_t, norm(state, gain_col), 1, 0)).astype(BF16)


def product_rows(mine, other, lines, out, check_out, left, right, stage):
    core = lax.axis_index("core")
    low = lax.broadcasted_iota(jnp.int32, (16, LANES), 1) < 64

    def paired(ref, src, rows):
        first = ref[src, rows, :].astype(F32)
        second = ref[src + 1, rows, :].astype(F32)
        head = jnp.where(low, first, pltpu.roll(second, 64, 1))
        tail = jnp.where(low, pltpu.roll(first, 64, 1), second)
        return jnp.concatenate([head, tail], axis=0).astype(BF16)

    for p in range(8):
        for a in range(CHUNKS):
            lanes = slice(a * LANES, (a + 1) * LANES)
            src = p * 8 + 2 * a
            left[p * 32 : (p + 1) * 32, lanes] = paired(mine, src, slice(0, 16))
            at = pl.multiple_of(p * 64 + core * 32, 32)
            right[pl.ds(at, 32), lanes] = paired(mine, src, slice(16, 32))
            at = pl.multiple_of(p * 64 + (1 - core) * 32, 32)
            right[pl.ds(at, 32), lanes] = paired(other, src, slice(16, 32))
    product = dot(left[...], right[...], 1, 1)
    for chunk in range(CHUNKS):
        stage[pl.ds(chunk, 256, stride=4), :] = product[:, chunk * LANES : (chunk + 1) * LANES]
    out[...] = stage[...].astype(BF16).reshape(64, 16, LANES)
    weight_rows = lines[OUT_CHECK, :].astype(BF16)
    total = sum(dot(part, left[...], 1, 1) for part in thirds(dot(weight_rows, right[...], 1, 0)))
    check_out[...] = total / NT


def update_rows(recv_stage, stride, r, state, gate, final_gain, final_t):
    product = jnp.concatenate(
        [recv_stage[pl.ds(r * 4 + chunk, CM, stride=stride), :] for chunk in range(CHUNKS)], axis=1
    )
    update = dot(final_t, norm(product, final_gain), 1, 0)
    return state.astype(F32) + gate.astype(F32) * update


def project_rows(
    mask_s, lines, recv, state_in, gate, packed, finals, gains, out, state_out, stage, recv_stage
):
    row0 = first_row() + 4 * lax.axis_index("q")
    mask_all = lines[MASK, :]
    gain_col = gains[:, 1:2]
    final_col = gains[0:CM, 3:4]
    final_t = finals[:, 0:CM]
    weight_t = packed[IN_PROJ, :]
    recv_stage[...] = recv[...].astype(F32).reshape(CM * 16, LANES)
    for r in range(4):
        span = slice(r * NT, (r + 1) * NT)
        state = update_rows(
            recv_stage, 16, r, state_in[:, span], gate[:, span], final_col, final_t
        )
        state_out[:, span] = state.astype(BF16)
        mixed = dot(weight_t, norm(state, gain_col), 1, 0)
        mask = mask_all * mask_s[row0 + r].astype(F32)
        left = sigmoid(mixed[0:CM]) * mixed[CM : 2 * CM] * mask
        right = sigmoid(mixed[2 * CM : 3 * CM]) * mixed[3 * CM : 4 * CM] * mask
        for chunk in range(CHUNKS):
            lanes = slice(chunk * LANES, (chunk + 1) * LANES)
            stage[pl.ds(r * 8 + chunk, CM, stride=32), :] = left[:, lanes]
            stage[pl.ds(r * 8 + 4 + chunk, CM, stride=32), :] = right[:, lanes]
    out[...] = stage[...].astype(BF16).reshape(CM, 32, LANES)


def gate_only(state, packed, gains, gate_out):
    gain_col = gains[:, 1:2]
    weight_t = packed[IN_GATE, :]
    for r in range(4):
        span = slice(r * NT, (r + 1) * NT)
        normed = norm(state[:, span].astype(F32), gain_col)
        gate_out[:, span] = sigmoid(dot(weight_t, normed, 1, 0)).astype(BF16)


def product_cols(mine, other, lines, check_in, out, left, right, product, stage, stage_out):
    core = lax.axis_index("core")
    for side, buf in enumerate((mine, other)):
        stage[...] = buf[...].astype(F32).reshape(64 * 32, LANES)
        rows = slice(side * 256, (side + 1) * 256)
        for chunk in range(CHUNKS):
            lanes = slice(chunk * LANES, (chunk + 1) * LANES)
            left[rows, lanes] = stage[pl.ds(chunk, 256, stride=8), :].astype(BF16)
            right[rows, lanes] = stage[pl.ds(4 + chunk, 256, stride=8), :].astype(BF16)
    product[...] = dot(left[...], right[...], 0, 0)
    for p in range(8):
        rows = product[pl.ds(pl.multiple_of(p * 64 + core * 32, 32), 32), :]
        for chunk in range(CHUNKS):
            stage_out[pl.ds(p * 128 + chunk, 32, stride=4), :] = rows[
                :, chunk * LANES : (chunk + 1) * LANES
            ]
    out[:, 0:16, :] = stage_out[...].astype(BF16).reshape(64, 16, LANES)
    weight_rows = lines[IN_CHECK, :].astype(BF16)
    total = sum(dot(part, right[...], 1, 0) for part in thirds(dot(weight_rows, left[...], 1, 1)))
    high = check_in[...].astype(BF16).astype(F32)
    lines = []
    for part, count in ((high, 2), (check_in[...] - high, 2), (total / NT, 4)):
        lines += [part[0:1, c * LANES : (c + 1) * LANES] for c in range(count)]
    tail = jnp.concatenate(lines, axis=0).astype(BF16)
    out[:, 16:24, :] = jnp.broadcast_to(tail[None], (64, 8, LANES))


def bias_rows(
    recv, state_in, gate, packed, finals, gains, out, state_out, recv_stage, bias_stage
):
    gain_col = gains[:, 2:3]
    final_col = gains[0:CM, 4:5]
    final_t = finals[:, CM : 2 * CM]
    weight_t = packed[BIAS.start : PACKED, :]
    recv_stage[...] = recv[...].astype(F32).reshape(CM * 24, LANES)
    for r in range(4):
        span = slice(r * NT, (r + 1) * NT)
        state = update_rows(recv_stage, 24, r, state_in[:, span], gate[:, span], final_col, final_t)
        state_out[:, span] = state.astype(BF16)
        normed = norm(state, gain_col)
        bias = dot(weight_t, normed, 1, 0) * LOG2E
        for chunk in range(CHUNKS):
            bias_stage[pl.ds(r * 16 + chunk, HEADS, stride=4), :] = bias[
                0:HEADS, chunk * LANES : (chunk + 1) * LANES
            ]
    out[...] = jnp.broadcast_to(bias_stage[...].astype(BF16)[None], (64, 64, LANES))


def attention_inputs(
    recv, state, packed, gains, query_out, key_out, value_out, gate_out, check_row, check_col,
    recv_stage, turn,
):
    gain_col = gains[:, 2:3]
    recv_stage[...] = recv[:, 16:24, :].astype(F32).reshape(CM * 8, LANES)
    p, q = lax.axis_index("p"), lax.axis_index("q")

    def rows_of(at):
        return recv_stage[pl.ds(at, CM, stride=8), :]

    turn[0] = jnp.transpose(rows_of(p // 4) + rows_of(2 + p // 4))
    check_row[...] = turn[0, pl.ds(pl.multiple_of(lax.rem(p, 4) * 32, 32), 32), :]
    turn[1] = jnp.transpose(rows_of(4 + q // 2))
    check_col[...] = turn[1, pl.ds(pl.multiple_of(lax.rem(q, 2) * 64, 64), 64), :]
    for r in range(4):
        span = slice(r * NT, (r + 1) * NT)
        rows = norm(state[:, span].astype(F32), gain_col)
        query_out[:, span] = (dot(packed[QUERY, :], rows, 1, 0) * (LOG2E * DH ** (-0.5))).astype(
            BF16
        )
        key_out[span, :] = dot(rows, packed[KEY, :], 0, 0).astype(BF16)
        value_out[:, span] = dot(packed[VALUE, :], rows, 1, 0).astype(BF16)
        gate_out[:, span] = sigmoid(dot(packed[ATT_GATE, :], rows, 1, 0)).astype(BF16)


def attend(
    lines, mine, other, query, key, value, gate, state, packed, out, bias_stage, bias
):
    core = lax.axis_index("core")
    bias_stage[core] = mine[...].astype(F32).reshape(64 * 64, LANES)
    bias_stage[1 - core] = other[...].astype(F32).reshape(64 * 64, LANES)
    key_bias = jnp.where(lines[MASK, :] > 0, 0.0, -1000000000.0 * LOG2E).astype(F32)
    key_cols = [column(key_bias[:, c * LANES : (c + 1) * LANES]) for c in range(CHUNKS)]
    weight_t = packed[ATT_OUT, :]

    def turn_bias(h):
        for chunk in range(CHUNKS):
            blocks = [
                bias_stage[plane, pl.ds(p * 512 + h * 4 + chunk, 32, stride=16), :]
                for p in range(8)
                for plane in range(2)
            ]
            turned = jnp.transpose(jnp.concatenate(blocks, axis=0))
            bias[h, chunk * LANES : (chunk + 1) * LANES, :] = turned + key_cols[chunk]

    def scores(h, query_row, key_row):
        zeros = jnp.zeros((DH, NT), BF16)
        masked = jnp.concatenate(
            [query_row[h * DH : (h + 1) * DH] if at == h else zeros for at in range(HEADS)], axis=0
        )
        return dot(key_row, masked, 1, 0) + bias[h]

    def weighted(h, weights, value_row):
        padded = jnp.concatenate(
            [value_row[h * DH : (h + 1) * DH], jnp.ones((16, NT), BF16)], axis=0
        )
        both = dot(padded, weights.astype(BF16), 1, 0)
        return both[0:DH] / both[DH : DH + 1], both[DH : DH + 1]

    def finish(r, span, parts):
        attended = jnp.concatenate(parts, axis=0) * gate[:, span].astype(F32)
        result = state[:, span].astype(F32) + dot(weight_t, attended.astype(BF16), 1, 0)
        out[:, r, :, :] = jnp.transpose(result).astype(BF16).reshape(8, 64, CZ)

    low = high = jnp.ones((1, NT), F32)
    parts = [[] for _ in range(4)]
    for h in range(HEADS):
        turn_bias(h)
        for r in range(4):
            span = slice(r * NT, (r + 1) * NT)
            weights = jnp.exp2(scores(h, query[:, span], key[span, :]))
            part, total = weighted(h, weights, value[:, span])
            low, high = jnp.minimum(low, total), jnp.maximum(high, total)
            parts[r].append(part)
    for r in range(4):
        finish(r, slice(r * NT, (r + 1) * NT), parts[r])
    in_range = jnp.logical_and(jnp.min(low) > 1e-25, jnp.max(high) < 1e30)

    @pl.when(jnp.logical_not(in_range))
    def _():
        def one_row(r, carry):
            span = pl.ds(pl.multiple_of(r * NT, NT), NT)
            again = []
            for h in range(HEADS):
                values = scores(h, query[:, span], key[span, :])
                weights = jnp.exp2(values - jnp.max(values, axis=0, keepdims=True))
                again.append(weighted(h, weights, value[:, span])[0])
            finish(r, span, again)
            return carry

        lax.fori_loop(0, 4, one_row, 0)


def swap(values):
    return lax.ppermute(values, "core", [(0, 1), (1, 0)])


def exchange(values, axes):
    return lax.all_to_all(values, axes, 0, 0, tiled=True)


def on_device(
    pair_input,
    token_mask,
    out_check_weights,
    in_check_weights,
    out_norm_gain,
    out_proj,
    out_gate,
    out_final_gain,
    out_final,
    in_norm_gain,
    in_proj,
    in_gate,
    in_final_gain,
    in_final,
    att_norm_gain,
    att_qkv,
    att_bias,
    att_gate,
    att_out,
):
    def row(vector):
        return vector.reshape(1, vector.shape[0])

    tokens = 4 * NT
    mask_v = row(token_mask)
    state_rows = exchange(pair_input.reshape(8, 4, 64, CZ), "q")
    (sent,) = call(
        project_tile,
        [((CM, 32, LANES), BF16)],
        [((CM * 32, LANES), F32)],
        [("s", token_mask), ("w", mask_v), ("w", pair_input.reshape(tokens, CZ)),
         ("w", row(out_norm_gain)), ("w", out_proj)],
    )
    weights = (
        row(out_norm_gain), out_gate, row(out_final_gain), out_final, row(in_norm_gain), in_proj, in_gate,
        row(in_final_gain), in_final, row(att_norm_gain), att_qkv, att_bias.T, att_gate, att_out,
        mask_v, row(out_check_weights), row(in_check_weights),
    )
    packed, finals, gains, lines = call(
        prepare,
        [((PACKED, CZ), BF16), ((CZ, CZ), BF16), ((CZ, 8), F32), ((24, NT), F32)],
        [(value.shape, value.dtype) for value in weights] + [((COUNT,), None)],
        [("h", value) for value in weights],
    )
    state_rows, sent, packed, finals, gains, lines = lax.optimization_barrier(
        (state_rows, sent, packed, finals, gains, lines)
    )
    mine = exchange(sent, PLANE)
    mine, state_rows = lax.optimization_barrier((mine, state_rows))
    other = swap(mine)
    wide = (CZ, tokens)
    state, gate = call(
        gate_rows,
        [(wide, BF16), (wide, BF16)],
        [],
        [("v", state_rows), ("v", packed), ("v", gains)],
    )
    other, state, gate = lax.optimization_barrier((other, state, gate))
    sent, check_out = call(
        product_rows,
        [((64, 16, LANES), BF16), ((8, 256), F32)],
        [((256, NT), BF16), ((NT, NT), BF16), ((1024, LANES), F32)],
        [("v", mine), ("v", other), ("v", lines)],
    )
    recv = exchange(sent, PLANE)
    sent, state = call(
        project_rows,
        [((CM, 32, LANES), BF16), (wide, BF16)],
        [((CM * 32, LANES), F32), ((CM * 16, LANES), F32)],
        [("s", token_mask), ("v", lines), ("v", recv), ("v", state), ("v", gate),
         ("v", packed), ("v", finals), ("v", gains)],
    )
    mine = exchange(sent, PLANE)
    mine, state = lax.optimization_barrier((mine, state))
    other = swap(mine)
    (gate,) = call(
        gate_only, [(wide, BF16)], [], [("v", state), ("v", packed), ("v", gains)]
    )
    other, gate = lax.optimization_barrier((other, gate))
    (sent,) = call(
        product_cols,
        [((64, 24, LANES), BF16)],
        [((NT, NT), BF16), ((NT, NT), BF16), ((NT, NT), F32), ((64 * 32, LANES), F32),
         ((1024, LANES), F32)],
        [("v", mine), ("v", other), ("v", lines), ("v", check_out)],
    )
    recv = exchange(sent, PLANE)
    sent, state = call(
        bias_rows,
        [((64, 64, LANES), BF16), (wide, BF16)],
        [((CM * 24, LANES), F32), ((64, LANES), F32)],
        [("v", recv), ("v", state), ("v", gate), ("v", packed), ("v", finals), ("v", gains)],
    )
    mine = exchange(sent, PLANE)
    mine, state = lax.optimization_barrier((mine, state))
    other = swap(mine)
    query, key, value, gate, check_row, check_col = call(
        attention_inputs,
        [(wide, BF16), ((tokens, CZ), BF16), (wide, BF16), (wide, BF16), ((32, CM), F32),
         ((64, CM), F32)],
        [((CM * 8, LANES), F32), ((2, LANES, CM), F32)],
        [("v", recv), ("v", state), ("v", packed), ("v", gains)],
    )
    other, query = lax.optimization_barrier((other, query))
    (sent,) = call(
        attend,
        [((8, 4, 64, CZ), BF16)],
        [((2, 64 * 64, LANES), F32), ((HEADS, NT, NT), F32)],
        [("v", lines), ("v", mine), ("v", other), ("v", query), ("v", key), ("v", value),
         ("v", gate), ("v", state), ("v", packed)],
    )
    result = exchange(sent, "q").reshape(32, 64, CZ)
    return result, check_row, check_col


def solution(mesh):
    grid = Mesh(mesh.devices.reshape(8, 2, 8), ("p", "core", "q"))
    tile = P(("p", "core"), "q", None)
    in_specs = (tile,) + (P(),) * 18
    out_specs = (tile, P(("p", "core"), None), P("q", None))
    return jax.shard_map(
        on_device, mesh=grid, in_specs=in_specs, out_specs=out_specs, check_vma=False
    )
```

```python
import jax
import jax.numpy as jnp
from jax import lax
from jax.experimental import pallas as pl
from jax.experimental.pallas import tpu as pltpu
from jax.sharding import Mesh, PartitionSpec as P

F32 = jnp.float32
BF16 = jnp.bfloat16
NT = 512
CZ = 128
CM = 64
HEADS = 4
DH = 32
LANES = 128
CHUNKS = NT // LANES
PLANE = ("p", "q")
VMEM = pl.BlockSpec(memory_space=pltpu.VMEM)
SMEM = pl.BlockSpec(memory_space=pltpu.SMEM)
HBM = pl.BlockSpec(memory_space=pltpu.HBM)
SPECS = {"s": SMEM, "v": VMEM, "h": HBM, "w": VMEM}
LOG2E = 1.4426950408889634


def dot(left, right, left_dim, right_dim):
    return lax.dot_general(
        left, right, (((left_dim,), (right_dim,)), ((), ())), preferred_element_type=F32
    )


def column(row):
    return jnp.transpose(jnp.broadcast_to(row, (8, row.shape[1])))[:, 0:1]


def flipped(weight):
    return jnp.transpose(weight.astype(F32)).astype(BF16)


def eye():
    rows = lax.broadcasted_iota(jnp.int32, (LANES, LANES), 0)
    cols = lax.broadcasted_iota(jnp.int32, (LANES, LANES), 1)
    return jnp.where(rows == cols, 1.0, 0.0).astype(BF16)


def centre(values, gain_col):
    mean = jnp.mean(values, axis=0, keepdims=True)
    centered = values - mean
    variance = jnp.mean(centered * centered, axis=0, keepdims=True)
    return centered * lax.rsqrt(variance + 1e-05) * gain_col


def norm(values, gain_col):
    return centre(values, gain_col).astype(BF16)


def sigmoid(values):
    return jax.nn.sigmoid(values)


def thirds(values):
    high = values.astype(BF16)
    rest = values - high.astype(F32)
    middle = rest.astype(BF16)
    return high, middle, (rest - middle.astype(F32)).astype(BF16)


def call(kernel, outs, scratch, ins, mib=24):
    def shape_of(shape, kind, place="v"):
        return (pltpu.HBM if place == "h" else jax.ShapeDtypeStruct)(shape, kind)

    def placed(place, value):
        return pltpu.with_memory_space_constraint(value, pltpu.HBM) if place in "hw" else value

    return pl.pallas_call(
        kernel,
        out_shape=tuple(shape_of(*out) for out in outs),
        in_specs=[SPECS[place] for place, _ in ins],
        out_specs=tuple(HBM if out[2:] == ("h",) else VMEM for out in outs),
        scratch_shapes=[
            pltpu.SemaphoreType.DMA(shape) if kind is None else pltpu.VMEM(shape, kind)
            for shape, kind in scratch
        ],
        compiler_params=pltpu.CompilerParams(vmem_limit_bytes=mib * 1024 * 1024),
    )(*[placed(place, value) for place, value in ins])


def start(copies):
    for copy in copies:
        copy.start()
    return copies


def wait(copies):
    for copy in copies:
        copy.wait()


def first_row():
    return (2 * lax.axis_index("p") + lax.axis_index("core")) * 32


def project_tile(mask_s, mask_v, x, gain, weight, out, stage):
    row0 = first_row()
    shift = lax.rem(NT - 64 * lax.axis_index("q"), NT)
    mask_all = jnp.broadcast_to(mask_v[...].astype(F32), (8, NT))
    col_mask = pltpu.roll(mask_all, shift, 1)[0:1, 0:64]
    gain_col = column(gain[...])
    weight_t = flipped(weight[...])
    unit = eye()
    for group in range(4):
        steps = range(group * 4, group * 4 + 4)
        pieces, masks = [], []
        for s in steps:
            for i in (s, s + 16):
                pieces.append(x[i * 64 : (i + 1) * 64, :])
                masks.append(col_mask * mask_s[row0 + i].astype(F32))
        state = dot(unit, jnp.concatenate(pieces, axis=0), 1, 1)
        mask = jnp.concatenate(masks, axis=1)
        mixed = dot(weight_t, norm(state, gain_col), 1, 0)
        left = sigmoid(mixed[0:CM]) * mixed[CM : 2 * CM] * mask
        right = sigmoid(mixed[2 * CM : 3 * CM]) * mixed[3 * CM : 4 * CM] * mask
        for at, s in enumerate(steps):
            lanes = slice(at * LANES, (at + 1) * LANES)
            stage[pl.ds(s, CM, stride=32), :] = left[:, lanes]
            stage[pl.ds(16 + s, CM, stride=32), :] = right[:, lanes]
    out[...] = stage[...].astype(BF16).reshape(CM, 32, LANES)


OUT_GATE = slice(0, 128)
IN_PROJ = slice(128, 384)
IN_GATE = slice(384, 512)
QUERY = slice(512, 640)
KEY = slice(640, 768)
VALUE = slice(768, 896)
ATT_GATE = slice(896, 1024)
ATT_OUT = slice(1024, 1152)
BIAS = slice(1152, 1156)
PACKED = 1168
LARGE = 3e38
COUNT = 17
MASK = slice(0, 1)
OUT_CHECK = slice(8, 16)
IN_CHECK = slice(16, 24)


def prepare(*refs):
    sources, (packed, finals, gains, lines) = refs[:COUNT], refs[COUNT : COUNT + 4]
    targets, sems = refs[COUNT + 4 : 2 * COUNT + 4], refs[2 * COUNT + 4]
    wait(
        start(
            [
                pltpu.make_async_copy(source, target, sems.at[at])
                for at, (source, target) in enumerate(zip(sources, targets))
            ]
        )
    )
    (
        out_norm_gain, out_gate, out_final_gain, out_final, in_norm_gain, in_proj, in_gate,
        in_final_gain, in_final, att_norm_gain, att_qkv, att_bias, att_gate, att_out,
        mask, out_check, in_check,
    ) = targets
    for at, line in enumerate((mask, out_check, in_check)):
        lines[at * 8 : (at + 1) * 8, :] = jnp.broadcast_to(line[...].astype(F32), (8, NT))
    packed[OUT_GATE, :] = flipped(out_gate[...])
    packed[IN_PROJ, :] = flipped(in_proj[...])
    packed[IN_GATE, :] = flipped(in_gate[...])
    packed[QUERY, :] = flipped(att_qkv[:, 0:128])
    packed[KEY, :] = att_qkv[:, 128:256]
    packed[VALUE, :] = flipped(att_qkv[:, 256:384])
    packed[ATT_GATE, :] = flipped(att_gate[...])
    packed[ATT_OUT, :] = flipped(att_out[...])
    turned = jnp.concatenate([att_bias[...], jnp.zeros((16 - HEADS, CZ), BF16)], axis=0)
    packed[BIAS.start : PACKED, :] = turned
    for at, weight in enumerate((out_final, out_final, in_final, in_final)):
        finals[:, at * CM : (at + 1) * CM] = flipped(weight[...])
    pad = jnp.zeros((1, CM), F32)
    rows = [
        out_norm_gain[...],
        in_norm_gain[...],
        att_norm_gain[...],
        jnp.concatenate([out_final_gain[...], pad], axis=1),
        jnp.concatenate([in_final_gain[...], pad], axis=1),
        jnp.zeros((3, CZ), F32),
    ]
    gains[...] = jnp.transpose(jnp.concatenate(rows, axis=0))


def gate_rows(x, packed, gains, state_out, gate_out):
    gain_col = gains[:, 0:1]
    weight_t = packed[OUT_GATE, :]
    unit = eye()
    for r in range(4):
        rows = jnp.concatenate([x[q, r] for q in range(8)], axis=0)
        state = dot(unit, rows, 1, 1)
        span = slice(r * NT, (r + 1) * NT)
        state_out[:, span] = state.astype(BF16)
        gate_out[:, span] = sigmoid(dot(weight_t, norm(state, gain_col), 1, 0)).astype(BF16)


def product_rows(mine, other, lines, out, check_out, left, right, stage):
    core = lax.axis_index("core")
    low = lax.broadcasted_iota(jnp.int32, (16, LANES), 1) < 64

    def paired(ref, src, rows):
        first = ref[src, rows, :].astype(F32)
        second = ref[src + 1, rows, :].astype(F32)
        head = jnp.where(low, first, pltpu.roll(second, 64, 1))
        tail = jnp.where(low, pltpu.roll(first, 64, 1), second)
        return jnp.concatenate([head, tail], axis=0).astype(BF16)

    for p in range(8):
        for a in range(CHUNKS):
            lanes = slice(a * LANES, (a + 1) * LANES)
            src = p * 8 + 2 * a
            left[p * 32 : (p + 1) * 32, lanes] = paired(mine, src, slice(0, 16))
            at = pl.multiple_of(p * 64 + core * 32, 32)
            right[pl.ds(at, 32), lanes] = paired(mine, src, slice(16, 32))
            at = pl.multiple_of(p * 64 + (1 - core) * 32, 32)
            right[pl.ds(at, 32), lanes] = paired(other, src, slice(16, 32))
    product = dot(left[...], right[...], 1, 1)
    for chunk in range(CHUNKS):
        stage[pl.ds(chunk, 256, stride=4), :] = product[:, chunk * LANES : (chunk + 1) * LANES]
    out[...] = stage[...].astype(BF16).reshape(64, 16, LANES)
    weight_rows = lines[OUT_CHECK, :].astype(BF16)
    total = sum(dot(part, left[...], 1, 1) for part in thirds(dot(weight_rows, right[...], 1, 0)))
    check_out[...] = total / NT


def update_rows(recv_stage, stride, r, state, gate, final_gain, final_t):
    product = jnp.concatenate(
        [recv_stage[pl.ds(r * 4 + chunk, CM, stride=stride), :] for chunk in range(CHUNKS)], axis=1
    )
    normed = centre(product, final_gain)
    high = normed.astype(BF16)
    low = (normed - high.astype(F32)).astype(BF16)
    update = dot(final_t, jnp.concatenate([high, low], axis=0), 1, 0)
    return state.astype(F32) + gate.astype(F32) * update


def project_rows(
    mask_s, lines, recv, state_in, gate, packed, finals, gains, out, state_out, stage, recv_stage
):
    row0 = first_row() + 4 * lax.axis_index("q")
    mask_all = lines[MASK, :]
    gain_col = gains[:, 1:2]
    final_col = gains[0:CM, 3:4]
    final_t = finals[:, 0 : 2 * CM]
    weight_t = packed[IN_PROJ, :]
    recv_stage[...] = recv[...].astype(F32).reshape(CM * 16, LANES)
    for r in range(4):
        span = slice(r * NT, (r + 1) * NT)
        state = update_rows(
            recv_stage, 16, r, state_in[:, span], gate[:, span], final_col, final_t
        )
        state_out[:, span] = state
        mixed = dot(weight_t, norm(state, gain_col), 1, 0)
        mask = mask_all * mask_s[row0 + r].astype(F32)
        left = sigmoid(mixed[0:CM]) * mixed[CM : 2 * CM] * mask
        right = sigmoid(mixed[2 * CM : 3 * CM]) * mixed[3 * CM : 4 * CM] * mask
        for chunk in range(CHUNKS):
            lanes = slice(chunk * LANES, (chunk + 1) * LANES)
            stage[pl.ds(r * 8 + chunk, CM, stride=32), :] = left[:, lanes]
            stage[pl.ds(r * 8 + 4 + chunk, CM, stride=32), :] = right[:, lanes]
    out[...] = stage[...].astype(BF16).reshape(CM, 32, LANES)


def gate_only(state, packed, gains, gate_out):
    gain_col = gains[:, 1:2]
    weight_t = packed[IN_GATE, :]
    for r in range(4):
        span = slice(r * NT, (r + 1) * NT)
        normed = norm(state[:, span].astype(F32), gain_col)
        gate_out[:, span] = sigmoid(dot(weight_t, normed, 1, 0)).astype(BF16)


def product_cols(mine, other, lines, check_in, out, left, right, product, stage, stage_out):
    core = lax.axis_index("core")
    for side, buf in enumerate((mine, other)):
        stage[...] = buf[...].astype(F32).reshape(64 * 32, LANES)
        rows = slice(side * 256, (side + 1) * 256)
        for chunk in range(CHUNKS):
            lanes = slice(chunk * LANES, (chunk + 1) * LANES)
            left[rows, lanes] = stage[pl.ds(chunk, 256, stride=8), :].astype(BF16)
            right[rows, lanes] = stage[pl.ds(4 + chunk, 256, stride=8), :].astype(BF16)
    product[...] = dot(left[...], right[...], 0, 0)
    for p in range(8):
        rows = product[pl.ds(pl.multiple_of(p * 64 + core * 32, 32), 32), :]
        for chunk in range(CHUNKS):
            stage_out[pl.ds(p * 128 + chunk, 32, stride=4), :] = rows[
                :, chunk * LANES : (chunk + 1) * LANES
            ]
    out[:, 0:16, :] = stage_out[...].astype(BF16).reshape(64, 16, LANES)
    weight_rows = lines[IN_CHECK, :].astype(BF16)
    total = sum(dot(part, right[...], 1, 0) for part in thirds(dot(weight_rows, left[...], 1, 1)))
    high = check_in[...].astype(BF16).astype(F32)
    lines = []
    for part, count in ((high, 2), (check_in[...] - high, 2), (total / NT, 4)):
        lines += [part[0:1, c * LANES : (c + 1) * LANES] for c in range(count)]
    tail = jnp.concatenate(lines, axis=0).astype(BF16)
    out[:, 16:24, :] = jnp.broadcast_to(tail[None], (64, 8, LANES))


def bias_rows(
    lines, recv, state_in, gate, packed, finals, gains, out, state_out, normed_out,
    recv_stage, bias_stage,
):
    live = jnp.broadcast_to(lines[MASK, :], (PACKED - BIAS.start, NT)) > 0
    gain_col = gains[:, 2:3]
    final_col = gains[0:CM, 4:5]
    final_t = finals[:, 2 * CM : 4 * CM]
    weight_t = packed[BIAS.start : PACKED, :]
    recv_stage[...] = recv[...].astype(F32).reshape(CM * 24, LANES)
    for r in range(4):
        span = slice(r * NT, (r + 1) * NT)
        state = update_rows(recv_stage, 24, r, state_in[:, span], gate[:, span], final_col, final_t)
        state_out[:, span] = state.astype(BF16)
        normed = norm(state, gain_col)
        normed_out[:, span] = normed
        bias = dot(weight_t, normed, 1, 0) * LOG2E
        top = jnp.max(jnp.where(live, bias, -LARGE), axis=1, keepdims=True)
        bias = bias - jnp.where(top > -LARGE, top, 0.0)
        for chunk in range(CHUNKS):
            bias_stage[pl.ds(r * 16 + chunk, HEADS, stride=4), :] = bias[
                0:HEADS, chunk * LANES : (chunk + 1) * LANES
            ]
    out[...] = jnp.broadcast_to(bias_stage[...].astype(BF16)[None], (64, 64, LANES))


def attention_inputs(
    recv, mine, normed, packed,
    query_out, key_out, value_out, gate_out, check_row, check_col, mine_out,
    recv_stage, turn,
):
    mine_out[...] = mine[...].astype(F32).reshape(64 * 64, LANES)
    recv_stage[...] = recv[:, 16:24, :].astype(F32).reshape(CM * 8, LANES)
    p, q = lax.axis_index("p"), lax.axis_index("q")

    def rows_of(at):
        return recv_stage[pl.ds(at, CM, stride=8), :]

    turn[0] = jnp.transpose(rows_of(p // 4) + rows_of(2 + p // 4))
    check_row[...] = turn[0, pl.ds(pl.multiple_of(lax.rem(p, 4) * 32, 32), 32), :]
    turn[1] = jnp.transpose(rows_of(4 + q // 2))
    check_col[...] = turn[1, pl.ds(pl.multiple_of(lax.rem(q, 2) * 64, 64), 64), :]
    for r in range(4):
        span = slice(r * NT, (r + 1) * NT)
        rows = normed[:, span]
        query_out[:, span] = (dot(packed[QUERY, :], rows, 1, 0) * (LOG2E * DH ** (-0.5))).astype(
            BF16
        )
        key_out[span, :] = dot(rows, packed[KEY, :], 0, 0).astype(BF16)
        value_out[:, span] = dot(packed[VALUE, :], rows, 1, 0).astype(BF16)
        gate_out[:, span] = sigmoid(dot(packed[ATT_GATE, :], rows, 1, 0)).astype(BF16)


def attend(
    lines, mine, bias_other, query, key, value, gate, state, packed, out, other, bias
):
    first = lax.axis_index("core") == 0
    other[...] = bias_other[...].astype(F32).reshape(64 * 64, LANES)
    key_bias = jnp.where(lines[MASK, :] > 0, 0.0, -1000000000.0 * LOG2E).astype(F32)
    key_cols = [column(key_bias[:, c * LANES : (c + 1) * LANES]) for c in range(CHUNKS)]
    weight_t = packed[ATT_OUT, :]

    def turn_bias(h):
        for chunk in range(CHUNKS):
            blocks = []
            for p in range(8):
                rows = pl.ds(p * 512 + h * 4 + chunk, 32, stride=16)
                here, there = mine[rows, :], other[rows, :]
                blocks += [jnp.where(first, here, there), jnp.where(first, there, here)]
            turned = jnp.transpose(jnp.concatenate(blocks, axis=0))
            bias[h, chunk * LANES : (chunk + 1) * LANES, :] = turned + key_cols[chunk]

    def scores(h, query_row, key_row):
        zeros = jnp.zeros((DH, NT), BF16)
        masked = jnp.concatenate(
            [query_row[h * DH : (h + 1) * DH] if at == h else zeros for at in range(HEADS)], axis=0
        )
        return dot(key_row, masked, 1, 0) + bias[h]

    def weighted(h, weights, value_row):
        padded = jnp.concatenate(
            [value_row[h * DH : (h + 1) * DH], jnp.ones((16, NT), BF16)], axis=0
        )
        both = dot(padded, weights.astype(BF16), 1, 0)
        return both[0:DH] / both[DH : DH + 1], both[DH : DH + 1]

    def finish(r, span, parts):
        attended = jnp.concatenate(parts, axis=0) * gate[:, span].astype(F32)
        result = state[:, span].astype(F32) + dot(weight_t, attended.astype(BF16), 1, 0)
        out[:, r, :, :] = jnp.transpose(result).astype(BF16).reshape(8, 64, CZ)

    low = high = jnp.ones((1, NT), F32)
    parts = [[] for _ in range(4)]
    for h in range(HEADS):
        turn_bias(h)
        for r in range(4):
            span = slice(r * NT, (r + 1) * NT)
            weights = jnp.exp2(scores(h, query[:, span], key[span, :]))
            part, total = weighted(h, weights, value[:, span])
            low, high = jnp.minimum(low, total), jnp.maximum(high, total)
            parts[r].append(part)
    for r in range(4):
        finish(r, slice(r * NT, (r + 1) * NT), parts[r])
    in_range = jnp.logical_and(jnp.min(low) > 1e-25, jnp.max(high) < 1e30)

    @pl.when(jnp.logical_not(in_range))
    def _():
        def one_row(r, carry):
            span = pl.ds(pl.multiple_of(r * NT, NT), NT)
            again = []
            for h in range(HEADS):
                values = scores(h, query[:, span], key[span, :])
                weights = jnp.exp2(values - jnp.max(values, axis=0, keepdims=True))
                again.append(weighted(h, weights, value[:, span])[0])
            finish(r, span, again)
            return carry

        lax.fori_loop(0, 4, one_row, 0)


def swap(values):
    return lax.ppermute(values, "core", [(0, 1), (1, 0)])


def exchange(values, axes):
    return lax.all_to_all(values, axes, 0, 0, tiled=True)


def on_device(
    pair_input,
    token_mask,
    out_check_weights,
    in_check_weights,
    out_norm_gain,
    out_proj,
    out_gate,
    out_final_gain,
    out_final,
    in_norm_gain,
    in_proj,
    in_gate,
    in_final_gain,
    in_final,
    att_norm_gain,
    att_qkv,
    att_bias,
    att_gate,
    att_out,
):
    def row(vector):
        return vector.reshape(1, vector.shape[0])

    tokens = 4 * NT
    mask_v = row(token_mask)
    state_rows = exchange(pair_input.reshape(8, 4, 64, CZ), "q")
    (sent,) = call(
        project_tile,
        [((CM, 32, LANES), BF16)],
        [((CM * 32, LANES), F32)],
        [("s", token_mask), ("w", mask_v), ("w", pair_input.reshape(tokens, CZ)),
         ("w", row(out_norm_gain)), ("w", out_proj)],
    )
    weights = (
        row(out_norm_gain), out_gate, row(out_final_gain), out_final, row(in_norm_gain), in_proj, in_gate,
        row(in_final_gain), in_final, row(att_norm_gain), att_qkv, att_bias.T, att_gate, att_out,
        mask_v, row(out_check_weights), row(in_check_weights),
    )
    packed, finals, gains, lines = call(
        prepare,
        [((PACKED, CZ), BF16), ((CZ, 4 * CM), BF16), ((CZ, 8), F32), ((24, NT), F32)],
        [(value.shape, value.dtype) for value in weights] + [((COUNT,), None)],
        [("h", value) for value in weights],
    )
    state_rows, sent, packed, finals, gains, lines = lax.optimization_barrier(
        (state_rows, sent, packed, finals, gains, lines)
    )
    mine = exchange(sent, PLANE)
    mine, state_rows = lax.optimization_barrier((mine, state_rows))
    other = swap(mine)
    wide = (CZ, tokens)
    state, gate = call(
        gate_rows,
        [(wide, BF16), (wide, BF16)],
        [],
        [("v", state_rows), ("v", packed), ("v", gains)],
    )
    other, state, gate = lax.optimization_barrier((other, state, gate))
    sent, check_out = call(
        product_rows,
        [((64, 16, LANES), BF16), ((8, 256), F32)],
        [((256, NT), BF16), ((NT, NT), BF16), ((1024, LANES), F32)],
        [("v", mine), ("v", other), ("v", lines)],
    )
    recv = exchange(sent, PLANE)
    sent, state = call(
        project_rows,
        [((CM, 32, LANES), BF16), (wide, F32)],
        [((CM * 32, LANES), F32), ((CM * 16, LANES), F32)],
        [("s", token_mask), ("v", lines), ("v", recv), ("v", state), ("v", gate),
         ("v", packed), ("v", finals), ("v", gains)],
    )
    mine = exchange(sent, PLANE)
    mine, state = lax.optimization_barrier((mine, state))
    other = swap(mine)
    (gate,) = call(
        gate_only, [(wide, BF16)], [], [("v", state), ("v", packed), ("v", gains)]
    )
    other, gate = lax.optimization_barrier((other, gate))
    (sent,) = call(
        product_cols,
        [((64, 24, LANES), BF16)],
        [((NT, NT), BF16), ((NT, NT), BF16), ((NT, NT), F32), ((64 * 32, LANES), F32),
         ((1024, LANES), F32)],
        [("v", mine), ("v", other), ("v", lines), ("v", check_out)],
    )
    recv = exchange(sent, PLANE)
    sent, state, normed = call(
        bias_rows,
        [((64, 64, LANES), BF16), (wide, BF16), (wide, BF16)],
        [((CM * 24, LANES), F32), ((64, LANES), F32)],
        [("v", lines), ("v", recv), ("v", state), ("v", gate), ("v", packed), ("v", finals),
         ("v", gains)],
    )
    mine = exchange(sent, PLANE)
    mine, normed = lax.optimization_barrier((mine, normed))
    other = swap(mine)
    query, key, value, gate, check_row, check_col, staged = call(
        attention_inputs,
        [(wide, BF16), ((tokens, CZ), BF16), (wide, BF16), (wide, BF16), ((32, CM), F32),
         ((64, CM), F32), ((64 * 64, LANES), F32)],
        [((CM * 8, LANES), F32), ((2, LANES, CM), F32)],
        [("v", recv), ("v", mine), ("v", normed), ("v", packed)],
    )
    other, query = lax.optimization_barrier((other, query))
    (sent,) = call(
        attend,
        [((8, 4, 64, CZ), BF16)],
        [((64 * 64, LANES), F32), ((HEADS, NT, NT), F32)],
        [("v", lines), ("v", staged), ("v", other), ("v", query), ("v", key), ("v", value),
         ("v", gate), ("v", state), ("v", packed)],
    )
    result = exchange(sent, "q").reshape(32, 64, CZ)
    return result, check_row, check_col


def solution(mesh):
    grid = Mesh(mesh.devices.reshape(8, 2, 8), ("p", "core", "q"))
    tile = P(("p", "core"), "q", None)
    in_specs = (tile,) + (P(),) * 18
    out_specs = (tile, P(("p", "core"), None), P("q", None))
    return jax.shard_map(
        on_device, mesh=grid, in_specs=in_specs, out_specs=out_specs, check_vma=False
    )
```

```python
import jax
import jax.numpy as jnp
from jax import lax
from jax.experimental import pallas as pl
from jax.experimental.pallas import tpu as pltpu
from jax.sharding import Mesh, PartitionSpec as P

F32 = jnp.float32
BF16 = jnp.bfloat16
NT = 512
CZ = 128
CM = 64
HEADS = 4
DH = 32
LANES = 128
CHUNKS = NT // LANES
PLANE = ("p", "q")
VMEM = pl.BlockSpec(memory_space=pltpu.VMEM)
SMEM = pl.BlockSpec(memory_space=pltpu.SMEM)
HBM = pl.BlockSpec(memory_space=pltpu.HBM)
SPECS = {"s": SMEM, "v": VMEM, "h": HBM, "w": VMEM}
LOG2E = 1.4426950408889634


def dot(left, right, left_dim, right_dim):
    return lax.dot_general(
        left, right, (((left_dim,), (right_dim,)), ((), ())), preferred_element_type=F32
    )


def column(row):
    return jnp.transpose(jnp.broadcast_to(row, (8, row.shape[1])))[:, 0:1]


def flipped(weight):
    return jnp.transpose(weight.astype(F32)).astype(BF16)


def eye():
    rows = lax.broadcasted_iota(jnp.int32, (LANES, LANES), 0)
    cols = lax.broadcasted_iota(jnp.int32, (LANES, LANES), 1)
    return jnp.where(rows == cols, 1.0, 0.0).astype(BF16)


def centre(values, gain_col):
    mean = jnp.mean(values, axis=0, keepdims=True)
    centered = values - mean
    variance = jnp.mean(centered * centered, axis=0, keepdims=True)
    return centered * lax.rsqrt(variance + 1e-05) * gain_col


def norm(values, gain_col):
    return centre(values, gain_col).astype(BF16)


def sigmoid(values):
    return jax.nn.sigmoid(values)


def thirds(values):
    high = values.astype(BF16)
    rest = values - high.astype(F32)
    middle = rest.astype(BF16)
    return jnp.concatenate([high, middle, (rest - middle.astype(F32)).astype(BF16)], axis=0)


def folded(parts):
    return parts[0:8] + (parts[8:16] + parts[16:24])


def call(kernel, outs, scratch, ins, mib=24):
    def shape_of(shape, kind, place="v"):
        return (pltpu.HBM if place == "h" else jax.ShapeDtypeStruct)(shape, kind)

    def placed(place, value):
        return pltpu.with_memory_space_constraint(value, pltpu.HBM) if place in "hw" else value

    return pl.pallas_call(
        kernel,
        out_shape=tuple(shape_of(*out) for out in outs),
        in_specs=[SPECS[place] for place, _ in ins],
        out_specs=tuple(HBM if out[2:] == ("h",) else VMEM for out in outs),
        scratch_shapes=[
            pltpu.SemaphoreType.DMA(shape) if kind is None else pltpu.VMEM(shape, kind)
            for shape, kind in scratch
        ],
        compiler_params=pltpu.CompilerParams(vmem_limit_bytes=mib * 1024 * 1024),
    )(*[placed(place, value) for place, value in ins])


def start(copies):
    for copy in copies:
        copy.start()
    return copies


def wait(copies):
    for copy in copies:
        copy.wait()


def first_row():
    return (2 * lax.axis_index("p") + lax.axis_index("core")) * 32


def project_tile(mask_s, mask_v, x, gain, weight, out, stage):
    row0 = first_row()
    shift = lax.rem(NT - 64 * lax.axis_index("q"), NT)
    mask_all = jnp.broadcast_to(mask_v[...].astype(F32), (8, NT))
    col_mask = pltpu.roll(mask_all, shift, 1)[0:1, 0:64]
    gain_col = column(gain[...])
    weight_t = flipped(weight[...])
    unit = eye()
    for group in range(4):
        steps = range(group * 4, group * 4 + 4)
        pieces, masks = [], []
        for s in steps:
            for i in (s, s + 16):
                pieces.append(x[i * 64 : (i + 1) * 64, :])
                masks.append(col_mask * mask_s[row0 + i].astype(F32))
        state = dot(unit, jnp.concatenate(pieces, axis=0), 1, 1)
        mask = jnp.concatenate(masks, axis=1)
        mixed = dot(weight_t, norm(state, gain_col), 1, 0)
        left = sigmoid(mixed[0:CM]) * mixed[CM : 2 * CM] * mask
        right = sigmoid(mixed[2 * CM : 3 * CM]) * mixed[3 * CM : 4 * CM] * mask
        for at, s in enumerate(steps):
            lanes = slice(at * LANES, (at + 1) * LANES)
            stage[pl.ds(s, CM, stride=32), :] = left[:, lanes]
            stage[pl.ds(16 + s, CM, stride=32), :] = right[:, lanes]
    out[...] = stage[...].astype(BF16).reshape(CM, 32, LANES)


OUT_GATE = slice(0, 128)
IN_PROJ = slice(128, 384)
IN_GATE = slice(384, 512)
QUERY = slice(512, 640)
KEY = slice(640, 768)
VALUE = slice(768, 896)
ATT_GATE = slice(896, 1024)
ATT_OUT = slice(1024, 1152)
BIAS = slice(1152, 1156)
PACKED = 1168
GROUP = 4
LARGE = 3e38
COUNT = 17
MASK = slice(0, 1)
OUT_CHECK = slice(8, 16)
IN_CHECK = slice(16, 24)


def prepare(*refs):
    sources, (packed, finals, gains, lines) = refs[:COUNT], refs[COUNT : COUNT + 4]
    targets, sems = refs[COUNT + 4 : 2 * COUNT + 4], refs[2 * COUNT + 4]
    wait(
        start(
            [
                pltpu.make_async_copy(source, target, sems.at[at])
                for at, (source, target) in enumerate(zip(sources, targets))
            ]
        )
    )
    (
        out_norm_gain, out_gate, out_final_gain, out_final, in_norm_gain, in_proj, in_gate,
        in_final_gain, in_final, att_norm_gain, att_qkv, att_bias, att_gate, att_out,
        mask, out_check, in_check,
    ) = targets
    for at, line in enumerate((mask, out_check, in_check)):
        lines[at * 8 : (at + 1) * 8, :] = jnp.broadcast_to(line[...].astype(F32), (8, NT))
    packed[OUT_GATE, :] = flipped(out_gate[...])
    packed[IN_PROJ, :] = flipped(in_proj[...])
    packed[IN_GATE, :] = flipped(in_gate[...])
    packed[QUERY, :] = flipped(att_qkv[:, 0:128])
    packed[KEY, :] = att_qkv[:, 128:256]
    packed[VALUE, :] = flipped(att_qkv[:, 256:384])
    packed[ATT_GATE, :] = flipped(att_gate[...])
    packed[ATT_OUT, :] = flipped(att_out[...])
    turned = jnp.concatenate([att_bias[...], jnp.zeros((16 - HEADS, CZ), BF16)], axis=0)
    packed[BIAS.start : PACKED, :] = turned
    for at, weight in enumerate((out_final, out_final, in_final, in_final)):
        finals[:, at * CM : (at + 1) * CM] = flipped(weight[...])
    pad = jnp.zeros((1, CM), F32)
    rows = [
        out_norm_gain[...],
        in_norm_gain[...],
        att_norm_gain[...],
        jnp.concatenate([out_final_gain[...], pad], axis=1),
        jnp.concatenate([in_final_gain[...], pad], axis=1),
        jnp.zeros((3, CZ), F32),
    ]
    gains[...] = jnp.transpose(jnp.concatenate(rows, axis=0))


def gate_rows(x, packed, gains, state_out, gate_out):
    gain_col = gains[:, 0:1]
    weight_t = packed[OUT_GATE, :]
    unit = eye()
    for r in range(4):
        rows = jnp.concatenate([x[q, r] for q in range(8)], axis=0)
        state = dot(unit, rows, 1, 1)
        span = slice(r * NT, (r + 1) * NT)
        state_out[:, span] = state.astype(BF16)
        gate_out[:, span] = sigmoid(dot(weight_t, norm(state, gain_col), 1, 0)).astype(BF16)


def product_rows(mine, other, out, left, right, stage):
    core = lax.axis_index("core")
    low = lax.broadcasted_iota(jnp.int32, (16, LANES), 1) < 64

    def paired(ref, src, rows):
        first = ref[src, rows, :].astype(F32)
        second = ref[src + 1, rows, :].astype(F32)
        head = jnp.where(low, first, pltpu.roll(second, 64, 1))
        tail = jnp.where(low, pltpu.roll(first, 64, 1), second)
        return jnp.concatenate([head, tail], axis=0).astype(BF16)

    for p in range(8):
        for a in range(CHUNKS):
            lanes = slice(a * LANES, (a + 1) * LANES)
            src = p * 8 + 2 * a
            left[p * 32 : (p + 1) * 32, lanes] = paired(mine, src, slice(0, 16))
            at = pl.multiple_of(p * 64 + core * 32, 32)
            right[pl.ds(at, 32), lanes] = paired(mine, src, slice(16, 32))
            at = pl.multiple_of(p * 64 + (1 - core) * 32, 32)
            right[pl.ds(at, 32), lanes] = paired(other, src, slice(16, 32))
    product = dot(left[...], right[...], 1, 1)
    for chunk in range(CHUNKS):
        stage[pl.ds(chunk, 256, stride=4), :] = product[:, chunk * LANES : (chunk + 1) * LANES]
    out[...] = stage[...].astype(BF16).reshape(64, 16, LANES)


def update_rows(recv_stage, stride, members, state, gate, final_gain, final_t):
    product = jnp.concatenate(
        [
            recv_stage[pl.ds(r * 4 + chunk, CM, stride=stride), :]
            for r in members
            for chunk in range(CHUNKS)
        ],
        axis=1,
    )
    normed = centre(product, final_gain)
    high = normed.astype(BF16)
    low = (normed - high.astype(F32)).astype(BF16)
    update = dot(final_t, jnp.concatenate([high, low], axis=0), 1, 0)
    return state.astype(F32) + gate.astype(F32) * update


def project_rows(
    mask_s, lines, recv, state_in, gate, packed, finals, gains, out, state_out, stage, recv_stage
):
    row0 = first_row() + 4 * lax.axis_index("q")
    mask_all = lines[MASK, :]
    gain_col = gains[:, 1:2]
    final_col = gains[0:CM, 3:4]
    final_t = finals[:, 0 : 2 * CM]
    weight_t = packed[IN_PROJ, :]
    recv_stage[...] = recv[...].astype(F32).reshape(CM * 16, LANES)
    for group in range(0, 4, GROUP):
        members = range(group, group + GROUP)
        span = slice(group * NT, (group + GROUP) * NT)
        state = update_rows(
            recv_stage, 16, members, state_in[:, span], gate[:, span], final_col, final_t
        )
        state_out[:, span] = state
        mixed = dot(weight_t, norm(state, gain_col), 1, 0)
        mask = jnp.concatenate([mask_all * mask_s[row0 + r].astype(F32) for r in members], axis=1)
        left = sigmoid(mixed[0:CM]) * mixed[CM : 2 * CM] * mask
        right = sigmoid(mixed[2 * CM : 3 * CM]) * mixed[3 * CM : 4 * CM] * mask
        for at, r in enumerate(members):
            for chunk in range(CHUNKS):
                lanes = slice(at * NT + chunk * LANES, at * NT + (chunk + 1) * LANES)
                stage[pl.ds(r * 8 + chunk, CM, stride=32), :] = left[:, lanes]
                stage[pl.ds(r * 8 + 4 + chunk, CM, stride=32), :] = right[:, lanes]
    out[...] = stage[...].astype(BF16).reshape(CM, 32, LANES)


def gate_and_check(state, packed, gains, left, right, lines, gate_out, check_out):
    weight_rows = lines[OUT_CHECK, :].astype(BF16)
    total = folded(dot(thirds(dot(weight_rows, right[...], 1, 0)), left[...], 1, 1))
    check_out[...] = total / NT
    gain_col = gains[:, 1:2]
    weight_t = packed[IN_GATE, :]
    for r in range(4):
        span = slice(r * NT, (r + 1) * NT)
        normed = norm(state[:, span].astype(F32), gain_col)
        gate_out[:, span] = sigmoid(dot(weight_t, normed, 1, 0)).astype(BF16)


def product_cols(mine, other, lines, check_in, out, left, right, product, stage, stage_out):
    core = lax.axis_index("core")
    for side, buf in enumerate((mine, other)):
        stage[...] = buf[...].astype(F32).reshape(64 * 32, LANES)
        rows = slice(side * 256, (side + 1) * 256)
        for chunk in range(CHUNKS):
            lanes = slice(chunk * LANES, (chunk + 1) * LANES)
            left[rows, lanes] = stage[pl.ds(chunk, 256, stride=8), :].astype(BF16)
            right[rows, lanes] = stage[pl.ds(4 + chunk, 256, stride=8), :].astype(BF16)
    product[...] = dot(left[...], right[...], 0, 0)
    for p in range(8):
        rows = product[pl.ds(pl.multiple_of(p * 64 + core * 32, 32), 32), :]
        for chunk in range(CHUNKS):
            stage_out[pl.ds(p * 128 + chunk, 32, stride=4), :] = rows[
                :, chunk * LANES : (chunk + 1) * LANES
            ]
    out[:, 0:16, :] = stage_out[...].astype(BF16).reshape(64, 16, LANES)
    weight_rows = lines[IN_CHECK, :].astype(BF16)
    total = folded(dot(thirds(dot(weight_rows, left[...], 1, 1)), right[...], 1, 0))
    high = check_in[...].astype(BF16).astype(F32)
    lines = []
    for part, count in ((high, 2), (check_in[...] - high, 2), (total / NT, 4)):
        lines += [part[0:1, c * LANES : (c + 1) * LANES] for c in range(count)]
    tail = jnp.concatenate(lines, axis=0).astype(BF16)
    out[:, 16:24, :] = jnp.broadcast_to(tail[None], (64, 8, LANES))


def bias_rows(
    lines, recv, state_in, gate, packed, finals, gains, out, state_out, normed_out,
    recv_stage, bias_stage,
):
    live = jnp.broadcast_to(lines[MASK, :], (PACKED - BIAS.start, NT)) > 0
    gain_col = gains[:, 2:3]
    final_col = gains[0:CM, 4:5]
    final_t = finals[:, 2 * CM : 4 * CM]
    weight_t = packed[BIAS.start : PACKED, :]
    recv_stage[...] = recv[...].astype(F32).reshape(CM * 24, LANES)
    for group in range(0, 4, GROUP):
        members = range(group, group + GROUP)
        span = slice(group * NT, (group + GROUP) * NT)
        state = update_rows(
            recv_stage, 24, members, state_in[:, span], gate[:, span], final_col, final_t
        )
        state_out[:, span] = state.astype(BF16)
        normed = norm(state, gain_col)
        normed_out[:, span] = normed
        bias_all = dot(weight_t, normed, 1, 0) * LOG2E
        for at, r in enumerate(members):
            bias = bias_all[:, at * NT : (at + 1) * NT]
            top = jnp.max(jnp.where(live, bias, -LARGE), axis=1, keepdims=True)
            bias = bias - jnp.where(top > -LARGE, top, 0.0)
            for chunk in range(CHUNKS):
                bias_stage[pl.ds(r * 16 + chunk, HEADS, stride=4), :] = bias[
                    0:HEADS, chunk * LANES : (chunk + 1) * LANES
                ]
    out[...] = jnp.broadcast_to(bias_stage[...].astype(BF16)[None], (64, 64, LANES))


def attention_inputs(
    recv, mine, normed, packed,
    query_out, key_out, value_out, gate_out, check_row, check_col, mine_out,
    recv_stage, turn,
):
    mine_out[...] = mine[...].astype(F32).reshape(64 * 64, LANES)
    recv_stage[...] = recv[:, 16:24, :].astype(F32).reshape(CM * 8, LANES)
    p, q = lax.axis_index("p"), lax.axis_index("q")

    def rows_of(at):
        return recv_stage[pl.ds(at, CM, stride=8), :]

    turn[0] = jnp.transpose(rows_of(p // 4) + rows_of(2 + p // 4))
    check_row[...] = turn[0, pl.ds(pl.multiple_of(lax.rem(p, 4) * 32, 32), 32), :]
    turn[1] = jnp.transpose(rows_of(4 + q // 2))
    check_col[...] = turn[1, pl.ds(pl.multiple_of(lax.rem(q, 2) * 64, 64), 64), :]
    for r in range(4):
        span = slice(r * NT, (r + 1) * NT)
        rows = normed[:, span]
        query_out[:, span] = (dot(packed[QUERY, :], rows, 1, 0) * (LOG2E * DH ** (-0.5))).astype(
            BF16
        )
        key_out[span, :] = dot(rows, packed[KEY, :], 0, 0).astype(BF16)
        value_out[:, span] = dot(packed[VALUE, :], rows, 1, 0).astype(BF16)
        gate_out[:, span] = sigmoid(dot(packed[ATT_GATE, :], rows, 1, 0)).astype(BF16)


def attend(
    lines, mine, bias_other, query, key, value, gate, state, packed, out, other, bias
):
    first = lax.axis_index("core") == 0
    other[...] = bias_other[...].astype(F32).reshape(64 * 64, LANES)
    key_bias = jnp.where(lines[MASK, :] > 0, 0.0, -1000000000.0 * LOG2E).astype(F32)
    key_cols = [column(key_bias[:, c * LANES : (c + 1) * LANES]) for c in range(CHUNKS)]
    weight_t = packed[ATT_OUT, :]

    def turn_bias(h):
        for chunk in range(CHUNKS):
            blocks = []
            for p in range(8):
                rows = pl.ds(p * 512 + h * 4 + chunk, 32, stride=16)
                here, there = mine[rows, :], other[rows, :]
                blocks += [jnp.where(first, here, there), jnp.where(first, there, here)]
            turned = jnp.transpose(jnp.concatenate(blocks, axis=0))
            bias[h, chunk * LANES : (chunk + 1) * LANES, :] = turned + key_cols[chunk]

    def scores(h, query_row, key_row):
        zeros = jnp.zeros((DH, NT), BF16)
        masked = jnp.concatenate(
            [query_row[h * DH : (h + 1) * DH] if at == h else zeros for at in range(HEADS)], axis=0
        )
        return dot(key_row, masked, 1, 0) + bias[h]

    def weighted(h, weights, value_row):
        padded = jnp.concatenate(
            [value_row[h * DH : (h + 1) * DH], jnp.ones((16, NT), BF16)], axis=0
        )
        both = dot(padded, weights.astype(BF16), 1, 0)
        return both[0:DH] / both[DH : DH + 1], both[DH : DH + 1]

    def finish(r, span, parts):
        attended = jnp.concatenate(parts, axis=0) * gate[:, span].astype(F32)
        result = state[:, span].astype(F32) + dot(weight_t, attended.astype(BF16), 1, 0)
        out[:, r, :, :] = jnp.transpose(result).astype(BF16).reshape(8, 64, CZ)

    low = high = jnp.ones((1, NT), F32)
    parts = [[] for _ in range(4)]
    for h in range(HEADS):
        turn_bias(h)
        for r in range(4):
            span = slice(r * NT, (r + 1) * NT)
            weights = jnp.exp2(scores(h, query[:, span], key[span, :]))
            part, total = weighted(h, weights, value[:, span])
            low, high = jnp.minimum(low, total), jnp.maximum(high, total)
            parts[r].append(part)
    for r in range(4):
        finish(r, slice(r * NT, (r + 1) * NT), parts[r])
    in_range = jnp.logical_and(jnp.min(low) > 1e-25, jnp.max(high) < 1e30)

    @pl.when(jnp.logical_not(in_range))
    def _():
        def one_row(r, carry):
            span = pl.ds(pl.multiple_of(r * NT, NT), NT)
            again = []
            for h in range(HEADS):
                values = scores(h, query[:, span], key[span, :])
                weights = jnp.exp2(values - jnp.max(values, axis=0, keepdims=True))
                again.append(weighted(h, weights, value[:, span])[0])
            finish(r, span, again)
            return carry

        lax.fori_loop(0, 4, one_row, 0)


def swap(values):
    return lax.ppermute(values, "core", [(0, 1), (1, 0)])


def exchange(values, axes):
    return lax.all_to_all(values, axes, 0, 0, tiled=True)


def on_device(
    pair_input,
    token_mask,
    out_check_weights,
    in_check_weights,
    out_norm_gain,
    out_proj,
    out_gate,
    out_final_gain,
    out_final,
    in_norm_gain,
    in_proj,
    in_gate,
    in_final_gain,
    in_final,
    att_norm_gain,
    att_qkv,
    att_bias,
    att_gate,
    att_out,
):
    def row(vector):
        return vector.reshape(1, vector.shape[0])

    tokens = 4 * NT
    mask_v = row(token_mask)
    state_rows = exchange(pair_input.reshape(8, 4, 64, CZ), "q")
    (sent,) = call(
        project_tile,
        [((CM, 32, LANES), BF16)],
        [((CM * 32, LANES), F32)],
        [("s", token_mask), ("w", mask_v), ("w", pair_input.reshape(tokens, CZ)),
         ("w", row(out_norm_gain)), ("w", out_proj)],
    )
    weights = (
        row(out_norm_gain), out_gate, row(out_final_gain), out_final, row(in_norm_gain), in_proj, in_gate,
        row(in_final_gain), in_final, row(att_norm_gain), att_qkv, att_bias.T, att_gate, att_out,
        mask_v, row(out_check_weights), row(in_check_weights),
    )
    packed, finals, gains, lines = call(
        prepare,
        [((PACKED, CZ), BF16), ((CZ, 4 * CM), BF16), ((CZ, 8), F32), ((24, NT), F32)],
        [(value.shape, value.dtype) for value in weights] + [((COUNT,), None)],
        [("h", value) for value in weights],
    )
    state_rows, sent, packed, finals, gains, lines = lax.optimization_barrier(
        (state_rows, sent, packed, finals, gains, lines)
    )
    mine = exchange(sent, PLANE)
    mine, state_rows = lax.optimization_barrier((mine, state_rows))
    other = swap(mine)
    wide = (CZ, tokens)
    state, gate = call(
        gate_rows,
        [(wide, BF16), (wide, BF16)],
        [],
        [("v", state_rows), ("v", packed), ("v", gains)],
    )
    other, state, gate = lax.optimization_barrier((other, state, gate))
    sent, left, right = call(
        product_rows,
        [((64, 16, LANES), BF16), ((256, NT), BF16), ((NT, NT), BF16)],
        [((1024, LANES), F32)],
        [("v", mine), ("v", other)],
    )
    recv = exchange(sent, PLANE)
    sent, state = call(
        project_rows,
        [((CM, 32, LANES), BF16), (wide, F32)],
        [((CM * 32, LANES), F32), ((CM * 16, LANES), F32)],
        [("s", token_mask), ("v", lines), ("v", recv), ("v", state), ("v", gate),
         ("v", packed), ("v", finals), ("v", gains)],
    )
    mine = exchange(sent, PLANE)
    mine, state = lax.optimization_barrier((mine, state))
    other = swap(mine)
    gate, check_out = call(
        gate_and_check,
        [(wide, BF16), ((8, 256), F32)],
        [],
        [("v", state), ("v", packed), ("v", gains), ("v", left), ("v", right), ("v", lines)],
    )
    other, gate, check_out = lax.optimization_barrier((other, gate, check_out))
    (sent,) = call(
        product_cols,
        [((64, 24, LANES), BF16)],
        [((NT, NT), BF16), ((NT, NT), BF16), ((NT, NT), F32), ((64 * 32, LANES), F32),
         ((1024, LANES), F32)],
        [("v", mine), ("v", other), ("v", lines), ("v", check_out)],
    )
    recv = exchange(sent, PLANE)
    sent, state, normed = call(
        bias_rows,
        [((64, 64, LANES), BF16), (wide, BF16), (wide, BF16)],
        [((CM * 24, LANES), F32), ((64, LANES), F32)],
        [("v", lines), ("v", recv), ("v", state), ("v", gate), ("v", packed), ("v", finals),
         ("v", gains)],
    )
    mine = exchange(sent, PLANE)
    mine, normed = lax.optimization_barrier((mine, normed))
    other = swap(mine)
    query, key, value, gate, check_row, check_col, staged = call(
        attention_inputs,
        [(wide, BF16), ((tokens, CZ), BF16), (wide, BF16), (wide, BF16), ((32, CM), F32),
         ((64, CM), F32), ((64 * 64, LANES), F32)],
        [((CM * 8, LANES), F32), ((2, LANES, CM), F32)],
        [("v", recv), ("v", mine), ("v", normed), ("v", packed)],
    )
    other, query = lax.optimization_barrier((other, query))
    (sent,) = call(
        attend,
        [((8, 4, 64, CZ), BF16)],
        [((64 * 64, LANES), F32), ((HEADS, NT, NT), F32)],
        [("v", lines), ("v", staged), ("v", other), ("v", query), ("v", key), ("v", value),
         ("v", gate), ("v", state), ("v", packed)],
    )
    result = exchange(sent, "q").reshape(32, 64, CZ)
    return result, check_row, check_col


def solution(mesh):
    grid = Mesh(mesh.devices.reshape(8, 2, 8), ("p", "core", "q"))
    tile = P(("p", "core"), "q", None)
    in_specs = (tile,) + (P(),) * 18
    out_specs = (tile, P(("p", "core"), None), P("q", None))
    return jax.shard_map(
        on_device, mesh=grid, in_specs=in_specs, out_specs=out_specs, check_vma=False
    )
```

```python
import jax
import jax.numpy as jnp
from jax import lax
from jax.experimental import pallas as pl
from jax.experimental.pallas import tpu as pltpu
from jax.sharding import Mesh, PartitionSpec as P

F32 = jnp.float32
BF16 = jnp.bfloat16
NT = 512
CZ = 128
CM = 64
HEADS = 4
DH = 32
LANES = 128
CHUNKS = NT // LANES
PLANE = ("p", "q")
VMEM = pl.BlockSpec(memory_space=pltpu.VMEM)
SMEM = pl.BlockSpec(memory_space=pltpu.SMEM)
HBM = pl.BlockSpec(memory_space=pltpu.HBM)
SPECS = {"s": SMEM, "v": VMEM, "h": HBM, "w": VMEM}
LOG2E = 1.4426950408889634


def dot(left, right, left_dim, right_dim):
    return lax.dot_general(
        left, right, (((left_dim,), (right_dim,)), ((), ())), preferred_element_type=F32
    )


def column(row):
    return jnp.transpose(jnp.broadcast_to(row, (8, row.shape[1])))[:, 0:1]


def flipped(weight):
    return jnp.transpose(weight.astype(F32)).astype(BF16)


def eye():
    rows = lax.broadcasted_iota(jnp.int32, (LANES, LANES), 0)
    cols = lax.broadcasted_iota(jnp.int32, (LANES, LANES), 1)
    return jnp.where(rows == cols, 1.0, 0.0).astype(BF16)


def centre(values, gain_col):
    mean = jnp.mean(values, axis=0, keepdims=True)
    centered = values - mean
    variance = jnp.mean(centered * centered, axis=0, keepdims=True)
    return centered * lax.rsqrt(variance + 1e-05) * gain_col


def norm(values, gain_col):
    return centre(values, gain_col).astype(BF16)


def sigmoid(values):
    return jax.nn.sigmoid(values)


def thirds(values):
    high = values.astype(BF16)
    rest = values - high.astype(F32)
    middle = rest.astype(BF16)
    return jnp.concatenate([high, middle, (rest - middle.astype(F32)).astype(BF16)], axis=0)


def folded(parts):
    return parts[0:8] + (parts[8:16] + parts[16:24])


def call(kernel, outs, scratch, ins, mib=24):
    def shape_of(shape, kind, place="v"):
        return (pltpu.HBM if place == "h" else jax.ShapeDtypeStruct)(shape, kind)

    def placed(place, value):
        return pltpu.with_memory_space_constraint(value, pltpu.HBM) if place in "hw" else value

    return pl.pallas_call(
        kernel,
        out_shape=tuple(shape_of(*out) for out in outs),
        in_specs=[SPECS[place] for place, _ in ins],
        out_specs=tuple(HBM if out[2:] == ("h",) else VMEM for out in outs),
        scratch_shapes=[
            pltpu.SemaphoreType.DMA(shape) if kind is None else pltpu.VMEM(shape, kind)
            for shape, kind in scratch
        ],
        compiler_params=pltpu.CompilerParams(vmem_limit_bytes=mib * 1024 * 1024),
    )(*[placed(place, value) for place, value in ins])


def start(copies):
    for copy in copies:
        copy.start()
    return copies


def wait(copies):
    for copy in copies:
        copy.wait()


def first_row():
    return (2 * lax.axis_index("p") + lax.axis_index("core")) * 32


def project_tile(mask_s, mask_v, x, gain, weight, out, stage):
    row0 = first_row()
    shift = lax.rem(NT - 64 * lax.axis_index("q"), NT)
    mask_all = jnp.broadcast_to(mask_v[...].astype(F32), (8, NT))
    col_mask = pltpu.roll(mask_all, shift, 1)[0:1, 0:64]
    gain_col = column(gain[...])
    weight_t = flipped(weight[...])
    unit = eye()
    for group in range(4):
        steps = range(group * 4, group * 4 + 4)
        pieces, masks = [], []
        for s in steps:
            for i in (s, s + 16):
                pieces.append(x[i * 64 : (i + 1) * 64, :])
                masks.append(col_mask * mask_s[row0 + i].astype(F32))
        state = dot(unit, jnp.concatenate(pieces, axis=0), 1, 1)
        mask = jnp.concatenate(masks, axis=1)
        mixed = dot(weight_t, norm(state, gain_col), 1, 0)
        left = sigmoid(mixed[0:CM]) * mixed[CM : 2 * CM] * mask
        right = sigmoid(mixed[2 * CM : 3 * CM]) * mixed[3 * CM : 4 * CM] * mask
        for at, s in enumerate(steps):
            lanes = slice(at * LANES, (at + 1) * LANES)
            stage[pl.ds(s, CM, stride=32), :] = left[:, lanes]
            stage[pl.ds(16 + s, CM, stride=32), :] = right[:, lanes]
    out[...] = stage[...].astype(BF16).reshape(CM, 32, LANES)


OUT_GATE = slice(0, 128)
IN_PROJ = slice(128, 384)
IN_GATE = slice(384, 512)
QUERY = slice(512, 640)
KEY = slice(640, 768)
VALUE = slice(768, 896)
ATT_GATE = slice(896, 1024)
ATT_OUT = slice(1024, 1152)
BIAS = slice(1152, 1156)
PACKED = 1168
GROUP = 4
LARGE = 3e38
COUNT = 17
MASK = slice(0, 1)
OUT_CHECK = slice(8, 16)
IN_CHECK = slice(16, 24)


def prepare(*refs):
    sources, (packed, finals, gains, lines) = refs[:COUNT], refs[COUNT : COUNT + 4]
    targets, sems = refs[COUNT + 4 : 2 * COUNT + 4], refs[2 * COUNT + 4]
    wait(
        start(
            [
                pltpu.make_async_copy(source, target, sems.at[at])
                for at, (source, target) in enumerate(zip(sources, targets))
            ]
        )
    )
    (
        out_norm_gain, out_gate, out_final_gain, out_final, in_norm_gain, in_proj, in_gate,
        in_final_gain, in_final, att_norm_gain, att_qkv, att_bias, att_gate, att_out,
        mask, out_check, in_check,
    ) = targets
    for at, line in enumerate((mask, out_check, in_check)):
        lines[at * 8 : (at + 1) * 8, :] = jnp.broadcast_to(line[...].astype(F32), (8, NT))
    packed[OUT_GATE, :] = flipped(out_gate[...])
    packed[IN_PROJ, :] = flipped(in_proj[...])
    packed[IN_GATE, :] = flipped(in_gate[...])
    packed[QUERY, :] = flipped(att_qkv[:, 0:128])
    packed[KEY, :] = att_qkv[:, 128:256]
    packed[VALUE, :] = flipped(att_qkv[:, 256:384])
    packed[ATT_GATE, :] = flipped(att_gate[...])
    packed[ATT_OUT, :] = flipped(att_out[...])
    turned = jnp.concatenate([att_bias[...], jnp.zeros((16 - HEADS, CZ), BF16)], axis=0)
    packed[BIAS.start : PACKED, :] = turned
    for at, weight in enumerate((out_final, out_final, in_final, in_final)):
        finals[:, at * CM : (at + 1) * CM] = flipped(weight[...])
    pad = jnp.zeros((1, CM), F32)
    rows = [
        out_norm_gain[...],
        in_norm_gain[...],
        att_norm_gain[...],
        jnp.concatenate([out_final_gain[...], pad], axis=1),
        jnp.concatenate([in_final_gain[...], pad], axis=1),
        jnp.zeros((3, CZ), F32),
    ]
    gains[...] = jnp.transpose(jnp.concatenate(rows, axis=0))


def gate_rows(x, packed, gains, state_out, gate_out):
    gain_col = gains[:, 0:1]
    weight_t = packed[OUT_GATE, :]
    unit = eye()
    for r in range(4):
        rows = jnp.concatenate([x[q, r] for q in range(8)], axis=0)
        state = dot(unit, rows, 1, 1)
        span = slice(r * NT, (r + 1) * NT)
        state_out[:, span] = state.astype(BF16)
        gate_out[:, span] = sigmoid(dot(weight_t, norm(state, gain_col), 1, 0)).astype(BF16)


def product_rows(mine, other, out, left, right, stage):
    core = lax.axis_index("core")
    low = lax.broadcasted_iota(jnp.int32, (16, LANES), 1) < 64

    def paired(ref, src, rows):
        first = ref[src, rows, :].astype(F32)
        second = ref[src + 1, rows, :].astype(F32)
        head = jnp.where(low, first, pltpu.roll(second, 64, 1))
        tail = jnp.where(low, pltpu.roll(first, 64, 1), second)
        return jnp.concatenate([head, tail], axis=0).astype(BF16)

    for p in range(8):
        for a in range(CHUNKS):
            lanes = slice(a * LANES, (a + 1) * LANES)
            src = p * 8 + 2 * a
            left[p * 32 : (p + 1) * 32, lanes] = paired(mine, src, slice(0, 16))
            at = pl.multiple_of(p * 64 + core * 32, 32)
            right[pl.ds(at, 32), lanes] = paired(mine, src, slice(16, 32))
            at = pl.multiple_of(p * 64 + (1 - core) * 32, 32)
            right[pl.ds(at, 32), lanes] = paired(other, src, slice(16, 32))
    product = dot(left[...], right[...], 1, 1)
    for chunk in range(CHUNKS):
        stage[pl.ds(chunk, 256, stride=4), :] = product[:, chunk * LANES : (chunk + 1) * LANES]
    out[...] = stage[...].astype(BF16).reshape(64, 16, LANES)


def update_rows(recv_stage, stride, members, state, gate, final_gain, final_t):
    product = jnp.concatenate(
        [
            recv_stage[pl.ds(r * 4 + chunk, CM, stride=stride), :]
            for r in members
            for chunk in range(CHUNKS)
        ],
        axis=1,
    )
    normed = centre(product, final_gain)
    high = normed.astype(BF16)
    low = (normed - high.astype(F32)).astype(BF16)
    update = dot(final_t, jnp.concatenate([high, low], axis=0), 1, 0)
    return state.astype(F32) + gate.astype(F32) * update


def project_rows(
    mask_s, lines, recv, state_in, gate, packed, finals, gains, out, state_out, stage, recv_stage
):
    row0 = first_row() + 4 * lax.axis_index("q")
    mask_all = lines[MASK, :]
    gain_col = gains[:, 1:2]
    final_col = gains[0:CM, 3:4]
    final_t = finals[:, 0 : 2 * CM]
    weight_t = packed[IN_PROJ, :]
    recv_stage[...] = recv[...].astype(F32).reshape(CM * 16, LANES)
    for group in range(0, 4, GROUP):
        members = range(group, group + GROUP)
        span = slice(group * NT, (group + GROUP) * NT)
        state = update_rows(
            recv_stage, 16, members, state_in[:, span], gate[:, span], final_col, final_t
        )
        state_out[:, span] = state
        mixed = dot(weight_t, norm(state, gain_col), 1, 0)
        mask = jnp.concatenate([mask_all * mask_s[row0 + r].astype(F32) for r in members], axis=1)
        left = sigmoid(mixed[0:CM]) * mixed[CM : 2 * CM] * mask
        right = sigmoid(mixed[2 * CM : 3 * CM]) * mixed[3 * CM : 4 * CM] * mask
        for at, r in enumerate(members):
            for chunk in range(CHUNKS):
                lanes = slice(at * NT + chunk * LANES, at * NT + (chunk + 1) * LANES)
                stage[pl.ds(r * 8 + chunk, CM, stride=32), :] = left[:, lanes]
                stage[pl.ds(r * 8 + 4 + chunk, CM, stride=32), :] = right[:, lanes]
    out[...] = stage[...].astype(BF16).reshape(CM, 32, LANES)


def gate_and_check(state, packed, gains, left, right, lines, gate_out, check_out):
    weight_rows = lines[OUT_CHECK, :].astype(BF16)
    total = folded(dot(thirds(dot(weight_rows, right[...], 1, 0)), left[...], 1, 1))
    check_out[...] = total / NT
    gain_col = gains[:, 1:2]
    weight_t = packed[IN_GATE, :]
    for r in range(4):
        span = slice(r * NT, (r + 1) * NT)
        normed = norm(state[:, span].astype(F32), gain_col)
        gate_out[:, span] = sigmoid(dot(weight_t, normed, 1, 0)).astype(BF16)


def product_cols(mine, other, lines, check_in, out, left, right, product, stage, stage_out):
    core = lax.axis_index("core")
    for side, buf in enumerate((mine, other)):
        stage[...] = buf[...].astype(F32).reshape(64 * 32, LANES)
        rows = slice(side * 256, (side + 1) * 256)
        for chunk in range(CHUNKS):
            lanes = slice(chunk * LANES, (chunk + 1) * LANES)
            left[rows, lanes] = stage[pl.ds(chunk, 256, stride=8), :].astype(BF16)
            right[rows, lanes] = stage[pl.ds(4 + chunk, 256, stride=8), :].astype(BF16)
    product[...] = dot(left[...], right[...], 0, 0)
    for p in range(8):
        rows = product[pl.ds(pl.multiple_of(p * 64 + core * 32, 32), 32), :]
        for chunk in range(CHUNKS):
            stage_out[pl.ds(p * 128 + chunk, 32, stride=4), :] = rows[
                :, chunk * LANES : (chunk + 1) * LANES
            ]
    out[:, 0:16, :] = stage_out[...].astype(BF16).reshape(64, 16, LANES)
    weight_rows = lines[IN_CHECK, :].astype(BF16)
    total = folded(dot(thirds(dot(weight_rows, left[...], 1, 1)), right[...], 1, 0))
    high = check_in[...].astype(BF16).astype(F32)
    lines = []
    for part, count in ((high, 2), (check_in[...] - high, 2), (total / NT, 4)):
        lines += [part[0:1, c * LANES : (c + 1) * LANES] for c in range(count)]
    tail = jnp.concatenate(lines, axis=0).astype(BF16)
    out[:, 16:24, :] = jnp.broadcast_to(tail[None], (64, 8, LANES))


def bias_rows(
    lines, recv, state_in, gate, packed, finals, gains, out, state_out, normed_out,
    recv_stage, bias_stage,
):
    live = jnp.broadcast_to(lines[MASK, :], (PACKED - BIAS.start, NT)) > 0
    gain_col = gains[:, 2:3]
    final_col = gains[0:CM, 4:5]
    final_t = finals[:, 2 * CM : 4 * CM]
    weight_t = packed[BIAS.start : PACKED, :]
    recv_stage[...] = recv[...].astype(F32).reshape(CM * 24, LANES)
    for group in range(0, 4, GROUP):
        members = range(group, group + GROUP)
        span = slice(group * NT, (group + GROUP) * NT)
        state = update_rows(
            recv_stage, 24, members, state_in[:, span], gate[:, span], final_col, final_t
        )
        state_out[:, span] = state.astype(BF16)
        normed = norm(state, gain_col)
        normed_out[:, span] = normed
        bias_all = dot(weight_t, normed, 1, 0) * LOG2E
        for at, r in enumerate(members):
            bias = bias_all[:, at * NT : (at + 1) * NT]
            top = jnp.max(jnp.where(live, bias, -LARGE), axis=1, keepdims=True)
            bias = bias - jnp.where(top > -LARGE, top, 0.0)
            for chunk in range(CHUNKS):
                bias_stage[pl.ds(r * 16 + chunk, HEADS, stride=4), :] = bias[
                    0:HEADS, chunk * LANES : (chunk + 1) * LANES
                ]
    out[...] = jnp.broadcast_to(bias_stage[...].astype(BF16)[None], (64, 64, LANES))


def attention_inputs(
    recv, mine, normed, packed,
    query_out, key_out, value_out, gate_out, check_row, check_col, mine_out,
    recv_stage, turn,
):
    mine_out[...] = mine[...].astype(F32).reshape(64 * 64, LANES)
    recv_stage[...] = recv[:, 16:24, :].astype(F32).reshape(CM * 8, LANES)
    p, q = lax.axis_index("p"), lax.axis_index("q")

    def rows_of(at):
        return recv_stage[pl.ds(at, CM, stride=8), :]

    turn[0] = jnp.transpose(rows_of(p // 4) + rows_of(2 + p // 4))
    check_row[...] = turn[0, pl.ds(pl.multiple_of(lax.rem(p, 4) * 32, 32), 32), :]
    turn[1] = jnp.transpose(rows_of(4 + q // 2))
    check_col[...] = turn[1, pl.ds(pl.multiple_of(lax.rem(q, 2) * 64, 64), 64), :]
    for r in range(4):
        span = slice(r * NT, (r + 1) * NT)
        rows = normed[:, span]
        query_out[:, span] = (dot(packed[QUERY, :], rows, 1, 0) * (LOG2E * DH ** (-0.5))).astype(
            BF16
        )
        key_out[span, :] = dot(rows, packed[KEY, :], 0, 0).astype(BF16)
        value_out[:, span] = dot(packed[VALUE, :], rows, 1, 0).astype(BF16)
        gate_out[:, span] = sigmoid(dot(packed[ATT_GATE, :], rows, 1, 0)).astype(BF16)


def attend(
    lines, mine, bias_other, query, key, value, gate, state, packed, out, other, bias
):
    first = lax.axis_index("core") == 0
    other[...] = bias_other[...].astype(F32).reshape(64 * 64, LANES)
    key_bias = jnp.where(lines[MASK, :] > 0, 0.0, -1000000000.0 * LOG2E).astype(F32)
    key_cols = [column(key_bias[:, c * LANES : (c + 1) * LANES]) for c in range(CHUNKS)]
    weight_t = packed[ATT_OUT, :]

    def turn_bias(h):
        for chunk in range(CHUNKS):
            blocks = []
            for p in range(8):
                rows = pl.ds(p * 512 + h * 4 + chunk, 32, stride=16)
                here, there = mine[rows, :], other[rows, :]
                blocks += [jnp.where(first, here, there), jnp.where(first, there, here)]
            turned = jnp.transpose(jnp.concatenate(blocks, axis=0))
            bias[h, chunk * LANES : (chunk + 1) * LANES, :] = turned + key_cols[chunk]

    def scores(h, query_row, key_row):
        zeros = jnp.zeros((DH, NT), BF16)
        masked = jnp.concatenate(
            [query_row[h * DH : (h + 1) * DH] if at == h else zeros for at in range(HEADS)], axis=0
        )
        return dot(key_row, masked, 1, 0) + bias[h]

    def weighted(h, weights, value_row):
        padded = jnp.concatenate(
            [value_row[h * DH : (h + 1) * DH], jnp.ones((16, NT), BF16)], axis=0
        )
        both = dot(padded, weights.astype(BF16), 1, 0)
        return both[0:DH] / both[DH : DH + 1], both[DH : DH + 1]

    def finish(r, span, parts):
        attended = jnp.concatenate(parts, axis=0) * gate[:, span].astype(F32)
        result = state[:, span].astype(F32) + dot(weight_t, attended.astype(BF16), 1, 0)
        out[:, r, :, :] = jnp.transpose(result).astype(BF16).reshape(8, 64, CZ)

    low = high = jnp.ones((1, NT), F32)
    parts = [[] for _ in range(4)]
    def weights_of(h, r):
        span = slice(r * NT, (r + 1) * NT)
        return jnp.exp2(scores(h, query[:, span], key[span, :])).astype(BF16)

    turn_bias(0)
    order = [(h, r) for h in range(HEADS) for r in range(4)]
    ahead = weights_of(0, 0)
    for at, (h, r) in enumerate(order):
        weights = ahead
        if at + 1 < len(order):
            if r == 2 and h + 1 < HEADS:
                turn_bias(h + 1)
            ahead = weights_of(*order[at + 1])
        part, total = weighted(h, weights, value[:, r * NT : (r + 1) * NT])
        low, high = jnp.minimum(low, total), jnp.maximum(high, total)
        parts[r].append(part)
    for r in range(4):
        finish(r, slice(r * NT, (r + 1) * NT), parts[r])
    in_range = jnp.logical_and(jnp.min(low) > 1e-25, jnp.max(high) < 1e30)

    @pl.when(jnp.logical_not(in_range))
    def _():
        def one_row(r, carry):
            span = pl.ds(pl.multiple_of(r * NT, NT), NT)
            again = []
            for h in range(HEADS):
                values = scores(h, query[:, span], key[span, :])
                weights = jnp.exp2(values - jnp.max(values, axis=0, keepdims=True))
                again.append(weighted(h, weights, value[:, span])[0])
            finish(r, span, again)
            return carry

        lax.fori_loop(0, 4, one_row, 0)


def swap(values):
    return lax.ppermute(values, "core", [(0, 1), (1, 0)])


def exchange(values, axes):
    return lax.all_to_all(values, axes, 0, 0, tiled=True)


def on_device(
    pair_input,
    token_mask,
    out_check_weights,
    in_check_weights,
    out_norm_gain,
    out_proj,
    out_gate,
    out_final_gain,
    out_final,
    in_norm_gain,
    in_proj,
    in_gate,
    in_final_gain,
    in_final,
    att_norm_gain,
    att_qkv,
    att_bias,
    att_gate,
    att_out,
):
    def row(vector):
        return vector.reshape(1, vector.shape[0])

    tokens = 4 * NT
    mask_v = row(token_mask)
    state_rows = exchange(pair_input.reshape(8, 4, 64, CZ), "q")
    (sent,) = call(
        project_tile,
        [((CM, 32, LANES), BF16)],
        [((CM * 32, LANES), F32)],
        [("s", token_mask), ("w", mask_v), ("w", pair_input.reshape(tokens, CZ)),
         ("w", row(out_norm_gain)), ("w", out_proj)],
    )
    weights = (
        row(out_norm_gain), out_gate, row(out_final_gain), out_final, row(in_norm_gain), in_proj, in_gate,
        row(in_final_gain), in_final, row(att_norm_gain), att_qkv, att_bias.T, att_gate, att_out,
        mask_v, row(out_check_weights), row(in_check_weights),
    )
    packed, finals, gains, lines = call(
        prepare,
        [((PACKED, CZ), BF16), ((CZ, 4 * CM), BF16), ((CZ, 8), F32), ((24, NT), F32)],
        [(value.shape, value.dtype) for value in weights] + [((COUNT,), None)],
        [("h", value) for value in weights],
    )
    state_rows, sent, packed, finals, gains, lines = lax.optimization_barrier(
        (state_rows, sent, packed, finals, gains, lines)
    )
    mine = exchange(sent, PLANE)
    mine, state_rows = lax.optimization_barrier((mine, state_rows))
    other = swap(mine)
    wide = (CZ, tokens)
    state, gate = call(
        gate_rows,
        [(wide, BF16), (wide, BF16)],
        [],
        [("v", state_rows), ("v", packed), ("v", gains)],
    )
    other, state, gate = lax.optimization_barrier((other, state, gate))
    sent, left, right = call(
        product_rows,
        [((64, 16, LANES), BF16), ((256, NT), BF16), ((NT, NT), BF16)],
        [((1024, LANES), F32)],
        [("v", mine), ("v", other)],
    )
    recv = exchange(sent, PLANE)
    sent, state = call(
        project_rows,
        [((CM, 32, LANES), BF16), (wide, F32)],
        [((CM * 32, LANES), F32), ((CM * 16, LANES), F32)],
        [("s", token_mask), ("v", lines), ("v", recv), ("v", state), ("v", gate),
         ("v", packed), ("v", finals), ("v", gains)],
    )
    mine = exchange(sent, PLANE)
    mine, state = lax.optimization_barrier((mine, state))
    other = swap(mine)
    gate, check_out = call(
        gate_and_check,
        [(wide, BF16), ((8, 256), F32)],
        [],
        [("v", state), ("v", packed), ("v", gains), ("v", left), ("v", right), ("v", lines)],
    )
    other, gate, check_out = lax.optimization_barrier((other, gate, check_out))
    (sent,) = call(
        product_cols,
        [((64, 24, LANES), BF16)],
        [((NT, NT), BF16), ((NT, NT), BF16), ((NT, NT), F32), ((64 * 32, LANES), F32),
         ((1024, LANES), F32)],
        [("v", mine), ("v", other), ("v", lines), ("v", check_out)],
    )
    recv = exchange(sent, PLANE)
    sent, state, normed = call(
        bias_rows,
        [((64, 64, LANES), BF16), (wide, BF16), (wide, BF16)],
        [((CM * 24, LANES), F32), ((64, LANES), F32)],
        [("v", lines), ("v", recv), ("v", state), ("v", gate), ("v", packed), ("v", finals),
         ("v", gains)],
    )
    mine = exchange(sent, PLANE)
    mine, normed = lax.optimization_barrier((mine, normed))
    other = swap(mine)
    query, key, value, gate, check_row, check_col, staged = call(
        attention_inputs,
        [(wide, BF16), ((tokens, CZ), BF16), (wide, BF16), (wide, BF16), ((32, CM), F32),
         ((64, CM), F32), ((64 * 64, LANES), F32)],
        [((CM * 8, LANES), F32), ((2, LANES, CM), F32)],
        [("v", recv), ("v", mine), ("v", normed), ("v", packed)],
    )
    other, query = lax.optimization_barrier((other, query))
    (sent,) = call(
        attend,
        [((8, 4, 64, CZ), BF16)],
        [((64 * 64, LANES), F32), ((HEADS, NT, NT), F32)],
        [("v", lines), ("v", staged), ("v", other), ("v", query), ("v", key), ("v", value),
         ("v", gate), ("v", state), ("v", packed)],
    )
    result = exchange(sent, "q").reshape(32, 64, CZ)
    return result, check_row, check_col


def solution(mesh):
    grid = Mesh(mesh.devices.reshape(8, 2, 8), ("p", "core", "q"))
    tile = P(("p", "core"), "q", None)
    in_specs = (tile,) + (P(),) * 18
    out_specs = (tile, P(("p", "core"), None), P("q", None))
    return jax.shard_map(
        on_device, mesh=grid, in_specs=in_specs, out_specs=out_specs, check_vma=False
    )
```

```python
import jax
import jax.numpy as jnp
from jax import lax
from jax.experimental import pallas as pl
from jax.experimental.pallas import tpu as pltpu
from jax.sharding import Mesh, PartitionSpec as P

F32 = jnp.float32
BF16 = jnp.bfloat16
NT = 512
CZ = 128
CM = 64
HEADS = 4
DH = 32
LANES = 128
CHUNKS = NT // LANES
PLANE = ("p", "q")
VMEM = pl.BlockSpec(memory_space=pltpu.VMEM)
SMEM = pl.BlockSpec(memory_space=pltpu.SMEM)
HBM = pl.BlockSpec(memory_space=pltpu.HBM)
SPECS = {"s": SMEM, "v": VMEM, "h": HBM, "w": VMEM}
LOG2E = 1.4426950408889634


def dot(left, right, left_dim, right_dim):
    return lax.dot_general(
        left, right, (((left_dim,), (right_dim,)), ((), ())), preferred_element_type=F32
    )


def column(row):
    return jnp.transpose(jnp.broadcast_to(row, (8, row.shape[1])))[:, 0:1]


def flipped(weight):
    return jnp.transpose(weight.astype(F32)).astype(BF16)


def eye():
    rows = lax.broadcasted_iota(jnp.int32, (LANES, LANES), 0)
    cols = lax.broadcasted_iota(jnp.int32, (LANES, LANES), 1)
    return jnp.where(rows == cols, 1.0, 0.0).astype(BF16)


def centre(values, gain_col):
    mean = jnp.mean(values, axis=0, keepdims=True)
    centered = values - mean
    variance = jnp.mean(centered * centered, axis=0, keepdims=True)
    return centered * lax.rsqrt(variance + 1e-05) * gain_col


def norm(values, gain_col):
    return centre(values, gain_col).astype(BF16)


def sigmoid(values):
    return jax.nn.sigmoid(values)


def thirds(values):
    high = values.astype(BF16)
    rest = values - high.astype(F32)
    middle = rest.astype(BF16)
    return jnp.concatenate([high, middle, (rest - middle.astype(F32)).astype(BF16)], axis=0)


def folded(parts):
    return parts[0:8] + (parts[8:16] + parts[16:24])


def call(kernel, outs, scratch, ins, mib=24):
    def shape_of(shape, kind, place="v"):
        return (pltpu.HBM if place == "h" else jax.ShapeDtypeStruct)(shape, kind)

    def placed(place, value):
        return pltpu.with_memory_space_constraint(value, pltpu.HBM) if place in "hw" else value

    return pl.pallas_call(
        kernel,
        out_shape=tuple(shape_of(*out) for out in outs),
        in_specs=[SPECS[place] for place, _ in ins],
        out_specs=tuple(HBM if out[2:] == ("h",) else VMEM for out in outs),
        scratch_shapes=[
            pltpu.SemaphoreType.DMA(shape) if kind is None else pltpu.VMEM(shape, kind)
            for shape, kind in scratch
        ],
        compiler_params=pltpu.CompilerParams(vmem_limit_bytes=mib * 1024 * 1024),
    )(*[placed(place, value) for place, value in ins])


def start(copies):
    for copy in copies:
        copy.start()
    return copies


def wait(copies):
    for copy in copies:
        copy.wait()


def first_row():
    return (2 * lax.axis_index("p") + lax.axis_index("core")) * 32


def project_tile(mask_s, mask_v, x, gain, weight, out, stage):
    row0 = first_row()
    shift = lax.rem(NT - 64 * lax.axis_index("q"), NT)
    mask_all = jnp.broadcast_to(mask_v[...].astype(F32), (8, NT))
    col_mask = pltpu.roll(mask_all, shift, 1)[0:1, 0:64]
    gain_col = column(gain[...])
    weight_t = flipped(weight[...])
    unit = eye()
    for group in range(4):
        steps = range(group * 4, group * 4 + 4)
        pieces, masks = [], []
        for s in steps:
            for i in (s, s + 16):
                pieces.append(x[i * 64 : (i + 1) * 64, :])
                masks.append(col_mask * mask_s[row0 + i].astype(F32))
        state = dot(unit, jnp.concatenate(pieces, axis=0), 1, 1)
        mask = jnp.concatenate(masks, axis=1)
        mixed = dot(weight_t, norm(state, gain_col), 1, 0)
        left = sigmoid(mixed[0:CM]) * mixed[CM : 2 * CM] * mask
        right = sigmoid(mixed[2 * CM : 3 * CM]) * mixed[3 * CM : 4 * CM] * mask
        for at, s in enumerate(steps):
            lanes = slice(at * LANES, (at + 1) * LANES)
            stage[pl.ds(s, CM, stride=32), :] = left[:, lanes]
            stage[pl.ds(16 + s, CM, stride=32), :] = right[:, lanes]
    out[...] = stage[...].astype(BF16).reshape(CM, 32, LANES)


OUT_GATE = slice(0, 128)
IN_PROJ = slice(128, 384)
IN_GATE = slice(384, 512)
QUERY = slice(512, 640)
KEY = slice(640, 768)
VALUE = slice(768, 896)
ATT_GATE = slice(896, 1024)
ATT_OUT = slice(1024, 1152)
BIAS = slice(1152, 1156)
PACKED = 1168
GROUP = 4
LARGE = 3e38
COUNT = 17
MASK = slice(0, 1)
OUT_CHECK = slice(8, 16)
IN_CHECK = slice(16, 24)


def prepare(*refs):
    sources, (packed, finals, gains, lines) = refs[:COUNT], refs[COUNT : COUNT + 4]
    targets, sems = refs[COUNT + 4 : 2 * COUNT + 4], refs[2 * COUNT + 4]
    wait(
        start(
            [
                pltpu.make_async_copy(source, target, sems.at[at])
                for at, (source, target) in enumerate(zip(sources, targets))
            ]
        )
    )
    (
        out_norm_gain, out_gate, out_final_gain, out_final, in_norm_gain, in_proj, in_gate,
        in_final_gain, in_final, att_norm_gain, att_qkv, att_bias, att_gate, att_out,
        mask, out_check, in_check,
    ) = targets
    for at, line in enumerate((mask, out_check, in_check)):
        lines[at * 8 : (at + 1) * 8, :] = jnp.broadcast_to(line[...].astype(F32), (8, NT))
    packed[OUT_GATE, :] = flipped(out_gate[...])
    packed[IN_PROJ, :] = flipped(in_proj[...])
    packed[IN_GATE, :] = flipped(in_gate[...])
    packed[QUERY, :] = flipped(att_qkv[:, 0:128])
    packed[KEY, :] = att_qkv[:, 128:256]
    packed[VALUE, :] = flipped(att_qkv[:, 256:384])
    packed[ATT_GATE, :] = flipped(att_gate[...])
    packed[ATT_OUT, :] = flipped(att_out[...])
    packed[BIAS.start : PACKED, :] = att_bias[...]
    for at, weight in enumerate((out_final, out_final, in_final, in_final)):
        finals[:, at * CM : (at + 1) * CM] = flipped(weight[...])
    pad = jnp.zeros((1, CM), F32)
    rows = [
        out_norm_gain[...],
        in_norm_gain[...],
        att_norm_gain[...],
        jnp.concatenate([out_final_gain[...], pad], axis=1),
        jnp.concatenate([in_final_gain[...], pad], axis=1),
        jnp.zeros((3, CZ), F32),
    ]
    gains[...] = jnp.transpose(jnp.concatenate(rows, axis=0))


def gate_rows(x, packed, gains, state_out, gate_out):
    gain_col = gains[:, 0:1]
    weight_t = packed[OUT_GATE, :]
    unit = eye()
    for r in range(4):
        rows = jnp.concatenate([x[q, r] for q in range(8)], axis=0)
        state = dot(unit, rows, 1, 1)
        span = slice(r * NT, (r + 1) * NT)
        state_out[:, span] = state.astype(BF16)
        gate_out[:, span] = sigmoid(dot(weight_t, norm(state, gain_col), 1, 0)).astype(BF16)


def product_rows(mine, other, out, left, right, stage):
    core = lax.axis_index("core")
    low = lax.broadcasted_iota(jnp.int32, (16, LANES), 1) < 64

    def paired(ref, src, rows):
        first = ref[src, rows, :].astype(F32)
        second = ref[src + 1, rows, :].astype(F32)
        head = jnp.where(low, first, pltpu.roll(second, 64, 1))
        tail = jnp.where(low, pltpu.roll(first, 64, 1), second)
        return jnp.concatenate([head, tail], axis=0).astype(BF16)

    for p in range(8):
        for a in range(CHUNKS):
            lanes = slice(a * LANES, (a + 1) * LANES)
            src = p * 8 + 2 * a
            left[p * 32 : (p + 1) * 32, lanes] = paired(mine, src, slice(0, 16))
            at = pl.multiple_of(p * 64 + core * 32, 32)
            right[pl.ds(at, 32), lanes] = paired(mine, src, slice(16, 32))
            at = pl.multiple_of(p * 64 + (1 - core) * 32, 32)
            right[pl.ds(at, 32), lanes] = paired(other, src, slice(16, 32))
    product = dot(left[...], right[...], 1, 1)
    for chunk in range(CHUNKS):
        stage[pl.ds(chunk, 256, stride=4), :] = product[:, chunk * LANES : (chunk + 1) * LANES]
    out[...] = stage[...].astype(BF16).reshape(64, 16, LANES)


def update_rows(recv_stage, stride, members, state, gate, final_gain, final_t):
    product = jnp.concatenate(
        [
            recv_stage[pl.ds(r * 4 + chunk, CM, stride=stride), :]
            for r in members
            for chunk in range(CHUNKS)
        ],
        axis=1,
    )
    normed = centre(product, final_gain)
    high = normed.astype(BF16)
    low = (normed - high.astype(F32)).astype(BF16)
    update = dot(final_t, jnp.concatenate([high, low], axis=0), 1, 0)
    return state.astype(F32) + gate.astype(F32) * update


def project_rows(
    mask_s, lines, recv, state_in, gate, packed, finals, gains, out, state_out, stage, recv_stage
):
    row0 = first_row() + 4 * lax.axis_index("q")
    mask_all = lines[MASK, :]
    gain_col = gains[:, 1:2]
    final_col = gains[0:CM, 3:4]
    final_t = finals[:, 0 : 2 * CM]
    weight_t = packed[IN_PROJ, :]
    recv_stage[...] = recv[...].astype(F32).reshape(CM * 16, LANES)
    for group in range(0, 4, GROUP):
        members = range(group, group + GROUP)
        span = slice(group * NT, (group + GROUP) * NT)
        state = update_rows(
            recv_stage, 16, members, state_in[:, span], gate[:, span], final_col, final_t
        )
        state_out[:, span] = state
        mixed = dot(weight_t, norm(state, gain_col), 1, 0)
        mask = jnp.concatenate([mask_all * mask_s[row0 + r].astype(F32) for r in members], axis=1)
        left = sigmoid(mixed[0:CM]) * mixed[CM : 2 * CM] * mask
        right = sigmoid(mixed[2 * CM : 3 * CM]) * mixed[3 * CM : 4 * CM] * mask
        for at, r in enumerate(members):
            for chunk in range(CHUNKS):
                lanes = slice(at * NT + chunk * LANES, at * NT + (chunk + 1) * LANES)
                stage[pl.ds(r * 8 + chunk, CM, stride=32), :] = left[:, lanes]
                stage[pl.ds(r * 8 + 4 + chunk, CM, stride=32), :] = right[:, lanes]
    out[...] = stage[...].astype(BF16).reshape(CM, 32, LANES)


def gate_and_check(state, packed, gains, left, right, lines, gate_out, check_out):
    weight_rows = lines[OUT_CHECK, :].astype(BF16)
    total = folded(dot(thirds(dot(weight_rows, right[...], 1, 0)), left[...], 1, 1))
    check_out[...] = total / NT
    gain_col = gains[:, 1:2]
    weight_t = packed[IN_GATE, :]
    for r in range(4):
        span = slice(r * NT, (r + 1) * NT)
        normed = norm(state[:, span].astype(F32), gain_col)
        gate_out[:, span] = sigmoid(dot(weight_t, normed, 1, 0)).astype(BF16)


def product_cols(mine, other, lines, check_in, out, left, right, product, stage, stage_out):
    core = lax.axis_index("core")
    for side, buf in enumerate((mine, other)):
        stage[...] = buf[...].astype(F32).reshape(64 * 32, LANES)
        rows = slice(side * 256, (side + 1) * 256)
        for chunk in range(CHUNKS):
            lanes = slice(chunk * LANES, (chunk + 1) * LANES)
            left[rows, lanes] = stage[pl.ds(chunk, 256, stride=8), :].astype(BF16)
            right[rows, lanes] = stage[pl.ds(4 + chunk, 256, stride=8), :].astype(BF16)
    product[...] = dot(left[...], right[...], 0, 0)
    for p in range(8):
        rows = product[pl.ds(pl.multiple_of(p * 64 + core * 32, 32), 32), :]
        for chunk in range(CHUNKS):
            stage_out[pl.ds(p * 128 + chunk, 32, stride=4), :] = rows[
                :, chunk * LANES : (chunk + 1) * LANES
            ]
    out[:, 0:16, :] = stage_out[...].astype(BF16).reshape(64, 16, LANES)
    weight_rows = lines[IN_CHECK, :].astype(BF16)
    total = folded(dot(thirds(dot(weight_rows, left[...], 1, 1)), right[...], 1, 0))
    high = check_in[...].astype(BF16).astype(F32)
    lines = []
    for part, count in ((high, 2), (check_in[...] - high, 2), (total / NT, 4)):
        lines += [part[0:1, c * LANES : (c + 1) * LANES] for c in range(count)]
    tail = jnp.concatenate(lines, axis=0).astype(BF16)
    out[:, 16:24, :] = jnp.broadcast_to(tail[None], (64, 8, LANES))


def bias_rows(
    lines, recv, state_in, gate, packed, finals, gains, out, state_out, normed_out,
    recv_stage, bias_stage,
):
    live = jnp.broadcast_to(lines[MASK, :], (PACKED - BIAS.start, NT)) > 0
    gain_col = gains[:, 2:3]
    final_col = gains[0:CM, 4:5]
    final_t = finals[:, 2 * CM : 4 * CM]
    weight_t = packed[BIAS.start : PACKED, :]
    recv_stage[...] = recv[...].astype(F32).reshape(CM * 24, LANES)
    for group in range(0, 4, GROUP):
        members = range(group, group + GROUP)
        span = slice(group * NT, (group + GROUP) * NT)
        state = update_rows(
            recv_stage, 24, members, state_in[:, span], gate[:, span], final_col, final_t
        )
        state_out[:, span] = state.astype(BF16)
        normed = norm(state, gain_col)
        normed_out[:, span] = normed
        bias_all = dot(weight_t, normed, 1, 0) * LOG2E
        for at, r in enumerate(members):
            bias = bias_all[:, at * NT : (at + 1) * NT]
            top = jnp.max(jnp.where(live, bias, -LARGE), axis=1, keepdims=True)
            bias = bias - jnp.where(top > -LARGE, top, 0.0)
            for chunk in range(CHUNKS):
                bias_stage[pl.ds(r * 16 + chunk, HEADS, stride=4), :] = bias[
                    0:HEADS, chunk * LANES : (chunk + 1) * LANES
                ]
    out[...] = jnp.broadcast_to(bias_stage[...].astype(BF16)[None], (64, 64, LANES))


def attention_inputs(
    recv, mine, normed, packed,
    query_out, key_out, value_out, gate_out, check_row, check_col, mine_out,
    recv_stage, turn,
):
    mine_out[...] = mine[...].astype(F32).reshape(64 * 64, LANES)
    recv_stage[...] = recv[:, 16:24, :].astype(F32).reshape(CM * 8, LANES)
    p, q = lax.axis_index("p"), lax.axis_index("q")

    def rows_of(at):
        return recv_stage[pl.ds(at, CM, stride=8), :]

    turn[0] = jnp.transpose(rows_of(p // 4) + rows_of(2 + p // 4))
    check_row[...] = turn[0, pl.ds(pl.multiple_of(lax.rem(p, 4) * 32, 32), 32), :]
    turn[1] = jnp.transpose(rows_of(4 + q // 2))
    check_col[...] = turn[1, pl.ds(pl.multiple_of(lax.rem(q, 2) * 64, 64), 64), :]
    for r in range(4):
        span = slice(r * NT, (r + 1) * NT)
        rows = normed[:, span]
        query_out[:, span] = (dot(packed[QUERY, :], rows, 1, 0) * (LOG2E * DH ** (-0.5))).astype(
            BF16
        )
        key_out[span, :] = dot(rows, packed[KEY, :], 0, 0).astype(BF16)
        value_out[:, span] = dot(packed[VALUE, :], rows, 1, 0).astype(BF16)
        gate_out[:, span] = sigmoid(dot(packed[ATT_GATE, :], rows, 1, 0)).astype(BF16)


def attend(
    lines, mine, bias_other, query, key, value, gate, state, packed, out, other, bias
):
    first = lax.axis_index("core") == 0
    other[...] = bias_other[...].astype(F32).reshape(64 * 64, LANES)
    key_bias = jnp.where(lines[MASK, :] > 0, 0.0, -1000000000.0 * LOG2E).astype(F32)
    key_cols = [column(key_bias[:, c * LANES : (c + 1) * LANES]) for c in range(CHUNKS)]
    weight_t = packed[ATT_OUT, :]

    def turn_bias(h):
        for chunk in range(CHUNKS):
            blocks = []
            for p in range(8):
                rows = pl.ds(p * 512 + h * 4 + chunk, 32, stride=16)
                here, there = mine[rows, :], other[rows, :]
                blocks += [jnp.where(first, here, there), jnp.where(first, there, here)]
            turned = jnp.transpose(jnp.concatenate(blocks, axis=0))
            bias[h, chunk * LANES : (chunk + 1) * LANES, :] = turned + key_cols[chunk]

    def scores(h, query_row, key_row):
        zeros = jnp.zeros((DH, NT), BF16)
        masked = jnp.concatenate(
            [query_row[h * DH : (h + 1) * DH] if at == h else zeros for at in range(HEADS)], axis=0
        )
        return dot(key_row, masked, 1, 0) + bias[h]

    def weighted(h, weights, value_row):
        padded = jnp.concatenate(
            [value_row[h * DH : (h + 1) * DH], jnp.ones((16, NT), BF16)], axis=0
        )
        both = dot(padded, weights.astype(BF16), 1, 0)
        return both[0:DH] / both[DH : DH + 1], both[DH : DH + 1]

    def finish(r, span, parts):
        attended = jnp.concatenate(parts, axis=0) * gate[:, span].astype(F32)
        result = state[:, span].astype(F32) + dot(weight_t, attended.astype(BF16), 1, 0)
        out[:, r, :, :] = jnp.transpose(result).astype(BF16).reshape(8, 64, CZ)

    low = high = jnp.ones((1, NT), F32)
    parts = [[] for _ in range(4)]
    def weights_of(h, r):
        span = slice(r * NT, (r + 1) * NT)
        return jnp.exp2(scores(h, query[:, span], key[span, :])).astype(BF16)

    turn_bias(0)
    order = [(h, r) for h in range(HEADS) for r in range(4)]
    ahead = weights_of(0, 0)
    for at, (h, r) in enumerate(order):
        weights = ahead
        if at + 1 < len(order):
            if r == 2 and h + 1 < HEADS:
                turn_bias(h + 1)
            ahead = weights_of(*order[at + 1])
        part, total = weighted(h, weights, value[:, r * NT : (r + 1) * NT])
        low, high = jnp.minimum(low, total), jnp.maximum(high, total)
        parts[r].append(part)
    for r in range(4):
        finish(r, slice(r * NT, (r + 1) * NT), parts[r])
    in_range = jnp.logical_and(jnp.min(low) > 1e-25, jnp.max(high) < 1e30)

    @pl.when(jnp.logical_not(in_range))
    def _():
        def one_row(r, carry):
            span = pl.ds(pl.multiple_of(r * NT, NT), NT)
            again = []
            for h in range(HEADS):
                values = scores(h, query[:, span], key[span, :])
                weights = jnp.exp2(values - jnp.max(values, axis=0, keepdims=True))
                again.append(weighted(h, weights, value[:, span])[0])
            finish(r, span, again)
            return carry

        lax.fori_loop(0, 4, one_row, 0)


def swap(values):
    return lax.ppermute(values, "core", [(0, 1), (1, 0)])


def exchange(values, axes):
    return lax.all_to_all(values, axes, 0, 0, tiled=True)


def on_device(
    pair_input,
    token_mask,
    out_check_weights,
    in_check_weights,
    out_norm_gain,
    out_proj,
    out_gate,
    out_final_gain,
    out_final,
    in_norm_gain,
    in_proj,
    in_gate,
    in_final_gain,
    in_final,
    att_norm_gain,
    att_qkv,
    att_bias,
    att_gate,
    att_out,
):
    def row(vector):
        return vector.reshape(1, vector.shape[0])

    tokens = 4 * NT
    mask_v = row(token_mask)
    state_rows = exchange(pair_input.reshape(8, 4, 64, CZ), "q")
    (sent,) = call(
        project_tile,
        [((CM, 32, LANES), BF16)],
        [((CM * 32, LANES), F32)],
        [("s", token_mask), ("w", mask_v), ("w", pair_input.reshape(tokens, CZ)),
         ("w", row(out_norm_gain)), ("w", out_proj)],
    )
    heads_t = jnp.pad(att_bias.T, ((0, 16 - HEADS), (0, 0)))
    weights = (
        row(out_norm_gain), out_gate, row(out_final_gain), out_final, row(in_norm_gain), in_proj, in_gate,
        row(in_final_gain), in_final, row(att_norm_gain), att_qkv, heads_t, att_gate, att_out,
        mask_v, row(out_check_weights), row(in_check_weights),
    )
    packed, finals, gains, lines = call(
        prepare,
        [((PACKED, CZ), BF16), ((CZ, 4 * CM), BF16), ((CZ, 8), F32), ((24, NT), F32)],
        [(value.shape, value.dtype) for value in weights] + [((COUNT,), None)],
        [("h", value) for value in weights],
    )
    state_rows, sent, packed, finals, gains, lines = lax.optimization_barrier(
        (state_rows, sent, packed, finals, gains, lines)
    )
    mine = exchange(sent, PLANE)
    mine, state_rows = lax.optimization_barrier((mine, state_rows))
    other = swap(mine)
    wide = (CZ, tokens)
    state, gate = call(
        gate_rows,
        [(wide, BF16), (wide, BF16)],
        [],
        [("v", state_rows), ("v", packed), ("v", gains)],
    )
    other, state, gate = lax.optimization_barrier((other, state, gate))
    sent, left, right = call(
        product_rows,
        [((64, 16, LANES), BF16), ((256, NT), BF16), ((NT, NT), BF16)],
        [((1024, LANES), F32)],
        [("v", mine), ("v", other)],
    )
    recv = exchange(sent, PLANE)
    sent, state = call(
        project_rows,
        [((CM, 32, LANES), BF16), (wide, F32)],
        [((CM * 32, LANES), F32), ((CM * 16, LANES), F32)],
        [("s", token_mask), ("v", lines), ("v", recv), ("v", state), ("v", gate),
         ("v", packed), ("v", finals), ("v", gains)],
    )
    mine = exchange(sent, PLANE)
    mine, state = lax.optimization_barrier((mine, state))
    other = swap(mine)
    gate, check_out = call(
        gate_and_check,
        [(wide, BF16), ((8, 256), F32)],
        [],
        [("v", state), ("v", packed), ("v", gains), ("v", left), ("v", right), ("v", lines)],
    )
    other, gate, check_out = lax.optimization_barrier((other, gate, check_out))
    (sent,) = call(
        product_cols,
        [((64, 24, LANES), BF16)],
        [((NT, NT), BF16), ((NT, NT), BF16), ((NT, NT), F32), ((64 * 32, LANES), F32),
         ((1024, LANES), F32)],
        [("v", mine), ("v", other), ("v", lines), ("v", check_out)],
    )
    recv = exchange(sent, PLANE)
    sent, state, normed = call(
        bias_rows,
        [((64, 64, LANES), BF16), (wide, BF16), (wide, BF16)],
        [((CM * 24, LANES), F32), ((64, LANES), F32)],
        [("v", lines), ("v", recv), ("v", state), ("v", gate), ("v", packed), ("v", finals),
         ("v", gains)],
    )
    mine = exchange(sent, PLANE)
    mine, normed = lax.optimization_barrier((mine, normed))
    other = swap(mine)
    query, key, value, gate, check_row, check_col, staged = call(
        attention_inputs,
        [(wide, BF16), ((tokens, CZ), BF16), (wide, BF16), (wide, BF16), ((32, CM), F32),
         ((64, CM), F32), ((64 * 64, LANES), F32)],
        [((CM * 8, LANES), F32), ((2, LANES, CM), F32)],
        [("v", recv), ("v", mine), ("v", normed), ("v", packed)],
    )
    other, query = lax.optimization_barrier((other, query))
    (sent,) = call(
        attend,
        [((8, 4, 64, CZ), BF16)],
        [((64 * 64, LANES), F32), ((HEADS, NT, NT), F32)],
        [("v", lines), ("v", staged), ("v", other), ("v", query), ("v", key), ("v", value),
         ("v", gate), ("v", state), ("v", packed)],
    )
    result = exchange(sent, "q").reshape(32, 64, CZ)
    return result, check_row, check_col


def solution(mesh):
    grid = Mesh(mesh.devices.reshape(8, 2, 8), ("p", "core", "q"))
    tile = P(("p", "core"), "q", None)
    in_specs = (tile,) + (P(),) * 18
    out_specs = (tile, P(("p", "core"), None), P("q", None))
    return jax.shard_map(
        on_device, mesh=grid, in_specs=in_specs, out_specs=out_specs, check_vma=False
    )
```

```python
import jax
import jax.numpy as jnp
from jax import lax
from jax.experimental import pallas as pl
from jax.experimental.pallas import tpu as pltpu
from jax.sharding import Mesh, PartitionSpec as P

F32 = jnp.float32
BF16 = jnp.bfloat16
NT = 512
CZ = 128
CM = 64
HEADS = 4
DH = 32
LANES = 128
CHUNKS = NT // LANES
PLANE = ("p", "q")
VMEM = pl.BlockSpec(memory_space=pltpu.VMEM)
SMEM = pl.BlockSpec(memory_space=pltpu.SMEM)
HBM = pl.BlockSpec(memory_space=pltpu.HBM)
SPECS = {"s": SMEM, "v": VMEM, "h": HBM, "w": VMEM}
LOG2E = 1.4426950408889634


def dot(left, right, left_dim, right_dim):
    return lax.dot_general(
        left, right, (((left_dim,), (right_dim,)), ((), ())), preferred_element_type=F32
    )


def column(row):
    return jnp.transpose(jnp.broadcast_to(row, (8, row.shape[1])))[:, 0:1]


def flipped(weight):
    return jnp.transpose(weight.astype(F32)).astype(BF16)


def eye():
    rows = lax.broadcasted_iota(jnp.int32, (LANES, LANES), 0)
    cols = lax.broadcasted_iota(jnp.int32, (LANES, LANES), 1)
    return jnp.where(rows == cols, 1.0, 0.0).astype(BF16)


def centre(values, gain_col):
    mean = jnp.mean(values, axis=0, keepdims=True)
    centered = values - mean
    variance = jnp.mean(centered * centered, axis=0, keepdims=True)
    return centered * lax.rsqrt(variance + 1e-05) * gain_col


def norm(values, gain_col):
    return centre(values, gain_col).astype(BF16)


def sigmoid(values):
    return jax.nn.sigmoid(values)


def thirds(values):
    high = values.astype(BF16)
    rest = values - high.astype(F32)
    middle = rest.astype(BF16)
    return jnp.concatenate([high, middle, (rest - middle.astype(F32)).astype(BF16)], axis=0)


def folded(parts):
    return parts[0:8] + (parts[8:16] + parts[16:24])


def call(kernel, outs, scratch, ins, mib=24):
    def shape_of(shape, kind, place="v"):
        return (pltpu.HBM if place == "h" else jax.ShapeDtypeStruct)(shape, kind)

    def placed(place, value):
        return pltpu.with_memory_space_constraint(value, pltpu.HBM) if place in "hw" else value

    return pl.pallas_call(
        kernel,
        out_shape=tuple(shape_of(*out) for out in outs),
        in_specs=[SPECS[place] for place, _ in ins],
        out_specs=tuple(HBM if out[2:] == ("h",) else VMEM for out in outs),
        scratch_shapes=[
            pltpu.SemaphoreType.DMA(shape) if kind is None else pltpu.VMEM(shape, kind)
            for shape, kind in scratch
        ],
        compiler_params=pltpu.CompilerParams(vmem_limit_bytes=mib * 1024 * 1024),
    )(*[placed(place, value) for place, value in ins])


def start(copies):
    for copy in copies:
        copy.start()
    return copies


def wait(copies):
    for copy in copies:
        copy.wait()


def first_row():
    return (2 * lax.axis_index("p") + lax.axis_index("core")) * 32


def project_tile(mask_s, mask_v, x, gain, weight, out, stage):
    row0 = first_row()
    shift = lax.rem(NT - 64 * lax.axis_index("q"), NT)
    mask_all = jnp.broadcast_to(mask_v[...].astype(F32), (8, NT))
    col_mask = pltpu.roll(mask_all, shift, 1)[0:1, 0:64]
    gain_col = column(gain[...])
    weight_t = flipped(weight[...])
    unit = eye()
    for group in range(4):
        steps = range(group * 4, group * 4 + 4)
        pieces, masks = [], []
        for s in steps:
            for i in (s, s + 16):
                pieces.append(x[i * 64 : (i + 1) * 64, :])
                masks.append(col_mask * mask_s[row0 + i].astype(F32))
        state = dot(unit, jnp.concatenate(pieces, axis=0), 1, 1)
        mask = jnp.concatenate(masks, axis=1)
        mixed = dot(weight_t, norm(state, gain_col), 1, 0)
        left = sigmoid(mixed[0:CM]) * mixed[CM : 2 * CM] * mask
        right = sigmoid(mixed[2 * CM : 3 * CM]) * mixed[3 * CM : 4 * CM] * mask
        for at, s in enumerate(steps):
            lanes = slice(at * LANES, (at + 1) * LANES)
            stage[pl.ds(s, CM, stride=32), :] = left[:, lanes]
            stage[pl.ds(16 + s, CM, stride=32), :] = right[:, lanes]
    out[...] = stage[...].astype(BF16).reshape(CM, 32, LANES)


OUT_GATE = slice(0, 128)
IN_PROJ = slice(128, 384)
IN_GATE = slice(384, 512)
QUERY = slice(512, 640)
KEY = slice(640, 768)
VALUE = slice(768, 896)
ATT_GATE = slice(896, 1024)
ATT_OUT = slice(1024, 1152)
BIAS = slice(1152, 1156)
PACKED = 1168
GROUP = 4
LARGE = 3e38
COUNT = 17
MASK = slice(0, 1)
OUT_CHECK = slice(8, 16)
IN_CHECK = slice(16, 24)


def prepare(*refs):
    sources, (packed, finals, gains, lines) = refs[:COUNT], refs[COUNT : COUNT + 4]
    targets, sems = refs[COUNT + 4 : 2 * COUNT + 4], refs[2 * COUNT + 4]
    wait(
        start(
            [
                pltpu.make_async_copy(source, target, sems.at[at])
                for at, (source, target) in enumerate(zip(sources, targets))
            ]
        )
    )
    (
        out_norm_gain, out_gate, out_final_gain, out_final, in_norm_gain, in_proj, in_gate,
        in_final_gain, in_final, att_norm_gain, att_qkv, att_bias, att_gate, att_out,
        mask, out_check, in_check,
    ) = targets
    for at, line in enumerate((mask, out_check, in_check)):
        lines[at * 8 : (at + 1) * 8, :] = jnp.broadcast_to(line[...].astype(F32), (8, NT))
    packed[OUT_GATE, :] = flipped(out_gate[...])
    packed[IN_PROJ, :] = flipped(in_proj[...])
    packed[IN_GATE, :] = flipped(in_gate[...])
    packed[QUERY, :] = flipped(att_qkv[:, 0:128])
    packed[KEY, :] = att_qkv[:, 128:256]
    packed[VALUE, :] = flipped(att_qkv[:, 256:384])
    packed[ATT_GATE, :] = flipped(att_gate[...])
    packed[ATT_OUT, :] = flipped(att_out[...])
    packed[BIAS.start : PACKED, :] = att_bias[...]
    for at, weight in enumerate((out_final, out_final, in_final, in_final)):
        finals[:, at * CM : (at + 1) * CM] = flipped(weight[...])
    pad = jnp.zeros((1, CM), F32)
    rows = [
        out_norm_gain[...],
        in_norm_gain[...],
        att_norm_gain[...],
        jnp.concatenate([out_final_gain[...], pad], axis=1),
        jnp.concatenate([in_final_gain[...], pad], axis=1),
        jnp.zeros((3, CZ), F32),
    ]
    gains[...] = jnp.transpose(jnp.concatenate(rows, axis=0))


def gate_rows(x, packed, gains, state_out, gate_out):
    gain_col = gains[:, 0:1]
    weight_t = packed[OUT_GATE, :]
    unit = eye()
    for r in range(4):
        rows = jnp.concatenate([x[q, r] for q in range(8)], axis=0)
        state = dot(unit, rows, 1, 1)
        span = slice(r * NT, (r + 1) * NT)
        state_out[:, span] = state.astype(BF16)
        gate_out[:, span] = sigmoid(dot(weight_t, norm(state, gain_col), 1, 0)).astype(BF16)


def product_rows(mine, other, out, left, right, stage):
    core = lax.axis_index("core")
    low = lax.broadcasted_iota(jnp.int32, (16, LANES), 1) < 64

    def paired(ref, src, rows):
        first = ref[src, rows, :].astype(F32)
        second = ref[src + 1, rows, :].astype(F32)
        head = jnp.where(low, first, pltpu.roll(second, 64, 1))
        tail = jnp.where(low, pltpu.roll(first, 64, 1), second)
        return jnp.concatenate([head, tail], axis=0).astype(BF16)

    for p in range(8):
        for a in range(CHUNKS):
            lanes = slice(a * LANES, (a + 1) * LANES)
            src = p * 8 + 2 * a
            left[p * 32 : (p + 1) * 32, lanes] = paired(mine, src, slice(0, 16))
            at = pl.multiple_of(p * 64 + core * 32, 32)
            right[pl.ds(at, 32), lanes] = paired(mine, src, slice(16, 32))
            at = pl.multiple_of(p * 64 + (1 - core) * 32, 32)
            right[pl.ds(at, 32), lanes] = paired(other, src, slice(16, 32))
    product = dot(left[...], right[...], 1, 1)
    for chunk in range(CHUNKS):
        stage[pl.ds(chunk, 256, stride=4), :] = product[:, chunk * LANES : (chunk + 1) * LANES]
    out[...] = stage[...].astype(BF16).reshape(64, 16, LANES)


def update_rows(recv_stage, stride, members, state, gate, final_gain, final_t):
    product = jnp.concatenate(
        [
            recv_stage[pl.ds(r * 4 + chunk, CM, stride=stride), :]
            for r in members
            for chunk in range(CHUNKS)
        ],
        axis=1,
    )
    normed = centre(product, final_gain)
    high = normed.astype(BF16)
    low = (normed - high.astype(F32)).astype(BF16)
    update = dot(final_t, jnp.concatenate([high, low], axis=0), 1, 0)
    return state.astype(F32) + gate.astype(F32) * update


def project_rows(
    mask_s, lines, recv, state_in, gate, packed, finals, gains, out, state_out, stage, recv_stage
):
    row0 = first_row() + 4 * lax.axis_index("q")
    mask_all = lines[MASK, :]
    gain_col = gains[:, 1:2]
    final_col = gains[0:CM, 3:4]
    final_t = finals[:, 0 : 2 * CM]
    weight_t = packed[IN_PROJ, :]
    recv_stage[...] = recv[...].astype(F32).reshape(CM * 16, LANES)
    for group in range(0, 4, GROUP):
        members = range(group, group + GROUP)
        span = slice(group * NT, (group + GROUP) * NT)
        state = update_rows(
            recv_stage, 16, members, state_in[:, span], gate[:, span], final_col, final_t
        )
        state_out[:, span] = state
        mixed = dot(weight_t, norm(state, gain_col), 1, 0)
        mask = jnp.concatenate([mask_all * mask_s[row0 + r].astype(F32) for r in members], axis=1)
        left = sigmoid(mixed[0:CM]) * mixed[CM : 2 * CM] * mask
        right = sigmoid(mixed[2 * CM : 3 * CM]) * mixed[3 * CM : 4 * CM] * mask
        for at, r in enumerate(members):
            for chunk in range(CHUNKS):
                lanes = slice(at * NT + chunk * LANES, at * NT + (chunk + 1) * LANES)
                stage[pl.ds(r * 8 + chunk, CM, stride=32), :] = left[:, lanes]
                stage[pl.ds(r * 8 + 4 + chunk, CM, stride=32), :] = right[:, lanes]
    out[...] = stage[...].astype(BF16).reshape(CM, 32, LANES)


def gate_and_check(state, packed, gains, left, right, lines, gate_out, check_out):
    weight_rows = lines[OUT_CHECK, :].astype(BF16)
    total = folded(dot(thirds(dot(weight_rows, right[...], 1, 0)), left[...], 1, 1))
    check_out[...] = total / NT
    gain_col = gains[:, 1:2]
    weight_t = packed[IN_GATE, :]
    for r in range(4):
        span = slice(r * NT, (r + 1) * NT)
        normed = norm(state[:, span].astype(F32), gain_col)
        gate_out[:, span] = sigmoid(dot(weight_t, normed, 1, 0)).astype(BF16)


def product_cols(mine, other, lines, check_in, out, left, right, product, stage, stage_out):
    core = lax.axis_index("core")
    for side, buf in enumerate((mine, other)):
        stage[...] = buf[...].astype(F32).reshape(64 * 32, LANES)
        rows = slice(side * 256, (side + 1) * 256)
        for chunk in range(CHUNKS):
            lanes = slice(chunk * LANES, (chunk + 1) * LANES)
            left[rows, lanes] = stage[pl.ds(chunk, 256, stride=8), :].astype(BF16)
            right[rows, lanes] = stage[pl.ds(4 + chunk, 256, stride=8), :].astype(BF16)
    product[...] = dot(left[...], right[...], 0, 0)
    for p in range(8):
        rows = product[pl.ds(pl.multiple_of(p * 64 + core * 32, 32), 32), :]
        for chunk in range(CHUNKS):
            stage_out[pl.ds(p * 128 + chunk, 32, stride=4), :] = rows[
                :, chunk * LANES : (chunk + 1) * LANES
            ]
    out[:, 0:16, :] = stage_out[...].astype(BF16).reshape(64, 16, LANES)
    weight_rows = lines[IN_CHECK, :].astype(BF16)
    total = folded(dot(thirds(dot(weight_rows, left[...], 1, 1)), right[...], 1, 0))
    high = check_in[...].astype(BF16).astype(F32)
    lines = []
    for part, count in ((high, 2), (check_in[...] - high, 2), (total / NT, 4)):
        lines += [part[0:1, c * LANES : (c + 1) * LANES] for c in range(count)]
    lines.append(jnp.zeros((8, LANES), F32))
    tail = jnp.concatenate(lines, axis=0).astype(BF16)
    out[:, 16:32, :] = jnp.broadcast_to(tail[None], (64, 16, LANES))


def bias_rows(
    lines, recv, state_in, gate, packed, finals, gains, out, state_out, normed_out,
    recv_stage, bias_stage,
):
    live = jnp.broadcast_to(lines[MASK, :], (PACKED - BIAS.start, NT)) > 0
    gain_col = gains[:, 2:3]
    final_col = gains[0:CM, 4:5]
    final_t = finals[:, 2 * CM : 4 * CM]
    weight_t = packed[BIAS.start : PACKED, :]
    recv_stage[...] = recv[...].astype(F32).reshape(CM * 32, LANES)
    for group in range(0, 4, GROUP):
        members = range(group, group + GROUP)
        span = slice(group * NT, (group + GROUP) * NT)
        state = update_rows(
            recv_stage, 32, members, state_in[:, span], gate[:, span], final_col, final_t
        )
        state_out[:, span] = state.astype(BF16)
        normed = norm(state, gain_col)
        normed_out[:, span] = normed
        bias_all = dot(weight_t, normed, 1, 0) * LOG2E
        for at, r in enumerate(members):
            bias = bias_all[:, at * NT : (at + 1) * NT]
            top = jnp.max(jnp.where(live, bias, -LARGE), axis=1, keepdims=True)
            bias = bias - jnp.where(top > -LARGE, top, 0.0)
            for chunk in range(CHUNKS):
                bias_stage[pl.ds(r * 16 + chunk, HEADS, stride=4), :] = bias[
                    0:HEADS, chunk * LANES : (chunk + 1) * LANES
                ]
    out[...] = jnp.broadcast_to(bias_stage[...].astype(BF16)[None], (64, 64, LANES))


def attention_inputs(
    recv, mine, normed, packed,
    query_out, key_out, value_out, gate_out, check_row, check_col, mine_out,
    recv_stage, turn,
):
    mine_out[...] = mine[...].astype(F32).reshape(64 * 64, LANES)
    recv_stage[...] = recv[:, 16:32, :].astype(F32).reshape(CM * 16, LANES)
    p, q = lax.axis_index("p"), lax.axis_index("q")

    def rows_of(at):
        return recv_stage[pl.ds(at, CM, stride=16), :]

    turn[0] = jnp.transpose(rows_of(p // 4) + rows_of(2 + p // 4))
    check_row[...] = turn[0, pl.ds(pl.multiple_of(lax.rem(p, 4) * 32, 32), 32), :]
    turn[1] = jnp.transpose(rows_of(4 + q // 2))
    check_col[...] = turn[1, pl.ds(pl.multiple_of(lax.rem(q, 2) * 64, 64), 64), :]
    for r in range(4):
        span = slice(r * NT, (r + 1) * NT)
        rows = normed[:, span]
        query_out[:, span] = (dot(packed[QUERY, :], rows, 1, 0) * (LOG2E * DH ** (-0.5))).astype(
            BF16
        )
        key_out[span, :] = dot(rows, packed[KEY, :], 0, 0).astype(BF16)
        value_out[:, span] = dot(packed[VALUE, :], rows, 1, 0).astype(BF16)
        gate_out[:, span] = sigmoid(dot(packed[ATT_GATE, :], rows, 1, 0)).astype(BF16)


def attend(
    lines, mine, bias_other, query, key, value, gate, state, packed, out, other, bias
):
    first = lax.axis_index("core") == 0
    other[...] = bias_other[...].astype(F32).reshape(64 * 64, LANES)
    key_bias = jnp.where(lines[MASK, :] > 0, 0.0, -1000000000.0 * LOG2E).astype(F32)
    key_cols = [column(key_bias[:, c * LANES : (c + 1) * LANES]) for c in range(CHUNKS)]
    weight_t = packed[ATT_OUT, :]

    def turn_bias(h):
        for chunk in range(CHUNKS):
            blocks = []
            for p in range(8):
                rows = pl.ds(p * 512 + h * 4 + chunk, 32, stride=16)
                here, there = mine[rows, :], other[rows, :]
                blocks += [jnp.where(first, here, there), jnp.where(first, there, here)]
            turned = jnp.transpose(jnp.concatenate(blocks, axis=0))
            bias[h, chunk * LANES : (chunk + 1) * LANES, :] = turned + key_cols[chunk]

    def scores(h, query_row, key_row):
        zeros = jnp.zeros((DH, NT), BF16)
        masked = jnp.concatenate(
            [query_row[h * DH : (h + 1) * DH] if at == h else zeros for at in range(HEADS)], axis=0
        )
        return dot(key_row, masked, 1, 0) + bias[h]

    def weighted(h, weights, value_row):
        padded = jnp.concatenate(
            [value_row[h * DH : (h + 1) * DH], jnp.ones((16, NT), BF16)], axis=0
        )
        both = dot(padded, weights.astype(BF16), 1, 0)
        return both[0:DH] / both[DH : DH + 1], both[DH : DH + 1]

    def finish(r, span, parts):
        attended = jnp.concatenate(parts, axis=0) * gate[:, span].astype(F32)
        result = state[:, span].astype(F32) + dot(weight_t, attended.astype(BF16), 1, 0)
        out[:, r, :, :] = jnp.transpose(result).astype(BF16).reshape(8, 64, CZ)

    low = high = jnp.ones((1, NT), F32)
    parts = [[] for _ in range(4)]
    def weights_of(h, r):
        span = slice(r * NT, (r + 1) * NT)
        return jnp.exp2(scores(h, query[:, span], key[span, :])).astype(BF16)

    turn_bias(0)
    order = [(h, r) for h in range(HEADS) for r in range(4)]
    ahead = weights_of(0, 0)
    for at, (h, r) in enumerate(order):
        weights = ahead
        if at + 1 < len(order):
            if r == 2 and h + 1 < HEADS:
                turn_bias(h + 1)
            ahead = weights_of(*order[at + 1])
        part, total = weighted(h, weights, value[:, r * NT : (r + 1) * NT])
        low, high = jnp.minimum(low, total), jnp.maximum(high, total)
        parts[r].append(part)
    for r in range(4):
        finish(r, slice(r * NT, (r + 1) * NT), parts[r])
    in_range = jnp.logical_and(jnp.min(low) > 1e-25, jnp.max(high) < 1e30)

    @pl.when(jnp.logical_not(in_range))
    def _():
        def one_row(r, carry):
            span = pl.ds(pl.multiple_of(r * NT, NT), NT)
            again = []
            for h in range(HEADS):
                values = scores(h, query[:, span], key[span, :])
                weights = jnp.exp2(values - jnp.max(values, axis=0, keepdims=True))
                again.append(weighted(h, weights, value[:, span])[0])
            finish(r, span, again)
            return carry

        lax.fori_loop(0, 4, one_row, 0)


def swap(values):
    return lax.ppermute(values, "core", [(0, 1), (1, 0)])


def exchange(values, axes):
    return lax.all_to_all(values, axes, 0, 0, tiled=True)


def on_device(
    pair_input,
    token_mask,
    out_check_weights,
    in_check_weights,
    out_norm_gain,
    out_proj,
    out_gate,
    out_final_gain,
    out_final,
    in_norm_gain,
    in_proj,
    in_gate,
    in_final_gain,
    in_final,
    att_norm_gain,
    att_qkv,
    att_bias,
    att_gate,
    att_out,
):
    def row(vector):
        return vector.reshape(1, vector.shape[0])

    tokens = 4 * NT
    mask_v = row(token_mask)
    state_rows = exchange(pair_input.reshape(8, 4, 64, CZ), "q")
    (sent,) = call(
        project_tile,
        [((CM, 32, LANES), BF16)],
        [((CM * 32, LANES), F32)],
        [("s", token_mask), ("w", mask_v), ("w", pair_input.reshape(tokens, CZ)),
         ("w", row(out_norm_gain)), ("w", out_proj)],
    )
    heads_t = jnp.pad(att_bias.T, ((0, 16 - HEADS), (0, 0)))
    weights = (
        row(out_norm_gain), out_gate, row(out_final_gain), out_final, row(in_norm_gain), in_proj, in_gate,
        row(in_final_gain), in_final, row(att_norm_gain), att_qkv, heads_t, att_gate, att_out,
        mask_v, row(out_check_weights), row(in_check_weights),
    )
    packed, finals, gains, lines = call(
        prepare,
        [((PACKED, CZ), BF16), ((CZ, 4 * CM), BF16), ((CZ, 8), F32), ((24, NT), F32)],
        [(value.shape, value.dtype) for value in weights] + [((COUNT,), None)],
        [("h", value) for value in weights],
    )
    state_rows, sent, packed, finals, gains, lines = lax.optimization_barrier(
        (state_rows, sent, packed, finals, gains, lines)
    )
    mine = exchange(sent, PLANE)
    mine, state_rows = lax.optimization_barrier((mine, state_rows))
    other = swap(mine)
    wide = (CZ, tokens)
    state, gate = call(
        gate_rows,
        [(wide, BF16), (wide, BF16)],
        [],
        [("v", state_rows), ("v", packed), ("v", gains)],
    )
    other, state, gate = lax.optimization_barrier((other, state, gate))
    sent, left, right = call(
        product_rows,
        [((64, 16, LANES), BF16), ((256, NT), BF16), ((NT, NT), BF16)],
        [((1024, LANES), F32)],
        [("v", mine), ("v", other)],
    )
    recv = exchange(sent, PLANE)
    sent, state = call(
        project_rows,
        [((CM, 32, LANES), BF16), (wide, F32)],
        [((CM * 32, LANES), F32), ((CM * 16, LANES), F32)],
        [("s", token_mask), ("v", lines), ("v", recv), ("v", state), ("v", gate),
         ("v", packed), ("v", finals), ("v", gains)],
    )
    mine = exchange(sent, PLANE)
    mine, state = lax.optimization_barrier((mine, state))
    other = swap(mine)
    gate, check_out = call(
        gate_and_check,
        [(wide, BF16), ((8, 256), F32)],
        [],
        [("v", state), ("v", packed), ("v", gains), ("v", left), ("v", right), ("v", lines)],
    )
    other, gate, check_out = lax.optimization_barrier((other, gate, check_out))
    (sent,) = call(
        product_cols,
        [((64, 32, LANES), BF16)],
        [((NT, NT), BF16), ((NT, NT), BF16), ((NT, NT), F32), ((64 * 32, LANES), F32),
         ((1024, LANES), F32)],
        [("v", mine), ("v", other), ("v", lines), ("v", check_out)],
    )
    recv = exchange(sent, PLANE)
    sent, state, normed = call(
        bias_rows,
        [((64, 64, LANES), BF16), (wide, BF16), (wide, BF16)],
        [((CM * 32, LANES), F32), ((64, LANES), F32)],
        [("v", lines), ("v", recv), ("v", state), ("v", gate), ("v", packed), ("v", finals),
         ("v", gains)],
    )
    mine = exchange(sent, PLANE)
    mine, normed = lax.optimization_barrier((mine, normed))
    other = swap(mine)
    query, key, value, gate, check_row, check_col, staged = call(
        attention_inputs,
        [(wide, BF16), ((tokens, CZ), BF16), (wide, BF16), (wide, BF16), ((32, CM), F32),
         ((64, CM), F32), ((64 * 64, LANES), F32)],
        [((CM * 16, LANES), F32), ((2, LANES, CM), F32)],
        [("v", recv), ("v", mine), ("v", normed), ("v", packed)],
    )
    other, query = lax.optimization_barrier((other, query))
    (sent,) = call(
        attend,
        [((8, 4, 64, CZ), BF16)],
        [((64 * 64, LANES), F32), ((HEADS, NT, NT), F32)],
        [("v", lines), ("v", staged), ("v", other), ("v", query), ("v", key), ("v", value),
         ("v", gate), ("v", state), ("v", packed)],
    )
    result = exchange(sent, "q").reshape(32, 64, CZ)
    return result, check_row, check_col


def solution(mesh):
    grid = Mesh(mesh.devices.reshape(8, 2, 8), ("p", "core", "q"))
    tile = P(("p", "core"), "q", None)
    in_specs = (tile,) + (P(),) * 18
    out_specs = (tile, P(("p", "core"), None), P("q", None))
    return jax.shard_map(
        on_device, mesh=grid, in_specs=in_specs, out_specs=out_specs, check_vma=False
    )
```

```python
import jax
import jax.numpy as jnp
from jax import lax
from jax.experimental import pallas as pl
from jax.experimental.pallas import tpu as pltpu
from jax.sharding import Mesh, PartitionSpec as P

F32 = jnp.float32
BF16 = jnp.bfloat16
NT = 512
CZ = 128
CM = 64
HEADS = 4
DH = 32
LANES = 128
CHUNKS = NT // LANES
PLANE = ("p", "q")
VMEM = pl.BlockSpec(memory_space=pltpu.VMEM)
SMEM = pl.BlockSpec(memory_space=pltpu.SMEM)
HBM = pl.BlockSpec(memory_space=pltpu.HBM)
SPECS = {"s": SMEM, "v": VMEM, "h": HBM, "w": VMEM}
LOG2E = 1.4426950408889634


def dot(left, right, left_dim, right_dim):
    return lax.dot_general(
        left, right, (((left_dim,), (right_dim,)), ((), ())), preferred_element_type=F32
    )


def column(row):
    return jnp.transpose(jnp.broadcast_to(row, (8, row.shape[1])))[:, 0:1]


def flipped(weight):
    return jnp.transpose(weight.astype(F32)).astype(BF16)


def eye():
    rows = lax.broadcasted_iota(jnp.int32, (LANES, LANES), 0)
    cols = lax.broadcasted_iota(jnp.int32, (LANES, LANES), 1)
    return jnp.where(rows == cols, 1.0, 0.0).astype(BF16)


def centre(values, gain_col):
    mean = jnp.mean(values, axis=0, keepdims=True)
    centered = values - mean
    variance = jnp.mean(centered * centered, axis=0, keepdims=True)
    return centered * lax.rsqrt(variance + 1e-05) * gain_col


def norm(values, gain_col):
    return centre(values, gain_col).astype(BF16)


def sigmoid(values):
    return jax.nn.sigmoid(values)


def thirds(values):
    high = values.astype(BF16)
    rest = values - high.astype(F32)
    middle = rest.astype(BF16)
    return jnp.concatenate([high, middle, (rest - middle.astype(F32)).astype(BF16)], axis=0)


def folded(parts):
    return parts[0:8] + (parts[8:16] + parts[16:24])


def call(kernel, outs, scratch, ins, mib=24):
    def shape_of(shape, kind, place="v"):
        return (pltpu.HBM if place == "h" else jax.ShapeDtypeStruct)(shape, kind)

    def placed(place, value):
        return pltpu.with_memory_space_constraint(value, pltpu.HBM) if place in "hw" else value

    return pl.pallas_call(
        kernel,
        out_shape=tuple(shape_of(*out) for out in outs),
        in_specs=[SPECS[place] for place, _ in ins],
        out_specs=tuple(HBM if out[2:] == ("h",) else VMEM for out in outs),
        scratch_shapes=[
            pltpu.SemaphoreType.DMA(shape) if kind is None else pltpu.VMEM(shape, kind)
            for shape, kind in scratch
        ],
        compiler_params=pltpu.CompilerParams(vmem_limit_bytes=mib * 1024 * 1024),
    )(*[placed(place, value) for place, value in ins])


def start(copies):
    for copy in copies:
        copy.start()
    return copies


def wait(copies):
    for copy in copies:
        copy.wait()


def first_row():
    return (2 * lax.axis_index("p") + lax.axis_index("core")) * 32


def project_tile(mask_s, mask_v, x, gain, weight, out, stage):
    row0 = first_row()
    shift = lax.rem(NT - 64 * lax.axis_index("q"), NT)
    mask_all = jnp.broadcast_to(mask_v[...].astype(F32), (8, NT))
    col_mask = pltpu.roll(mask_all, shift, 1)[0:1, 0:64]
    gain_col = column(gain[...])
    weight_t = flipped(weight[...])
    unit = eye()
    for group in range(4):
        steps = range(group * 4, group * 4 + 4)
        pieces, masks = [], []
        for s in steps:
            for i in (s, s + 16):
                pieces.append(x[i * 64 : (i + 1) * 64, :])
                masks.append(col_mask * mask_s[row0 + i].astype(F32))
        state = dot(unit, jnp.concatenate(pieces, axis=0), 1, 1)
        mask = jnp.concatenate(masks, axis=1)
        mixed = dot(weight_t, norm(state, gain_col), 1, 0)
        left = sigmoid(mixed[0:CM]) * mixed[CM : 2 * CM] * mask
        right = sigmoid(mixed[2 * CM : 3 * CM]) * mixed[3 * CM : 4 * CM] * mask
        for at, s in enumerate(steps):
            lanes = slice(at * LANES, (at + 1) * LANES)
            stage[pl.ds(s, CM, stride=32), :] = left[:, lanes]
            stage[pl.ds(16 + s, CM, stride=32), :] = right[:, lanes]
    out[...] = stage[...].astype(BF16).reshape(CM, 32, LANES)


OUT_GATE = slice(0, 128)
IN_PROJ = slice(128, 384)
IN_GATE = slice(384, 512)
QUERY = slice(512, 640)
KEY = slice(640, 768)
VALUE = slice(768, 896)
ATT_GATE = slice(896, 1024)
ATT_OUT = slice(1024, 1152)
BIAS = slice(1152, 1156)
PACKED = 1168
GROUP = 4
LARGE = 3e38
COUNT = 17
MASK = slice(0, 1)
OUT_CHECK = slice(8, 16)
IN_CHECK = slice(16, 24)


def prepare(*refs):
    sources, (packed, finals, gains, lines) = refs[:COUNT], refs[COUNT : COUNT + 4]
    targets, sems = refs[COUNT + 4 : 2 * COUNT + 4], refs[2 * COUNT + 4]
    wait(
        start(
            [
                pltpu.make_async_copy(source, target, sems.at[at])
                for at, (source, target) in enumerate(zip(sources, targets))
            ]
        )
    )
    (
        out_norm_gain, out_gate, out_final_gain, out_final, in_norm_gain, in_proj, in_gate,
        in_final_gain, in_final, att_norm_gain, att_qkv, att_bias, att_gate, att_out,
        mask, out_check, in_check,
    ) = targets
    for at, line in enumerate((mask, out_check, in_check)):
        lines[at * 8 : (at + 1) * 8, :] = jnp.broadcast_to(line[...].astype(F32), (8, NT))
    packed[OUT_GATE, :] = flipped(out_gate[...])
    packed[IN_PROJ, :] = flipped(in_proj[...])
    packed[IN_GATE, :] = flipped(in_gate[...])
    packed[QUERY, :] = flipped(att_qkv[:, 0:128])
    packed[KEY, :] = att_qkv[:, 128:256]
    packed[VALUE, :] = flipped(att_qkv[:, 256:384])
    packed[ATT_GATE, :] = flipped(att_gate[...])
    packed[ATT_OUT, :] = flipped(att_out[...])
    packed[BIAS.start : PACKED, :] = att_bias[...]
    for at, weight in enumerate((out_final, out_final, in_final, in_final)):
        finals[:, at * CM : (at + 1) * CM] = flipped(weight[...])
    pad = jnp.zeros((1, CM), F32)
    rows = [
        out_norm_gain[...],
        in_norm_gain[...],
        att_norm_gain[...],
        jnp.concatenate([out_final_gain[...], pad], axis=1),
        jnp.concatenate([in_final_gain[...], pad], axis=1),
        jnp.zeros((3, CZ), F32),
    ]
    gains[...] = jnp.transpose(jnp.concatenate(rows, axis=0))


def gate_rows(x, packed, gains, state_out, gate_out):
    gain_col = gains[:, 0:1]
    weight_t = packed[OUT_GATE, :]
    unit = eye()
    for r in range(4):
        rows = jnp.concatenate([x[q, r] for q in range(8)], axis=0)
        state = dot(unit, rows, 1, 1)
        span = slice(r * NT, (r + 1) * NT)
        state_out[:, span] = state.astype(BF16)
        gate_out[:, span] = sigmoid(dot(weight_t, norm(state, gain_col), 1, 0)).astype(BF16)


def product_rows(mine, other, out, left, right, stage):
    core = lax.axis_index("core")
    low = lax.broadcasted_iota(jnp.int32, (16, LANES), 1) < 64

    def paired(ref, src, rows):
        first = ref[src, rows, :].astype(F32)
        second = ref[src + 1, rows, :].astype(F32)
        head = jnp.where(low, first, pltpu.roll(second, 64, 1))
        tail = jnp.where(low, pltpu.roll(first, 64, 1), second)
        return jnp.concatenate([head, tail], axis=0).astype(BF16)

    for p in range(8):
        for a in range(CHUNKS):
            lanes = slice(a * LANES, (a + 1) * LANES)
            src = p * 8 + 2 * a
            left[p * 32 : (p + 1) * 32, lanes] = paired(mine, src, slice(0, 16))
            at = pl.multiple_of(p * 64 + core * 32, 32)
            right[pl.ds(at, 32), lanes] = paired(mine, src, slice(16, 32))
            at = pl.multiple_of(p * 64 + (1 - core) * 32, 32)
            right[pl.ds(at, 32), lanes] = paired(other, src, slice(16, 32))
    product = dot(left[...], right[...], 1, 1)
    for chunk in range(CHUNKS):
        stage[pl.ds(chunk, 256, stride=4), :] = product[:, chunk * LANES : (chunk + 1) * LANES]
    out[...] = stage[...].astype(BF16).reshape(64, 16, LANES)


def update_rows(recv_stage, stride, members, state, gate, final_gain, final_t):
    product = jnp.concatenate(
        [
            recv_stage[pl.ds(r * 4 + chunk, CM, stride=stride), :]
            for r in members
            for chunk in range(CHUNKS)
        ],
        axis=1,
    )
    normed = centre(product, final_gain)
    high = normed.astype(BF16)
    low = (normed - high.astype(F32)).astype(BF16)
    update = dot(final_t, jnp.concatenate([high, low], axis=0), 1, 0)
    return state.astype(F32) + gate.astype(F32) * update


def project_rows(
    mask_s, lines, recv, state_in, gate, packed, finals, gains, out, state_out, stage, recv_stage
):
    row0 = first_row() + 4 * lax.axis_index("q")
    mask_all = lines[MASK, :]
    gain_col = gains[:, 1:2]
    final_col = gains[0:CM, 3:4]
    final_t = finals[:, 0 : 2 * CM]
    weight_t = packed[IN_PROJ, :]
    recv_stage[...] = recv[...].astype(F32).reshape(CM * 16, LANES)
    for group in range(0, 4, GROUP):
        members = range(group, group + GROUP)
        span = slice(group * NT, (group + GROUP) * NT)
        state = update_rows(
            recv_stage, 16, members, state_in[:, span], gate[:, span], final_col, final_t
        )
        state_out[:, span] = state
        mixed = dot(weight_t, norm(state, gain_col), 1, 0)
        mask = jnp.concatenate([mask_all * mask_s[row0 + r].astype(F32) for r in members], axis=1)
        left = sigmoid(mixed[0:CM]) * mixed[CM : 2 * CM] * mask
        right = sigmoid(mixed[2 * CM : 3 * CM]) * mixed[3 * CM : 4 * CM] * mask
        for at, r in enumerate(members):
            for chunk in range(CHUNKS):
                lanes = slice(at * NT + chunk * LANES, at * NT + (chunk + 1) * LANES)
                stage[pl.ds(r * 8 + chunk, CM, stride=32), :] = left[:, lanes]
                stage[pl.ds(r * 8 + 4 + chunk, CM, stride=32), :] = right[:, lanes]
    out[...] = stage[...].astype(BF16).reshape(CM, 32, LANES)


def gate_and_check(state, packed, gains, left, right, lines, gate_out, check_out):
    weight_rows = lines[OUT_CHECK, :].astype(BF16)
    total = folded(dot(thirds(dot(weight_rows, right[...], 1, 0)), left[...], 1, 1))
    check_out[...] = total / NT
    gain_col = gains[:, 1:2]
    weight_t = packed[IN_GATE, :]
    for r in range(4):
        span = slice(r * NT, (r + 1) * NT)
        normed = norm(state[:, span].astype(F32), gain_col)
        gate_out[:, span] = sigmoid(dot(weight_t, normed, 1, 0)).astype(BF16)


def product_cols(mine, other, lines, check_in, out, left, right, turned, stage, stage_out):
    core = lax.axis_index("core")
    for side, buf in enumerate((mine, other)):
        stage[...] = buf[...].astype(F32).reshape(64 * 32, LANES)
        rows = slice(side * 256, (side + 1) * 256)
        for chunk in range(CHUNKS):
            lanes = slice(chunk * LANES, (chunk + 1) * LANES)
            left[rows, lanes] = stage[pl.ds(chunk, 256, stride=8), :].astype(BF16)
            right[rows, lanes] = stage[pl.ds(4 + chunk, 256, stride=8), :].astype(BF16)
    turned[...] = jnp.transpose(left[...].astype(F32)).astype(BF16)
    chosen = [turned[pl.ds(pl.multiple_of(p * 64 + core * 32, 32), 32), :] for p in range(8)]
    product = dot(jnp.concatenate(chosen, axis=0), right[...], 1, 0)
    for chunk in range(CHUNKS):
        lanes = slice(chunk * LANES, (chunk + 1) * LANES)
        stage_out[pl.ds(chunk, 256, stride=4), :] = product[:, lanes]
    out[:, 0:16, :] = stage_out[...].astype(BF16).reshape(64, 16, LANES)
    weight_rows = lines[IN_CHECK, :].astype(BF16)
    total = folded(dot(thirds(dot(weight_rows, left[...], 1, 1)), right[...], 1, 0))
    high = check_in[...].astype(BF16).astype(F32)
    lines = []
    for part, count in ((high, 2), (check_in[...] - high, 2), (total / NT, 4)):
        lines += [part[0:1, c * LANES : (c + 1) * LANES] for c in range(count)]
    tail = jnp.concatenate(lines, axis=0).astype(BF16)
    out[:, 16:24, :] = jnp.broadcast_to(tail[None], (64, 8, LANES))


def bias_rows(
    lines, recv, state_in, gate, packed, finals, gains, out, state_out, normed_out,
    recv_stage, bias_stage,
):
    live = jnp.broadcast_to(lines[MASK, :], (PACKED - BIAS.start, NT)) > 0
    gain_col = gains[:, 2:3]
    final_col = gains[0:CM, 4:5]
    final_t = finals[:, 2 * CM : 4 * CM]
    weight_t = packed[BIAS.start : PACKED, :]
    recv_stage[...] = recv[...].astype(F32).reshape(CM * 24, LANES)
    for group in range(0, 4, GROUP):
        members = range(group, group + GROUP)
        span = slice(group * NT, (group + GROUP) * NT)
        state = update_rows(
            recv_stage, 24, members, state_in[:, span], gate[:, span], final_col, final_t
        )
        state_out[:, span] = state.astype(BF16)
        normed = norm(state, gain_col)
        normed_out[:, span] = normed
        bias_all = dot(weight_t, normed, 1, 0) * LOG2E
        for at, r in enumerate(members):
            bias = bias_all[:, at * NT : (at + 1) * NT]
            top = jnp.max(jnp.where(live, bias, -LARGE), axis=1, keepdims=True)
            bias = bias - jnp.where(top > -LARGE, top, 0.0)
            for chunk in range(CHUNKS):
                bias_stage[pl.ds(r * 16 + chunk, HEADS, stride=4), :] = bias[
                    0:HEADS, chunk * LANES : (chunk + 1) * LANES
                ]
    out[...] = jnp.broadcast_to(bias_stage[...].astype(BF16)[None], (64, 64, LANES))


def attention_inputs(
    recv, mine, normed, packed,
    query_out, key_out, value_out, gate_out, check_row, check_col, mine_out,
    recv_stage, turn,
):
    mine_out[...] = mine[...].astype(F32).reshape(64 * 64, LANES)
    recv_stage[...] = recv[:, 16:24, :].astype(F32).reshape(CM * 8, LANES)
    p, q = lax.axis_index("p"), lax.axis_index("q")

    def rows_of(at):
        return recv_stage[pl.ds(at, CM, stride=8), :]

    turn[0] = jnp.transpose(rows_of(p // 4) + rows_of(2 + p // 4))
    check_row[...] = turn[0, pl.ds(pl.multiple_of(lax.rem(p, 4) * 32, 32), 32), :]
    turn[1] = jnp.transpose(rows_of(4 + q // 2))
    check_col[...] = turn[1, pl.ds(pl.multiple_of(lax.rem(q, 2) * 64, 64), 64), :]
    for r in range(4):
        span = slice(r * NT, (r + 1) * NT)
        rows = normed[:, span]
        query_out[:, span] = (dot(packed[QUERY, :], rows, 1, 0) * (LOG2E * DH ** (-0.5))).astype(
            BF16
        )
        key_out[span, :] = dot(rows, packed[KEY, :], 0, 0).astype(BF16)
        value_out[:, span] = dot(packed[VALUE, :], rows, 1, 0).astype(BF16)
        gate_out[:, span] = sigmoid(dot(packed[ATT_GATE, :], rows, 1, 0)).astype(BF16)


def attend(
    lines, mine, bias_other, query, key, value, gate, state, packed, out, other, bias
):
    first = lax.axis_index("core") == 0
    other[...] = bias_other[...].astype(F32).reshape(64 * 64, LANES)
    key_bias = jnp.where(lines[MASK, :] > 0, 0.0, -1000000000.0 * LOG2E).astype(F32)
    key_cols = [column(key_bias[:, c * LANES : (c + 1) * LANES]) for c in range(CHUNKS)]
    weight_t = packed[ATT_OUT, :]

    def turn_bias(h):
        for chunk in range(CHUNKS):
            blocks = []
            for p in range(8):
                rows = pl.ds(p * 512 + h * 4 + chunk, 32, stride=16)
                here, there = mine[rows, :], other[rows, :]
                blocks += [jnp.where(first, here, there), jnp.where(first, there, here)]
            turned = jnp.transpose(jnp.concatenate(blocks, axis=0))
            bias[h, chunk * LANES : (chunk + 1) * LANES, :] = turned + key_cols[chunk]

    def scores(h, query_row, key_row):
        zeros = jnp.zeros((DH, NT), BF16)
        masked = jnp.concatenate(
            [query_row[h * DH : (h + 1) * DH] if at == h else zeros for at in range(HEADS)], axis=0
        )
        return dot(key_row, masked, 1, 0) + bias[h]

    def weighted(h, weights, value_row):
        padded = jnp.concatenate(
            [value_row[h * DH : (h + 1) * DH], jnp.ones((16, NT), BF16)], axis=0
        )
        both = dot(padded, weights.astype(BF16), 1, 0)
        return both[0:DH] / both[DH : DH + 1], both[DH : DH + 1]

    def finish(r, span, parts):
        attended = jnp.concatenate(parts, axis=0) * gate[:, span].astype(F32)
        result = state[:, span].astype(F32) + dot(weight_t, attended.astype(BF16), 1, 0)
        out[:, r, :, :] = jnp.transpose(result).astype(BF16).reshape(8, 64, CZ)

    low = high = jnp.ones((1, NT), F32)
    parts = [[] for _ in range(4)]
    def weights_of(h, r):
        span = slice(r * NT, (r + 1) * NT)
        return jnp.exp2(scores(h, query[:, span], key[span, :])).astype(BF16)

    turn_bias(0)
    order = [(h, r) for h in range(HEADS) for r in range(4)]
    ahead = weights_of(0, 0)
    for at, (h, r) in enumerate(order):
        weights = ahead
        if at + 1 < len(order):
            if r == 2 and h + 1 < HEADS:
                turn_bias(h + 1)
            ahead = weights_of(*order[at + 1])
        part, total = weighted(h, weights, value[:, r * NT : (r + 1) * NT])
        low, high = jnp.minimum(low, total), jnp.maximum(high, total)
        parts[r].append(part)
    for r in range(4):
        finish(r, slice(r * NT, (r + 1) * NT), parts[r])
    in_range = jnp.logical_and(jnp.min(low) > 1e-25, jnp.max(high) < 1e30)

    @pl.when(jnp.logical_not(in_range))
    def _():
        def one_row(r, carry):
            span = pl.ds(pl.multiple_of(r * NT, NT), NT)
            again = []
            for h in range(HEADS):
                values = scores(h, query[:, span], key[span, :])
                weights = jnp.exp2(values - jnp.max(values, axis=0, keepdims=True))
                again.append(weighted(h, weights, value[:, span])[0])
            finish(r, span, again)
            return carry

        lax.fori_loop(0, 4, one_row, 0)


def swap(values):
    return lax.ppermute(values, "core", [(0, 1), (1, 0)])


def exchange(values, axes):
    return lax.all_to_all(values, axes, 0, 0, tiled=True)


def on_device(
    pair_input,
    token_mask,
    out_check_weights,
    in_check_weights,
    out_norm_gain,
    out_proj,
    out_gate,
    out_final_gain,
    out_final,
    in_norm_gain,
    in_proj,
    in_gate,
    in_final_gain,
    in_final,
    att_norm_gain,
    att_qkv,
    att_bias,
    att_gate,
    att_out,
):
    def row(vector):
        return vector.reshape(1, vector.shape[0])

    tokens = 4 * NT
    mask_v = row(token_mask)
    state_rows = exchange(pair_input.reshape(8, 4, 64, CZ), "q")
    (sent,) = call(
        project_tile,
        [((CM, 32, LANES), BF16)],
        [((CM * 32, LANES), F32)],
        [("s", token_mask), ("w", mask_v), ("w", pair_input.reshape(tokens, CZ)),
         ("w", row(out_norm_gain)), ("w", out_proj)],
    )
    heads_t = jnp.pad(att_bias.T, ((0, 16 - HEADS), (0, 0)))
    weights = (
        row(out_norm_gain), out_gate, row(out_final_gain), out_final, row(in_norm_gain), in_proj, in_gate,
        row(in_final_gain), in_final, row(att_norm_gain), att_qkv, heads_t, att_gate, att_out,
        mask_v, row(out_check_weights), row(in_check_weights),
    )
    packed, finals, gains, lines = call(
        prepare,
        [((PACKED, CZ), BF16), ((CZ, 4 * CM), BF16), ((CZ, 8), F32), ((24, NT), F32)],
        [(value.shape, value.dtype) for value in weights] + [((COUNT,), None)],
        [("h", value) for value in weights],
    )
    state_rows, sent, packed, finals, gains, lines = lax.optimization_barrier(
        (state_rows, sent, packed, finals, gains, lines)
    )
    mine = exchange(sent, PLANE)
    mine, state_rows = lax.optimization_barrier((mine, state_rows))
    other = swap(mine)
    wide = (CZ, tokens)
    state, gate = call(
        gate_rows,
        [(wide, BF16), (wide, BF16)],
        [],
        [("v", state_rows), ("v", packed), ("v", gains)],
    )
    other, state, gate = lax.optimization_barrier((other, state, gate))
    sent, left, right = call(
        product_rows,
        [((64, 16, LANES), BF16), ((256, NT), BF16), ((NT, NT), BF16)],
        [((1024, LANES), F32)],
        [("v", mine), ("v", other)],
    )
    recv = exchange(sent, PLANE)
    sent, state = call(
        project_rows,
        [((CM, 32, LANES), BF16), (wide, F32)],
        [((CM * 32, LANES), F32), ((CM * 16, LANES), F32)],
        [("s", token_mask), ("v", lines), ("v", recv), ("v", state), ("v", gate),
         ("v", packed), ("v", finals), ("v", gains)],
    )
    mine = exchange(sent, PLANE)
    mine, state = lax.optimization_barrier((mine, state))
    other = swap(mine)
    gate, check_out = call(
        gate_and_check,
        [(wide, BF16), ((8, 256), F32)],
        [],
        [("v", state), ("v", packed), ("v", gains), ("v", left), ("v", right), ("v", lines)],
    )
    other, gate, check_out = lax.optimization_barrier((other, gate, check_out))
    (sent,) = call(
        product_cols,
        [((64, 24, LANES), BF16)],
        [((NT, NT), BF16), ((NT, NT), BF16), ((NT, NT), BF16), ((64 * 32, LANES), F32),
         ((1024, LANES), F32)],
        [("v", mine), ("v", other), ("v", lines), ("v", check_out)],
    )
    recv = exchange(sent, PLANE)
    sent, state, normed = call(
        bias_rows,
        [((64, 64, LANES), BF16), (wide, BF16), (wide, BF16)],
        [((CM * 24, LANES), F32), ((64, LANES), F32)],
        [("v", lines), ("v", recv), ("v", state), ("v", gate), ("v", packed), ("v", finals),
         ("v", gains)],
    )
    mine = exchange(sent, PLANE)
    mine, normed = lax.optimization_barrier((mine, normed))
    other = swap(mine)
    query, key, value, gate, check_row, check_col, staged = call(
        attention_inputs,
        [(wide, BF16), ((tokens, CZ), BF16), (wide, BF16), (wide, BF16), ((32, CM), F32),
         ((64, CM), F32), ((64 * 64, LANES), F32)],
        [((CM * 8, LANES), F32), ((2, LANES, CM), F32)],
        [("v", recv), ("v", mine), ("v", normed), ("v", packed)],
    )
    other, query = lax.optimization_barrier((other, query))
    (sent,) = call(
        attend,
        [((8, 4, 64, CZ), BF16)],
        [((64 * 64, LANES), F32), ((HEADS, NT, NT), F32)],
        [("v", lines), ("v", staged), ("v", other), ("v", query), ("v", key), ("v", value),
         ("v", gate), ("v", state), ("v", packed)],
    )
    result = exchange(sent, "q").reshape(32, 64, CZ)
    return result, check_row, check_col


def solution(mesh):
    grid = Mesh(mesh.devices.reshape(8, 2, 8), ("p", "core", "q"))
    tile = P(("p", "core"), "q", None)
    in_specs = (tile,) + (P(),) * 18
    out_specs = (tile, P(("p", "core"), None), P("q", None))
    return jax.shard_map(
        on_device, mesh=grid, in_specs=in_specs, out_specs=out_specs, check_vma=False
    )
```
